512 devices in a mesh: row: 32 (over z_hi, x, core), col: 16 (over z_lo, y).
Axes of the slice: x: 4, y: 8, z: 8 (z_hi: 4, z_lo: 2; z = z_hi * 2 + z_lo), core: 2. Of those that a mesh axis runs over, the one named last changes fastest.
Arguments:
- pair: float32 [768, 768, 128], P('row', 'col'), may hold values from -120 to 120
- residue_mask: int32 [768], replicated, may hold values from 0 to 1, as said below
- start_proj: bfloat16 [128, 512], replicated, may hold values from -0.5 to 0.5
- start_bias_w: bfloat16 [128, 4], replicated, may hold values from -16 to 16
- start_out: bfloat16 [128, 128], replicated, may hold values from -1 to 1
- end_proj: bfloat16 [128, 512], replicated, may hold values from -0.5 to 0.5
- end_bias_w: bfloat16 [128, 4], replicated, may hold values from -16 to 16
- end_out: bfloat16 [128, 128], replicated, may hold values from -1 to 1
Outputs:
- pair_out: float32 [768, 768, 128], P('row', 'col')
The draws below stay inside these ranges and needn't reach their ends.
Inputs may be any that keep to these rules, and one draw needn't show every extreme that they name: `residue_mask`: the first residue is always present.
All inputs are finite; a program needn't handle non-finite values.
Results may differ from the reference program's by a relative error of at most 0.023.
The reference program's roundings to bfloat16 on the way count: a program that leaves them out, or rounds other values in their place, can miss the bound.
Values may be sent and summed in bfloat16 or wider, within the bound.
A program may use at most 64 MiB of HBM per device.

```python
import jax
import jax.numpy as jnp
from jax import lax

NRES = 768
C = 128
HEADS = 4
HD = 32


def common_dirs(key):
    return jax.random.normal(jax.random.fold_in(key, 101), (2, C, HEADS), jnp.float32) / C ** 0.5


def draw_pair(key, part):
    key = jax.random.fold_in(key, 3)
    first = jax.random.fold_in(key, 0)
    field = jax.random.normal(first, (NRES, NRES, C), jnp.float32) * 0.05
    return jnp.clip(field, -120.0, 120.0)


def draw_residue_mask(key, part):
    key = jax.random.fold_in(key, 7)
    levels = jax.random.randint(key, (NRES,), 0, 8)
    present = (levels > 0).astype(jnp.int32)
    return jnp.where(jnp.arange(NRES) == 0, 1, present).astype(jnp.int32)


def draw_start_bias_w(key, part):
    dirs = common_dirs(key)
    return jnp.clip(dirs[0], -16.0, 16.0).astype(jnp.bfloat16)


def draw_end_bias_w(key, part):
    dirs = common_dirs(key)
    return jnp.clip(dirs[1], -16.0, 16.0).astype(jnp.bfloat16)


def gaussian(own_key, shape, scale, reach, held_as=jnp.bfloat16):
    result = jax.random.normal(own_key, shape, jnp.float32) * scale
    return jnp.minimum(jnp.maximum(result, -reach), reach).astype(held_as)


def setup_inputs(seed: int = 0) -> dict:
    splits = jax.random.split(jax.random.key(seed), 9)
    pair = draw_pair(jax.random.fold_in(splits[8], 71), 0)
    residue_mask = draw_residue_mask(jax.random.fold_in(splits[8], 71), 0)
    start_proj = gaussian(splits[2], (C, 4 * C), C ** -0.5, 0.5)
    start_bias_w = draw_start_bias_w(jax.random.fold_in(splits[8], 71), 0)
    start_out = gaussian(splits[4], (C, C), (C // 4) ** -0.5, 1.0)
    end_proj = gaussian(splits[5], (C, 4 * C), C ** -0.5, 0.5)
    end_bias_w = draw_end_bias_w(jax.random.fold_in(splits[8], 71), 0)
    end_out = gaussian(splits[7], (C, C), (C // 4) ** -0.5, 1.0)
    return {"pair": pair, "residue_mask": residue_mask, "start_proj": start_proj, "start_bias_w": start_bias_w, "start_out": start_out, "end_proj": end_proj, "end_bias_w": end_bias_w, "end_out": end_out}


def normalize(field):
    mean = lax.optimization_barrier(jnp.mean(field, axis=-1, keepdims=True))
    centered = field - mean
    var = lax.optimization_barrier(jnp.mean(centered * centered, axis=-1, keepdims=True))
    return (centered * lax.rsqrt(var + 1e-05)).astype(jnp.bfloat16)

def project(normed, proj_w):
    lead = normed.shape[:2]
    mixed = jnp.dot(normed.reshape(-1, C), proj_w, preferred_element_type=jnp.float32)
    mixed = mixed.reshape(lead + (4, HEADS, HD))
    query = mixed[:, :, 0] * HD ** (-0.5)
    gate = jax.nn.sigmoid(mixed[:, :, 3])
    return jnp.stack([query, mixed[:, :, 1], mixed[:, :, 2], gate], axis=2).astype(jnp.bfloat16)

def head_bias(normed, bias_w):
    lead = normed.shape[:2]
    flat = jnp.dot(normed.reshape(-1, C), bias_w, preferred_element_type=jnp.float32)
    return flat.astype(jnp.bfloat16).reshape(lead + (HEADS,))

def attend_heads(lane, bias_heads, keep):
    query = lane[:, 0].astype(jnp.float32)
    keys = lane[:, 1].astype(jnp.float32)
    values = lane[:, 2].astype(jnp.float32)
    scores = jnp.einsum('qhd,khd->hqk', query, keys, precision=lax.Precision.HIGHEST) + bias_heads
    scores = jnp.where(keep[None, None, :], scores, -1000000000.0)
    weights = lax.optimization_barrier(jax.nn.softmax(scores, axis=-1).astype(jnp.bfloat16))
    out = jnp.einsum('hqk,khd->qhd', weights.astype(jnp.float32), values, precision=lax.Precision.HIGHEST)
    return (out * lane[:, 3]).astype(jnp.bfloat16)

def reference(pair, residue_mask, start_proj, start_bias_w, start_out, end_proj, end_bias_w, end_out):
    keep = residue_mask > 0
    normed = normalize(pair)
    packed = lax.optimization_barrier(project(normed, start_proj))
    bias = lax.optimization_barrier(head_bias(normed, start_bias_w))
    bias_heads = bias.transpose(2, 0, 1).astype(jnp.float32)

    def start_row(lane):
        return attend_heads(lane, bias_heads, keep)
    gated = lax.map(start_row, packed)
    update = jnp.dot(gated.reshape(NRES * NRES, C), start_out, preferred_element_type=jnp.float32)
    pair_mid = pair + update.reshape(NRES, NRES, C)
    normed2 = normalize(pair_mid)
    packed2 = lax.optimization_barrier(project(normed2, end_proj))
    bias2 = lax.optimization_barrier(head_bias(normed2, end_bias_w))
    bias2_heads = bias2.transpose(2, 1, 0).astype(jnp.float32)

    def end_column(lane):
        return attend_heads(lane, bias2_heads, keep)
    gated2 = lax.map(end_column, packed2.transpose(1, 0, 2, 3, 4))
    gated2 = gated2.transpose(1, 0, 2, 3).reshape(NRES * NRES, C)
    update2 = jnp.dot(gated2, end_out, preferred_element_type=jnp.float32)
    return pair_mid + update2.reshape(NRES, NRES, C)
```

```python
import functools

import jax
import jax.numpy as jnp
from jax import lax
from jax.experimental import pallas as pl
from jax.experimental.pallas import tpu as pltpu
from jax.sharding import PartitionSpec as P

C = 128
HEADS = 4
HD = 32
MESH = pl.DeviceIdType.MESH
F32 = jnp.float32
BF16 = jnp.bfloat16
NT = (((1,), (1,)), ((), ()))
NEG = -1000000000.0


def iota(shape, dim):
    return lax.broadcasted_iota(jnp.int32, shape, dim)


def dot(a, b):
    return jnp.dot(a, b, preferred_element_type=F32)


def dot_nt(a, b):
    return lax.dot_general(a, b, NT, preferred_element_type=F32)


class Place:
    def __init__(self):
        r, c = lax.axis_index("row"), lax.axis_index("col")
        self.zh, self.x, self.co = r // 8, (r // 2) % 4, r % 2
        self.zl, self.y = c // 8, c % 8

    def dev(self, zh=None, x=None, co=None, zl=None, y=None):
        zh = self.zh if zh is None else zh
        x = self.x if x is None else x
        co = self.co if co is None else co
        zl = self.zl if zl is None else zl
        y = self.y if y is None else y
        return (zh * 8 + x * 2 + co, zl * 8 + y)


def send(src, dst, ssem, rsem, device):
    copy = pltpu.make_async_remote_copy(
        src_ref=src, dst_ref=dst, send_sem=ssem, recv_sem=rsem, device_id=device, device_id_type=MESH
    )
    copy.start()
    return copy


def got(dst, sem, device):
    pltpu.make_async_remote_copy(
        src_ref=dst, dst_ref=dst, send_sem=sem, recv_sem=sem, device_id=device, device_id_type=MESH
    ).wait_recv()


def sent(src, sem, device):
    pltpu.make_async_remote_copy(
        src_ref=src, dst_ref=src, send_sem=sem, recv_sem=sem, device_id=device, device_id_type=MESH
    ).wait_send()


def layer_norm(field):
    mean = jnp.mean(field, axis=-1, keepdims=True)
    centered = field - mean
    var = jnp.mean(centered * centered, axis=-1, keepdims=True)
    return centered * lax.rsqrt(var + 1e-05)


def local_bias(normed, bias_w, spread):
    flat = lax.dot_general(bias_w, normed, (((0,), (1,)), ((), ())), preferred_element_type=F32)
    spread[...] = jnp.zeros_like(spread)
    for r in range(24):
        spread[4 * r : 4 * r + 4, 0:48] = flat[:, 48 * r : 48 * r + 48]
    return spread[...].astype(BF16)


def join_columns(blocks, joined):
    total = None
    for b in range(8):
        lane, col = iota((128, 384), 0), iota((128, 384), 1)
        place = jnp.where((col == lane + 48 * b) & (lane < 48), 1.0, 0.0).astype(BF16)
        part = dot(blocks[b], place)
        total = part if total is None else total + part
    for j in range(3):
        joined[j] = total[:, 128 * j : 128 * j + 128]


def head_rows(joined, h):
    rows = jnp.concatenate([joined[j, pl.ds(h, 24, stride=4), :] for j in range(3)], axis=1)
    return jnp.concatenate([rows, jnp.zeros((8, 384), F32)], axis=0).astype(BF16)


def pick(head, at):
    row, col = iota((128, 128), 0), iota((128, 128), 1)
    hit = (row - 32 * head == col - at) & (col >= at) & (col < at + 32)
    return jnp.where(hit, 1.0, 0.0).astype(BF16)


def spread_out(out_w, wide):
    wide[...] = jnp.zeros_like(wide)
    for h in range(HEADS):
        for a in range(3):
            wide[h * 128 + 32 * a : h * 128 + 32 * a + 32, a * 128 : a * 128 + 128] = out_w[
                32 * h : 32 * h + 32, :
            ]


STEP = (0, 1, 3, 2)


def scratch1():
    dma = pltpu.SemaphoreType.DMA
    return {
        "nrm": pltpu.VMEM((8, 144, C), BF16),
        "x1": pltpu.VMEM((2, 2, 8, 3, 48, C), BF16),
        "spread": pltpu.VMEM((96, C), F32),
        "by": pltpu.VMEM((8, 96, C), BF16),
        "joined": pltpu.VMEM((3, 96, C), F32),
        "hs": pltpu.VMEM((4, 32, 384), BF16),
        "hr": pltpu.VMEM((2, 2, 32, 384), BF16),
        "bf": pltpu.VMEM((4, 4, 48, 768), BF16),
        "wall": pltpu.VMEM((3, C, 512), BF16),
        "wide": pltpu.VMEM((512, 384), BF16),
        "q": pltpu.VMEM((6, 4, 4, 48, C), BF16),
        "k": pltpu.VMEM((6, 768, C), BF16),
        "v": pltpu.VMEM((6, 768, C), BF16),
        "g": pltpu.VMEM((2, 4, 4, 48, C), BF16),
        "rs": pltpu.VMEM((2, 4, 4, 48, C), BF16),
        "rx": pltpu.VMEM((8, 4, 48, C), BF16),
        "by_s": dma((8,)),
        "by_r": dma((8,)),
        "xy_s": dma((8,)),
        "xy_r": dma((8,)),
        "xz_s": dma((8,)),
        "xz_r": dma((8,)),
        "xc_s": dma((2,)),
        "xc_r": dma((2,)),
        "h_s": dma((4,)),
        "h_r": dma((2, 2)),
        "bz_s": dma((4,)),
        "bz_r": dma((4,)),
        "bx_s": dma((4, 4)),
        "bx_r": dma((4, 4)),
        "rt_s": dma((2, 4, 4)),
        "rt_r": dma((8, 4)),
    }


def partners1(p):
    out = []
    for c in range(2):
        for z in range(2):
            for e in range(8):
                if (c, z, e) != (0, 0, 0):
                    out.append(p.dev(co=(p.co + c) % 2, zl=(p.zl + z) % 2, y=(p.y + e) % 8))
    for d in range(1, 4):
        out.append(p.dev(zh=(p.zh + d) % 4))
        out.append(p.dev(x=(p.x + d) % 4))
    return out


def phase1(p, ready, src, mask, proj, bias_w, out_w, dst, m):
    head = 2 * p.zl + p.co
    copies = []

    def norm_block(b, _):
        at = pl.multiple_of(b * 144, 16)
        m["nrm"][b] = layer_norm(src[pl.ds(at, 144), :]).astype(BF16)
        return 0

    lax.fori_loop(0, 8, norm_block, 0)
    m["by"][p.y] = local_bias(m["nrm"][...].reshape(1152, C), bias_w[...], m["spread"])
    ready()
    for d in range(1, 8):
        to = (p.y + d) % 8
        copies.append(
            send(m["by"].at[p.y], m["by"].at[p.y], m["by_s"].at[d], m["by_r"].at[p.y], p.dev(y=to))
        )
    for d in range(1, 8):
        to = (p.y + d) % 8
        copies.append(
            send(
                m["nrm"].at[to],
                m["x1f"].at[p.co, p.zl, p.y],
                m["xy_s"].at[d],
                m["xy_r"].at[p.y],
                p.dev(y=to),
            )
        )
    m["x1f"][p.co, p.zl, p.y] = m["nrm"][p.y]

    for a in range(3):
        first, here = pick(head, 0), pick(head, 32 * a)
        m["wall"][a, :, 0:128] = dot(proj[:, 0:128], first).astype(BF16)
        m["wall"][a, :, 128:256] = dot(proj[:, 128:256], first).astype(BF16)
        m["wall"][a, :, 256:384] = dot(proj[:, 256:384], here).astype(BF16)
        m["wall"][a, :, 384:512] = dot(proj[:, 384:512], here).astype(BF16)
    spread_out(out_w, m["wide"])

    for d in range(1, 8):
        fr = (p.y + d) % 8
        got(m["by"].at[fr], m["by_r"].at[fr], p.dev(y=fr))
    join_columns(m["by"], m["joined"])
    for h in range(HEADS):
        m["hs"][h] = head_rows(m["joined"], h)
    m["hr"][p.co, p.zl] = m["hs"][head]
    for c in range(2):
        for z in range(2):
            if (c, z) != (0, 0):
                co, zl = (p.co + c) % 2, (p.zl + z) % 2
                copies.append(
                    send(
                        m["hs"].at[2 * zl + co],
                        m["hr"].at[p.co, p.zl],
                        m["h_s"].at[2 * c + z],
                        m["h_r"].at[p.co, p.zl],
                        p.dev(co=co, zl=zl),
                    )
                )

    for d in range(8):
        fr = (p.y + d) % 8
        block = m["x1f"].at[p.co, p.zl, fr]
        if d:
            got(block, m["xy_r"].at[fr], p.dev(y=fr))
        copies.append(
            send(block, block, m["xz_s"].at[d], m["xz_r"].at[fr], p.dev(zl=(p.zl + 1) % 2))
        )
    half = m["x1f"].at[p.co, p.zl]
    copies.append(
        send(half, half, m["xc_s"].at[0], m["xc_r"].at[p.zl], p.dev(co=(p.co + 1) % 2))
    )

    for c in range(2):
        for z in range(2):
            if (c, z) != (0, 0):
                co, zl = (p.co + c) % 2, (p.zl + z) % 2
                got(m["hr"].at[co, zl], m["h_r"].at[co, zl], p.dev(co=co, zl=zl))
    halves = []
    for z in range(2):
        rows = [m["hr"][c, z].astype(F32)[0:24] for c in range(2)]
        halves.append(jnp.concatenate(rows, axis=0))
    whole = jnp.concatenate(halves, axis=1)
    m["bf"][p.x, p.zh] = jnp.where(mask[...] > 0, whole, NEG).astype(BF16)

    def to_columns(zh):
        block = m["bf"].at[p.x, zh]
        for d in range(1, 4):
            copies.append(
                send(
                    block,
                    block,
                    m["bx_s"].at[d, zh],
                    m["bx_r"].at[p.x, zh],
                    p.dev(x=(p.x + d) % 4),
                )
            )

    mine = m["bf"].at[p.x, p.zh]
    for d in range(1, 4):
        copies.append(
            send(mine, mine, m["bz_s"].at[d], m["bz_r"].at[p.zh], p.dev(zh=(p.zh + d) % 4))
        )
    to_columns(p.zh)
    other = (p.zl + 1) % 2
    for d in range(8):
        fr = (p.y + d) % 8
        got(m["x1f"].at[p.co, other, fr], m["xz_r"].at[fr], p.dev(zl=other))
    half = m["x1f"].at[p.co, other]
    copies.append(
        send(half, half, m["xc_s"].at[1], m["xc_r"].at[other], p.dev(co=(p.co + 1) % 2))
    )
    for d in range(1, 4):
        zh = (p.zh + d) % 4
        got(m["bf"].at[p.x, zh], m["bz_r"].at[zh], p.dev(zh=zh))
        to_columns(zh)

    lane = iota((768, C), 1)

    def prepare(t, _):
        co = (p.co + t) % 2

        @pl.when(t == 1)
        def _():
            for zl in range(2):
                got(m["x1f"].at[co, zl], m["xc_r"].at[zl], p.dev(co=co))

        gate = jnp.zeros((768, C), F32)
        for a in range(3):
            rows = m["x1f"][co, :, :, a * 48 : a * 48 + 48, :].reshape(768, C)
            mixed = dot(rows, m["wall"][a])
            item = 3 * co + a
            query = (mixed[:, 0:128] * HD ** (-0.5)).astype(BF16)
            m["q"][item] = query.reshape(4, 4, 48, C)
            m["k"][item] = mixed[:, 128:256].astype(BF16)
            value = jnp.where(lane == 96 + a, 1.0, mixed[:, 256:384])
            m["v"][item] = value.astype(BF16)
            gate = gate + mixed[:, 384:512]
        gate = jnp.where(lane < 96, jax.nn.sigmoid(gate), 0.0)
        m["g"][co] = gate.astype(BF16).reshape(4, 4, 48, C)
        return 0

    lax.fori_loop(0, 2, prepare, 0)

    lane = iota((192, C), 1)

    def attend(t, _):
        s, co = t // 2, t % 2
        x = (p.x + s + jnp.where(s == 2, 1, 0) - jnp.where(s == 3, 1, 0)) % 4

        @pl.when((s > 0) & (co == 0))
        def _():
            for zh in range(4):
                got(m["bf"].at[x, zh], m["bx_r"].at[x, zh], p.dev(x=x))

        bias = m["bf"][x].reshape(192, 768)
        out = jnp.zeros((192, C), F32)
        for a in range(3):
            item = 3 * co + a
            query = m["q"][item, :, x].reshape(192, C)
            scores = dot_nt(query, m["k"][item]) + bias.astype(F32)
            top = jnp.max(scores, axis=-1, keepdims=True)
            weights = jnp.exp(scores - top).astype(BF16)
            out = out + dot(weights, m["v"][item])
        inv = [1.0 / out[:, 96 + a : 97 + a] for a in range(3)]
        scale = jnp.where(lane < 32, inv[0], jnp.where(lane < 64, inv[1], inv[2]))
        gated = out * scale * m["g"][co, :, x].reshape(192, C).astype(F32)
        m["rs"][co, :, x] = gated.astype(BF16).reshape(4, 48, C)
        for zh in range(4):
            zl, y = zh // 2, (zh % 2) * 4 + x
            self = (co == p.co) & (zl == p.zl) & (y == p.y)

            @pl.when(self)
            def _():
                m["rx"][p.y, head] = m["rs"][co, zh, x]

            @pl.when(jnp.logical_not(self))
            def _():
                send(
                    m["rs"].at[co, zh, x],
                    m["rx"].at[p.y, head],
                    m["rt_s"].at[co, zh, x],
                    m["rt_r"].at[p.y, head],
                    p.dev(co=co, zl=zl, y=y),
                )

        return 0

    lax.fori_loop(0, 8, attend, 0)

    def take(t, _):
        y, h = t // 4, t % 4
        zl, co = h // 2, h % 2

        @pl.when(jnp.logical_not((y == p.y) & (h == head)))
        def _():
            got(m["rx"].at[y, h], m["rt_r"].at[y, h], p.dev(co=co, zl=zl, y=y))

        return 0

    lax.fori_loop(0, 32, take, 0)

    def finish(y, _):
        rows = jnp.concatenate([m["rx"][y, h] for h in range(HEADS)], axis=1)
        update = dot(rows, m["wide"][...])
        for a in range(3):
            at = pl.multiple_of((3 * y + a) * 48, 16)
            dst[pl.ds(at, 48), :] = src[pl.ds(at, 48), :] + update[:, a * 128 : a * 128 + 128]
        return 0

    lax.fori_loop(0, 8, finish, 0)

    for copy in copies:
        copy.wait_send()

    def leave(t, _):
        co, zh, x = t // 16, (t // 4) % 4, t % 4
        zl, y = zh // 2, (zh % 2) * 4 + x

        @pl.when(jnp.logical_not((co == p.co) & (zl == p.zl) & (y == p.y)))
        def _():
            sent(m["rs"].at[co, zh, x], m["rt_s"].at[co, zh, x], p.dev(co=co, zl=zl, y=y))

        return 0

    lax.fori_loop(0, 32, leave, 0)


def kernel1(names, src, mask, proj, bias_w, out_w, dst, *refs):
    m = dict(zip(names, refs))
    p = Place()
    partners = partners1(p)
    barrier = pltpu.get_barrier_semaphore()
    for device in partners:
        pl.semaphore_signal(barrier, inc=1, device_id=device, device_id_type=MESH)

    def ready():
        pl.semaphore_wait(barrier, len(partners))

    phase1(p, ready, src, mask, proj, bias_w, out_w, dst, m)


def call1(pair, mask, proj, bias_w, out_w):
    scratch = scratch1()
    scratch["x1f"] = pltpu.VMEM((2, 2, 8, 144, C), BF16)
    del scratch["x1"]
    vmem = pl.BlockSpec(memory_space=pltpu.VMEM)
    return pl.pallas_call(
        functools.partial(kernel1, tuple(scratch)),
        out_shape=jax.ShapeDtypeStruct(pair.shape, F32),
        in_specs=[vmem] * 5,
        out_specs=vmem,
        scratch_shapes=list(scratch.values()),
        compiler_params=pltpu.CompilerParams(
            collective_id=0, has_side_effects=True, vmem_limit_bytes=48 << 20
        ),
        name="start_attention",
    )(pair, mask, proj, bias_w, out_w)


def normalize(field):
    mean = jnp.mean(field, axis=-1, keepdims=True)
    centered = field - mean
    var = jnp.mean(centered * centered, axis=-1, keepdims=True)
    return (centered * lax.rsqrt(var + 1e-05)).astype(jnp.bfloat16)


def project(normed, proj_w):
    lead = normed.shape[:2]
    mixed = jnp.dot(normed.reshape(-1, C), proj_w, preferred_element_type=jnp.float32)
    mixed = mixed.reshape(lead + (4, HEADS, HD))
    query = mixed[:, :, 0] * HD ** (-0.5)
    gate = jax.nn.sigmoid(mixed[:, :, 3])
    return jnp.stack([query, mixed[:, :, 1], mixed[:, :, 2], gate], axis=2).astype(jnp.bfloat16)


def head_bias(normed, bias_w):
    lead = normed.shape[:2]
    flat = jnp.dot(normed.reshape(-1, C), bias_w, preferred_element_type=jnp.float32)
    return flat.astype(jnp.bfloat16).reshape(lead + (HEADS,))


def attend(lanes, piece, residue_mask):
    bias = piece[0].astype(jnp.float32)
    keep = residue_mask > 0

    def one_item(item):
        selected, whole = item
        scores = (
            jnp.einsum(
                "qd,kd->qk",
                selected[:, :HD],
                whole[:, HD : 2 * HD],
                preferred_element_type=jnp.float32,
            )
            + bias
        )
        scores = jnp.where(keep[None, :], scores, -1000000000.0)
        weights = jax.nn.softmax(scores, axis=-1).astype(jnp.bfloat16)
        out = jnp.dot(weights, whole[:, 2 * HD : 3 * HD], preferred_element_type=jnp.float32)
        return (out * selected[:, 3 * HD :]).astype(jnp.bfloat16)

    return lax.map(one_item, (lanes, lanes))


def shards(pair, residue_mask, start_proj, start_bias_w, start_out, end_proj, end_bias_w, end_out):
    rows, cols = pair.shape[:2]
    mask = residue_mask.reshape(1, -1)
    mid = call1(pair.reshape(rows * cols, C), mask, start_proj, start_bias_w, start_out)
    pair_mid = mid.reshape(rows, cols, C)
    n_row = lax.axis_size("row")
    quarter = n_row // HEADS
    normed2 = normalize(pair_mid)
    packed2 = project(normed2, end_proj)
    width = cols // quarter
    send2 = packed2.reshape(rows, quarter, width, 4, HEADS, HD).transpose(4, 1, 2, 0, 3, 5)
    send2 = send2.reshape(n_row, width, rows, 4 * HD)
    bias2 = head_bias(normed2, end_bias_w).transpose(2, 1, 0)
    broad = lax.all_gather(bias2, "col", axis=1, tiled=True)
    bias_send2 = jnp.repeat(broad, quarter, axis=0)
    moved2, bias_moved2 = (
        lax.all_to_all(send2, "row", split_axis=0, concat_axis=2, tiled=True),
        lax.all_to_all(bias_send2, "row", split_axis=0, concat_axis=2, tiled=True),
    )
    lanes2 = moved2[0]
    attended2 = attend(lanes2, bias_moved2, residue_mask)
    back2 = lax.all_to_all(attended2, "row", split_axis=1, concat_axis=0, tiled=True)
    merged2 = (
        back2.reshape(HEADS, quarter, width, rows, HD)
        .transpose(3, 1, 2, 0, 4)
        .reshape(rows * cols, C)
    )
    return pair_mid + jnp.dot(merged2, end_out, preferred_element_type=jnp.float32).reshape(
        rows, cols, C
    )


def solution(mesh):
    placed = (P("row", "col", None), P(), P(), P(), P(), P(), P(), P())
    return jax.shard_map(
        shards, mesh=mesh, in_specs=placed, out_specs=P("row", "col", None), check_vma=False
    )
```

```python
import functools

import jax
import jax.numpy as jnp
from jax import lax
from jax.experimental import pallas as pl
from jax.experimental.pallas import tpu as pltpu
from jax.sharding import PartitionSpec as P

C = 128
HEADS = 4
HD = 32
MESH = pl.DeviceIdType.MESH
F32 = jnp.float32
BF16 = jnp.bfloat16
NT = (((1,), (1,)), ((), ()))
NEG = -1000000000.0


def iota(shape, dim):
    return lax.broadcasted_iota(jnp.int32, shape, dim)


def dot(a, b):
    return jnp.dot(a, b, preferred_element_type=F32)


def dot_nt(a, b):
    return lax.dot_general(a, b, NT, preferred_element_type=F32)


class Place:
    def __init__(self):
        r, c = lax.axis_index("row"), lax.axis_index("col")
        self.zh, self.x, self.co = r // 8, (r // 2) % 4, r % 2
        self.zl, self.y = c // 8, c % 8
        self.yl = self.y % 2
        self.y1 = self.y + 1 - 2 * self.yl

    def dev(self, zh=None, x=None, co=None, zl=None, y=None):
        zh = self.zh if zh is None else zh
        x = self.x if x is None else x
        co = self.co if co is None else co
        zl = self.zl if zl is None else zl
        y = self.y if y is None else y
        return (zh * 8 + x * 2 + co, zl * 8 + y)


def send(src, dst, ssem, rsem, device):
    copy = pltpu.make_async_remote_copy(
        src_ref=src, dst_ref=dst, send_sem=ssem, recv_sem=rsem, device_id=device, device_id_type=MESH
    )
    copy.start()
    return copy


def got(dst, sem, device):
    pltpu.make_async_remote_copy(
        src_ref=dst, dst_ref=dst, send_sem=sem, recv_sem=sem, device_id=device, device_id_type=MESH
    ).wait_recv()


def sent(src, sem, device):
    pltpu.make_async_remote_copy(
        src_ref=src, dst_ref=src, send_sem=sem, recv_sem=sem, device_id=device, device_id_type=MESH
    ).wait_send()


def layer_norm(field):
    mean = jnp.mean(field, axis=-1, keepdims=True)
    centered = field - mean
    var = jnp.mean(centered * centered, axis=-1, keepdims=True)
    return centered * lax.rsqrt(var + 1e-05)


def local_bias(normed, bias_w, spread):
    flat = lax.dot_general(bias_w, normed, (((0,), (1,)), ((), ())), preferred_element_type=F32)
    spread[...] = jnp.zeros_like(spread)
    for r in range(24):
        spread[4 * r : 4 * r + 4, 0:48] = flat[:, 48 * r : 48 * r + 48]
    return spread[...].astype(BF16)


def join_columns(blocks, joined):
    total = None
    for b in range(8):
        lane, col = iota((128, 384), 0), iota((128, 384), 1)
        place = jnp.where((col == lane + 48 * b) & (lane < 48), 1.0, 0.0).astype(BF16)
        part = dot(blocks[b], place)
        total = part if total is None else total + part
    for j in range(3):
        joined[j] = total[:, 128 * j : 128 * j + 128]


def head_rows(joined, h):
    rows = jnp.concatenate([joined[j, pl.ds(h, 24, stride=4), :] for j in range(3)], axis=1)
    return jnp.concatenate([rows, jnp.zeros((8, 384), F32)], axis=0).astype(BF16)


def pick(head, at):
    row, col = iota((128, 128), 0), iota((128, 128), 1)
    hit = (row - 32 * head == col - at) & (col >= at) & (col < at + 32)
    return jnp.where(hit, 1.0, 0.0).astype(BF16)


def spread_out(out_w, wide):
    wide[...] = jnp.zeros_like(wide)
    for h in range(HEADS):
        for a in range(3):
            wide[h * 128 + 32 * a : h * 128 + 32 * a + 32, a * 128 : a * 128 + 128] = out_w[
                32 * h : 32 * h + 32, :
            ]


STEP = (0, 1, 3, 2)


def scratch1():
    dma = pltpu.SemaphoreType.DMA
    return {
        "nrm": pltpu.VMEM((8, 144, C), BF16),
        "x1f": pltpu.VMEM((2, 2, 8, 144, C), BF16),
        "spread": pltpu.VMEM((96, C), F32),
        "by": pltpu.VMEM((8, 96, C), BF16),
        "joined": pltpu.VMEM((3, 96, C), F32),
        "hs": pltpu.VMEM((4, 32, 384), BF16),
        "hr": pltpu.VMEM((2, 2, 32, 384), BF16),
        "bf": pltpu.VMEM((4, 4, 48, 768), BF16),
        "wall": pltpu.VMEM((3, C, 512), BF16),
        "wide": pltpu.VMEM((512, 384), BF16),
        "q": pltpu.VMEM((6, 4, 4, 48, C), BF16),
        "k": pltpu.VMEM((6, 768, C), BF16),
        "v": pltpu.VMEM((6, 768, C), BF16),
        "g": pltpu.VMEM((2, 4, 4, 48, C), BF16),
        "rs": pltpu.VMEM((2, 4, 4, 48, C), BF16),
        "rx": pltpu.VMEM((8, 4, 48, C), BF16),
        "by_s": dma((8,)),
        "by_r": dma((8,)),
        "xy_s": dma((8,)),
        "xy_r": dma((8,)),
        "xz_s": dma((8,)),
        "xz_r": dma((8,)),
        "xc_s": dma((2,)),
        "xc_r": dma((2,)),
        "h_s": dma((4,)),
        "h_r": dma((2, 2)),
        "bz_s": dma((4,)),
        "bz_r": dma((4,)),
        "bx_s": dma((4, 4)),
        "bx_r": dma((4, 4)),
        "rt_s": dma((2, 4, 4)),
        "rt_r": dma((8, 4)),
    }


def partners(p):
    out = []
    for c in range(2):
        for z in range(2):
            for e in range(8):
                if (c, z, e) != (0, 0, 0):
                    out.append(p.dev(co=(p.co + c) % 2, zl=(p.zl + z) % 2, y=(p.y + e) % 8))
    for a in range(4):
        for b in range(4):
            if (a, b) == (0, 0):
                continue
            zh, x = (p.zh + a) % 4, (p.x + b) % 4
            for co in range(2):
                out.append(p.dev(zh=zh, x=x, co=co))
                out.append(p.dev(zh=zh, x=x, co=co, y=p.y1))
    for a in range(1, 4):
        out.append(p.dev(zh=(p.zh + a) % 4, zl=1 - p.zl))
    return out


def phase1(p, ready, src, mask, proj, bias_w, out_w, dst, m):
    head = 2 * p.zl + p.co
    copies = []

    def norm_block(b, _):
        at = pl.multiple_of(b * 144, 16)
        m["nrm"][b] = layer_norm(src[pl.ds(at, 144), :]).astype(BF16)
        return 0

    lax.fori_loop(0, 8, norm_block, 0)
    m["by"][p.y] = local_bias(m["nrm"][...].reshape(1152, C), bias_w[...], m["spread"])
    ready()
    for d in range(1, 8):
        to = (p.y + d) % 8
        copies.append(
            send(m["by"].at[p.y], m["by"].at[p.y], m["by_s"].at[d], m["by_r"].at[p.y], p.dev(y=to))
        )
    for d in range(1, 8):
        to = (p.y + d) % 8
        copies.append(
            send(
                m["nrm"].at[to],
                m["x1f"].at[p.co, p.zl, p.y],
                m["xy_s"].at[d],
                m["xy_r"].at[p.y],
                p.dev(y=to),
            )
        )
    m["x1f"][p.co, p.zl, p.y] = m["nrm"][p.y]

    for a in range(3):
        first, here = pick(head, 0), pick(head, 32 * a)
        m["wall"][a, :, 0:128] = dot(proj[:, 0:128], first).astype(BF16)
        m["wall"][a, :, 128:256] = dot(proj[:, 128:256], first).astype(BF16)
        m["wall"][a, :, 256:384] = dot(proj[:, 256:384], here).astype(BF16)
        m["wall"][a, :, 384:512] = dot(proj[:, 384:512], here).astype(BF16)
    spread_out(out_w, m["wide"])

    for d in range(1, 8):
        fr = (p.y + d) % 8
        got(m["by"].at[fr], m["by_r"].at[fr], p.dev(y=fr))
    join_columns(m["by"], m["joined"])
    for h in range(HEADS):
        m["hs"][h] = head_rows(m["joined"], h)
    m["hr"][p.co, p.zl] = m["hs"][head]
    for c in range(2):
        for z in range(2):
            if (c, z) != (0, 0):
                co, zl = (p.co + c) % 2, (p.zl + z) % 2
                copies.append(
                    send(
                        m["hs"].at[2 * zl + co],
                        m["hr"].at[p.co, p.zl],
                        m["h_s"].at[2 * c + z],
                        m["h_r"].at[p.co, p.zl],
                        p.dev(co=co, zl=zl),
                    )
                )

    for d in range(8):
        fr = (p.y + d) % 8
        block = m["x1f"].at[p.co, p.zl, fr]
        if d:
            got(block, m["xy_r"].at[fr], p.dev(y=fr))
        copies.append(
            send(block, block, m["xz_s"].at[d], m["xz_r"].at[fr], p.dev(zl=(p.zl + 1) % 2))
        )
    half = m["x1f"].at[p.co, p.zl]
    copies.append(
        send(half, half, m["xc_s"].at[0], m["xc_r"].at[p.zl], p.dev(co=(p.co + 1) % 2))
    )

    for c in range(2):
        for z in range(2):
            if (c, z) != (0, 0):
                co, zl = (p.co + c) % 2, (p.zl + z) % 2
                got(m["hr"].at[co, zl], m["h_r"].at[co, zl], p.dev(co=co, zl=zl))
    halves = []
    for z in range(2):
        rows = [m["hr"][c, z].astype(F32)[0:24] for c in range(2)]
        halves.append(jnp.concatenate(rows, axis=0))
    whole = jnp.concatenate(halves, axis=1)
    m["bf"][p.x, p.zh] = jnp.where(mask[...] > 0, whole, NEG).astype(BF16)

    def to_columns(zh):
        block = m["bf"].at[p.x, zh]
        for d in range(1, 4):
            copies.append(
                send(
                    block,
                    block,
                    m["bx_s"].at[d, zh],
                    m["bx_r"].at[p.x, zh],
                    p.dev(x=(p.x + d) % 4),
                )
            )

    mine = m["bf"].at[p.x, p.zh]
    for d in range(1, 4):
        copies.append(
            send(mine, mine, m["bz_s"].at[d], m["bz_r"].at[p.zh], p.dev(zh=(p.zh + d) % 4))
        )
    to_columns(p.zh)
    other = (p.zl + 1) % 2
    for d in range(8):
        fr = (p.y + d) % 8
        got(m["x1f"].at[p.co, other, fr], m["xz_r"].at[fr], p.dev(zl=other))
    half = m["x1f"].at[p.co, other]
    copies.append(
        send(half, half, m["xc_s"].at[1], m["xc_r"].at[other], p.dev(co=(p.co + 1) % 2))
    )
    for d in range(1, 4):
        zh = (p.zh + d) % 4
        got(m["bf"].at[p.x, zh], m["bz_r"].at[zh], p.dev(zh=zh))
        to_columns(zh)

    lane = iota((768, C), 1)

    def prepare(t, _):
        co = (p.co + t) % 2

        @pl.when(t == 1)
        def _():
            for zl in range(2):
                got(m["x1f"].at[co, zl], m["xc_r"].at[zl], p.dev(co=co))

        gate = jnp.zeros((768, C), F32)
        for a in range(3):
            rows = m["x1f"][co, :, :, a * 48 : a * 48 + 48, :].reshape(768, C)
            mixed = dot(rows, m["wall"][a])
            item = 3 * co + a
            query = (mixed[:, 0:128] * HD ** (-0.5)).astype(BF16)
            m["q"][item] = query.reshape(4, 4, 48, C)
            m["k"][item] = mixed[:, 128:256].astype(BF16)
            value = jnp.where(lane == 96 + a, 1.0, mixed[:, 256:384])
            m["v"][item] = value.astype(BF16)
            gate = gate + mixed[:, 384:512]
        gate = jnp.where(lane < 96, jax.nn.sigmoid(gate), 0.0)
        m["g"][co] = gate.astype(BF16).reshape(4, 4, 48, C)
        return 0

    lax.fori_loop(0, 2, prepare, 0)

    lane = iota((192, C), 1)

    def attend(t, _):
        s, co = t // 2, t % 2
        x = (p.x + s + jnp.where(s == 2, 1, 0) - jnp.where(s == 3, 1, 0)) % 4

        @pl.when((s > 0) & (co == 0))
        def _():
            for zh in range(4):
                got(m["bf"].at[x, zh], m["bx_r"].at[x, zh], p.dev(x=x))

        bias = m["bf"][x].reshape(192, 768)
        out = jnp.zeros((192, C), F32)
        for a in range(3):
            item = 3 * co + a
            query = m["q"][item, :, x].reshape(192, C)
            scores = dot_nt(query, m["k"][item]) + bias.astype(F32)
            top = jnp.max(scores, axis=-1, keepdims=True)
            weights = jnp.exp(scores - top).astype(BF16)
            out = out + dot(weights, m["v"][item])
        inv = [1.0 / out[:, 96 + a : 97 + a] for a in range(3)]
        scale = jnp.where(lane < 32, inv[0], jnp.where(lane < 64, inv[1], inv[2]))
        gated = out * scale * m["g"][co, :, x].reshape(192, C).astype(F32)
        m["rs"][co, :, x] = gated.astype(BF16).reshape(4, 48, C)
        for zh in range(4):
            zl, y = zh // 2, (zh % 2) * 4 + x
            self = (co == p.co) & (zl == p.zl) & (y == p.y)

            @pl.when(self)
            def _():
                m["rx"][p.y, head] = m["rs"][co, zh, x]

            @pl.when(jnp.logical_not(self))
            def _():
                send(
                    m["rs"].at[co, zh, x],
                    m["rx"].at[p.y, head],
                    m["rt_s"].at[co, zh, x],
                    m["rt_r"].at[p.y, head],
                    p.dev(co=co, zl=zl, y=y),
                )

        return 0

    lax.fori_loop(0, 8, attend, 0)

    def take(t, _):
        y, h = t // 4, t % 4
        zl, co = h // 2, h % 2

        @pl.when(jnp.logical_not((y == p.y) & (h == head)))
        def _():
            got(m["rx"].at[y, h], m["rt_r"].at[y, h], p.dev(co=co, zl=zl, y=y))

        return 0

    lax.fori_loop(0, 32, take, 0)

    def finish(y, _):
        rows = jnp.concatenate([m["rx"][y, h] for h in range(HEADS)], axis=1)
        update = dot(rows, m["wide"][...])
        for a in range(3):
            at = pl.multiple_of((3 * y + a) * 48, 16)
            dst[pl.ds(at, 48), :] = src[pl.ds(at, 48), :] + update[:, a * 128 : a * 128 + 128]
        return 0

    lax.fori_loop(0, 8, finish, 0)

    def leave(t, _):
        co, zh, x = t // 16, (t // 4) % 4, t % 4
        zl, y = zh // 2, (zh % 2) * 4 + x

        @pl.when(jnp.logical_not((co == p.co) & (zl == p.zl) & (y == p.y)))
        def _():
            sent(m["rs"].at[co, zh, x], m["rt_s"].at[co, zh, x], p.dev(co=co, zl=zl, y=y))

        return 0

    def close():
        for copy in copies:
            copy.wait_send()
        lax.fori_loop(0, 32, leave, 0)

    return close


def scratch2():
    dma = pltpu.SemaphoreType.DMA
    return {
        "nrm": pltpu.VMEM((8, 144, C), BF16),
        "nf": pltpu.VMEM((1152, C), F32),
        "ns": pltpu.VMEM((4, 4, 80, C), BF16),
        "x2": pltpu.VMEM((2, 2, 4, 4, 80, C), BF16),
        "xx": pltpu.VMEM((6, 16, 48, C), BF16),
        "spread": pltpu.VMEM((96, C), F32),
        "by": pltpu.VMEM((8, 96, C), BF16),
        "joined": pltpu.VMEM((3, 96, C), F32),
        "hs": pltpu.VMEM((4, 32, 384), BF16),
        "hr": pltpu.VMEM((2, 32, 384), BF16),
        "b2": pltpu.VMEM((4, 4, 2, 48, 384), BF16),
        "wk": pltpu.VMEM((C, C), BF16),
        "wt": pltpu.VMEM((C, C), BF16),
        "wide": pltpu.VMEM((512, 384), BF16),
        "qt": pltpu.VMEM((6, 2, C, 384), BF16),
        "k": pltpu.VMEM((6, 768, C), BF16),
        "vt": pltpu.VMEM((6, 48, 768), BF16),
        "gt": pltpu.VMEM((6, 2, 32, 384), BF16),
        "ot": pltpu.VMEM((C, 384), BF16),
        "tr": pltpu.VMEM((392, C), F32),
        "rs": pltpu.VMEM((2, 2, 16, 32, C), BF16),
        "rx": pltpu.VMEM((16, 4, 32, C), BF16),
        "by_s": dma((8,)),
        "by_r": dma((8,)),
        "xa_s": dma((4, 4)),
        "xa_r": dma((4, 4)),
        "xy_s": dma((4, 4)),
        "xy_r": dma((4, 4)),
        "xc_s": dma((2,)),
        "xc_r": dma((2,)),
        "h_s": dma((1,)),
        "h_r": dma((1,)),
        "bz_s": dma((4, 2)),
        "bz_r": dma((4, 2)),
        "bx_s": dma((4, 4, 2)),
        "bx_r": dma((4, 4, 2)),
        "rt_s": dma((2, 2, 16)),
        "rt_r": dma((16, 4)),
    }


def pick_rows(head, at):
    row, col = iota((128, 128), 0), iota((128, 128), 1)
    hit = (row - at == col - 32 * head) & (row >= at) & (row < at + 32)
    return jnp.where(hit, 1.0, 0.0).astype(BF16)


def phase2(p, src, mask, proj, bias_w, out_w, dst, m):
    head = 2 * p.yl + p.co
    other = 1 - p.co
    copies = []

    def norm_block(b, _):
        at = pl.multiple_of(b * 144, 16)
        normed = layer_norm(src[pl.ds(at, 144), :]).astype(BF16)
        m["nrm"][b] = normed
        m["nf"][pl.ds(at, 144), :] = normed.astype(F32)
        return 0

    lax.fori_loop(0, 8, norm_block, 0)
    m["by"][p.y] = local_bias(m["nrm"][...].reshape(1152, C), bias_w[...], m["spread"])
    for d in range(1, 8):
        to = (p.y + d) % 8
        copies.append(
            send(m["by"].at[p.y], m["by"].at[p.y], m["by_s"].at[d], m["by_r"].at[p.y], p.dev(y=to))
        )

    for a in range(4):
        for b in range(4):
            zh, x = (p.zh + a) % 4, (p.x + b) % 4
            first = 3 * (zh * 4 + x)
            rows = [m["nf"][pl.ds(first + i, 24, stride=48), :] for i in range(3)]
            rows.append(jnp.zeros((8, C), F32))
            m["ns"][zh, x] = jnp.concatenate(rows, axis=0).astype(BF16)
            if (a, b) == (0, 0):
                m["x2"][p.yl, p.co, p.zh, p.x] = m["ns"][zh, x]
            else:
                copies.append(
                    send(
                        m["ns"].at[zh, x],
                        m["x2"].at[p.yl, p.co, p.zh, p.x],
                        m["xa_s"].at[a, b],
                        m["xa_r"].at[p.zh, p.x],
                        p.dev(zh=zh, x=x),
                    )
                )

    m["wk"][...] = dot(proj[:, 128:256], pick(head, 0)).astype(BF16)
    wt = dot_nt(pick_rows(head, 0), proj[:, 0:128])
    wt = wt + dot_nt(pick_rows(head, 32), proj[:, 256:384])
    wt = wt + dot_nt(pick_rows(head, 64), proj[:, 384:512])
    m["wt"][...] = wt.astype(BF16)
    spread_out(out_w, m["wide"])

    for d in range(1, 8):
        fr = (p.y + d) % 8
        got(m["by"].at[fr], m["by_r"].at[fr], p.dev(y=fr))
    join_columns(m["by"], m["joined"])
    for h in range(HEADS):
        m["hs"][h] = head_rows(m["joined"], h)
    m["hr"][p.co] = m["hs"][head]
    copies.append(
        send(
            m["hs"].at[2 * p.yl + other],
            m["hr"].at[p.co],
            m["h_s"].at[0],
            m["h_r"].at[0],
            p.dev(co=other),
        )
    )
    row, col = iota((48, 768), 0), iota((48, 768), 1)
    keep = jnp.where(col == row + 48 * (4 * p.zh + p.x), mask[...], 0)
    keep = jnp.sum(keep.astype(F32), axis=1, keepdims=True)
    got(m["hr"].at[other], m["h_r"].at[0], p.dev(co=other))
    whole = jnp.concatenate([m["hr"][c].astype(F32)[0:24] for c in range(2)], axis=0)
    m["b2"][p.zh, p.x, p.zl] = jnp.where(keep > 0.5, whole, NEG).astype(BF16)

    def to_columns(zh, zl):
        block = m["b2"].at[zh, p.x, zl]
        for d in range(1, 4):
            copies.append(
                send(
                    block,
                    block,
                    m["bx_s"].at[d, zh, zl],
                    m["bx_r"].at[p.x, zh, zl],
                    p.dev(x=(p.x + d) % 4),
                )
            )

    mine = m["b2"].at[p.zh, p.x, p.zl]
    for z in range(2):
        for a in range(4):
            if (a, z) != (0, 0):
                zh, zl = (p.zh + a) % 4, (p.zl + z) % 2
                copies.append(
                    send(
                        mine,
                        mine,
                        m["bz_s"].at[a, z],
                        m["bz_r"].at[p.zh, p.zl],
                        p.dev(zh=zh, zl=zl),
                    )
                )
    to_columns(p.zh, p.zl)

    for a in range(4):
        for b in range(4):
            zh, x = (p.zh + a) % 4, (p.x + b) % 4
            block = m["x2"].at[p.yl, p.co, zh, x]
            if (a, b) != (0, 0):
                got(block, m["xa_r"].at[zh, x], p.dev(zh=zh, x=x))
            copies.append(
                send(block, block, m["xy_s"].at[a, b], m["xy_r"].at[zh, x], p.dev(y=p.y1))
            )
    part = m["x2"].at[p.yl, p.co]
    copies.append(send(part, part, m["xc_s"].at[0], m["xc_r"].at[p.yl], p.dev(co=other)))

    for z in range(2):
        for a in range(4):
            if (a, z) != (0, 0):
                zh, zl = (p.zh + a) % 4, (p.zl + z) % 2
                got(m["b2"].at[zh, p.x, zl], m["bz_r"].at[zh, zl], p.dev(zh=zh, zl=zl))
                to_columns(zh, zl)

    for a in range(4):
        for b in range(4):
            zh, x = (p.zh + a) % 4, (p.x + b) % 4
            got(m["x2"].at[1 - p.yl, p.co, zh, x], m["xy_r"].at[zh, x], p.dev(y=p.y1))
    part = m["x2"].at[1 - p.yl, p.co]
    copies.append(send(part, part, m["xc_s"].at[1], m["xc_r"].at[1 - p.yl], p.dev(co=other)))

    sub = iota((16, 768), 0)
    ones = jnp.where(sub == 0, 1.0, 0.0)

    def prepare(t, _):
        yl = (p.yl + t) % 2
        got(m["x2"].at[yl, other], m["xc_r"].at[yl], p.dev(co=other))

        def arrange(n, _):
            zh, x = n // 4, n % 4
            cores = [m["x2"][yl, c, zh, x].astype(F32) for c in range(2)]
            for b in range(3):
                rows = [core[24 * b : 24 * b + 24] for core in cores]
                m["xx"][3 * yl + b, n] = jnp.concatenate(rows, axis=0).astype(BF16)
            return 0

        lax.fori_loop(0, 16, arrange, 0)
        for b in range(3):
            item = 3 * yl + b
            rows = m["xx"][item].reshape(768, C)
            m["k"][item] = dot(rows, m["wk"][...]).astype(BF16)
            mixed = dot_nt(m["wt"][...], rows)
            query = (mixed * HD ** (-0.5)).astype(BF16)
            gate = jax.nn.sigmoid(mixed[64:96]).astype(BF16)
            for z in range(2):
                m["qt"][item, z] = query[:, 384 * z : 384 * z + 384]
                m["gt"][item, z] = gate[:, 384 * z : 384 * z + 384]
            m["vt"][item] = jnp.concatenate([mixed[32:64], ones], axis=0).astype(BF16)
        return 0

    lax.fori_loop(0, 2, prepare, 0)

    m["ot"][...] = jnp.zeros_like(m["ot"])
    m["tr"][...] = jnp.zeros_like(m["tr"])
    eye = jnp.where(iota((128, 128), 0) == iota((128, 128), 1), 1.0, 0.0).astype(BF16)

    def attend(t, _):
        z, yl = (p.zl + t // 2) % 2, t % 2

        @pl.when(yl == 0)
        def _():
            for d in range(1, 4):
                x = (p.x + d) % 4
                for zh in range(4):
                    got(m["b2"].at[zh, x, z], m["bx_r"].at[x, zh, z], p.dev(x=x))

        bias = m["b2"][:, :, z].reshape(768, 384)
        for b in range(3):
            item = 3 * yl + b
            scores = dot(m["k"][item], m["qt"][item, z]) + bias.astype(F32)
            top = jnp.max(scores, axis=0, keepdims=True)
            weights = jnp.exp(scores - top).astype(BF16)
            out = dot(m["vt"][item], weights)
            gated = out[0:32] / out[32:33] * m["gt"][item, z].astype(F32)
            m["ot"][32 * b : 32 * b + 32, :] = gated.astype(BF16)
        for j in range(3):
            m["tr"][128 * j : 128 * j + 128, :] = dot_nt(eye, m["ot"][:, 128 * j : 128 * j + 128])
        y = p.y - p.yl + yl
        for n in range(16):
            zh, x, co = 2 * z + n // 8, (n // 2) % 4, n % 2
            m["rs"][z, yl, n] = m["tr"][24 * n : 24 * n + 32, :].astype(BF16)
            self = (zh == p.zh) & (p.x == x) & (p.co == co) & (yl == p.yl)

            @pl.when(self)
            def _():
                m["rx"][4 * p.zh + p.x, head] = m["rs"][z, yl, n]

            @pl.when(jnp.logical_not(self))
            def _():
                send(
                    m["rs"].at[z, yl, n],
                    m["rx"].at[4 * p.zh + p.x, head],
                    m["rt_s"].at[z, yl, n],
                    m["rt_r"].at[4 * p.zh + p.x, head],
                    p.dev(zh=zh, x=x, co=co, y=y),
                )

        return 0

    lax.fori_loop(0, 4, attend, 0)

    def take(t, _):
        s, h = t // 4, t % 4
        zh, x, yl, co = s // 4, s % 4, h // 2, h % 2

        @pl.when(jnp.logical_not((s == 4 * p.zh + p.x) & (h == head)))
        def _():
            got(
                m["rx"].at[s, h],
                m["rt_r"].at[s, h],
                p.dev(zh=zh, x=x, co=co, y=p.y - p.yl + yl),
            )

        return 0

    lax.fori_loop(0, 64, take, 0)

    def finish(g, _):
        rows = [m["rx"][pl.ds(4 * g, 4), h].reshape(128, C) for h in range(HEADS)]
        update = dot(jnp.concatenate(rows, axis=1), m["wide"][...])
        for s in range(4):
            for b in range(3):
                at = pl.ds(3 * (4 * g + s) + b, 24, stride=48)
                dst[at, :] = src[at, :] + update[32 * s : 32 * s + 24, b * 128 : b * 128 + 128]
        return 0

    lax.fori_loop(0, 4, finish, 0)

    def leave(t, _):
        z, yl, n = t // 32, (t // 16) % 2, t % 16
        zh, x, co = 2 * z + n // 8, (n // 2) % 4, n % 2
        y = p.y - p.yl + yl

        @pl.when(
            jnp.logical_not((zh == p.zh) & (x == p.x) & (co == p.co) & (yl == p.yl))
        )
        def _():
            sent(m["rs"].at[z, yl, n], m["rt_s"].at[z, yl, n], p.dev(zh=zh, x=x, co=co, y=y))

        return 0

    def close():
        for copy in copies:
            copy.wait_send()
        lax.fori_loop(0, 64, leave, 0)

    return close


def kernel(
    names1, names2, pair, mask, proj1, bias1_w, out1_w, proj2, bias2_w, out2_w, dst, mid, *refs
):
    m1 = dict(zip(names1, refs))
    m2 = dict(zip(names2, refs[len(names1) :]))
    p = Place()
    others = partners(p)
    barrier = pltpu.get_barrier_semaphore()
    for device in others:
        pl.semaphore_signal(barrier, inc=1, device_id=device, device_id_type=MESH)

    def ready():
        pl.semaphore_wait(barrier, len(others))

    close1 = phase1(p, ready, pair, mask, proj1, bias1_w, out1_w, mid, m1)
    close2 = phase2(p, mid, mask, proj2, bias2_w, out2_w, dst, m2)
    close1()
    close2()


def shards(pair, residue_mask, start_proj, start_bias_w, start_out, end_proj, end_bias_w, end_out):
    rows, cols = pair.shape[:2]
    one, two = scratch1(), scratch2()
    vmem = pl.BlockSpec(memory_space=pltpu.VMEM)
    out = pl.pallas_call(
        functools.partial(kernel, tuple(one), tuple(two)),
        out_shape=jax.ShapeDtypeStruct((rows * cols, C), F32),
        in_specs=[vmem] * 8,
        out_specs=vmem,
        scratch_shapes=[pltpu.VMEM((rows * cols, C), F32)] + list(one.values()) + list(two.values()),
        compiler_params=pltpu.CompilerParams(
            collective_id=0, has_side_effects=True, vmem_limit_bytes=56 << 20
        ),
        name="triangle_attention",
    )(
        pair.reshape(rows * cols, C),
        residue_mask.reshape(1, -1),
        start_proj,
        start_bias_w,
        start_out,
        end_proj,
        end_bias_w,
        end_out,
    )
    return out.reshape(rows, cols, C)


def solution(mesh):
    placed = (P("row", "col", None), P(), P(), P(), P(), P(), P(), P())
    return jax.shard_map(
        shards, mesh=mesh, in_specs=placed, out_specs=P("row", "col", None), check_vma=False
    )
```

```python
import functools

import jax
import jax.numpy as jnp
from jax import lax
from jax.experimental import pallas as pl
from jax.experimental.pallas import tpu as pltpu
from jax.sharding import PartitionSpec as P

C = 128
HEADS = 4
HD = 32
MESH = pl.DeviceIdType.MESH
F32 = jnp.float32
BF16 = jnp.bfloat16
NT = (((1,), (1,)), ((), ()))
NEG = -1000000000.0


def iota(shape, dim):
    return lax.broadcasted_iota(jnp.int32, shape, dim)


def dot(a, b):
    return jnp.dot(a, b, preferred_element_type=F32)


def dot_nt(a, b):
    return lax.dot_general(a, b, NT, preferred_element_type=F32)


class Place:
    def __init__(self):
        r, c = lax.axis_index("row"), lax.axis_index("col")
        self.zh, self.x, self.co = r // 8, (r // 2) % 4, r % 2
        self.zl, self.y = c // 8, c % 8
        self.yl = self.y % 2
        self.y1 = self.y + 1 - 2 * self.yl

    def dev(self, zh=None, x=None, co=None, zl=None, y=None):
        zh = self.zh if zh is None else zh
        x = self.x if x is None else x
        co = self.co if co is None else co
        zl = self.zl if zl is None else zl
        y = self.y if y is None else y
        return (zh * 8 + x * 2 + co, zl * 8 + y)


def send(src, dst, ssem, rsem, device):
    copy = pltpu.make_async_remote_copy(
        src_ref=src, dst_ref=dst, send_sem=ssem, recv_sem=rsem, device_id=device, device_id_type=MESH
    )
    copy.start()
    return copy


def got(dst, sem, device):
    pltpu.make_async_remote_copy(
        src_ref=dst, dst_ref=dst, send_sem=sem, recv_sem=sem, device_id=device, device_id_type=MESH
    ).wait_recv()


def sent(src, sem, device):
    pltpu.make_async_remote_copy(
        src_ref=src, dst_ref=src, send_sem=sem, recv_sem=sem, device_id=device, device_id_type=MESH
    ).wait_send()


def layer_norm(field):
    mean = jnp.mean(field, axis=-1, keepdims=True)
    centered = field - mean
    var = jnp.mean(centered * centered, axis=-1, keepdims=True)
    return centered * lax.rsqrt(var + 1e-05)


def local_bias(normed, bias_w, spread, heads):
    flat = dot_nt(bias_w, normed)
    spread[...] = jnp.zeros_like(spread)
    for r in range(24):
        row, lane = (r, 0) if r < 8 else (r - 8, 0 if r >= 16 else 64)
        spread[4 * row : 4 * row + 4, lane : lane + 48] = flat[:, 48 * r : 48 * r + 48]
    for h in range(HEADS):
        heads[h] = spread[pl.ds(h, 16, stride=4), :].astype(BF16)


def join_columns(blocks):
    lane = iota(blocks[0].shape, 1)
    parts = []
    for first in (0, 64):
        tiles = [jnp.zeros(blocks[0].shape, F32) for _ in range(3)]
        for b, block in enumerate(blocks):
            tile, at = (48 * b) // 128, (48 * b) % 128
            piece = jnp.where((lane >= first) & (lane < first + 48), block, 0.0)
            if (at - first) % 128:
                piece = pltpu.roll(piece, (at - first) % 128, 1)
            if at + 48 <= 128:
                tiles[tile] = tiles[tile] + piece
            else:
                tiles[tile] = tiles[tile] + jnp.where(lane >= at, piece, 0.0)
                tiles[tile + 1] = tiles[tile + 1] + jnp.where(lane < at, piece, 0.0)
        parts.append(tiles)
    joined = []
    for base in range(0, blocks[0].shape[0], 16):
        near, far = slice(base, base + 8), slice(base + 8, base + 16)
        joined.append(
            [
                jnp.concatenate([a[near], b[near], a[far]], axis=0)
                for a, b in zip(parts[0], parts[1])
            ]
        )
    return joined


def pick(head, at):
    row, col = iota((128, 128), 0), iota((128, 128), 1)
    hit = (row - 32 * head == col - at) & (col >= at) & (col < at + 32)
    return jnp.where(hit, 1.0, 0.0).astype(BF16)


def spread_out(out_w, wide):
    wide[...] = jnp.zeros_like(wide)
    for h in range(HEADS):
        for a in range(3):
            wide[h * 128 + 32 * a : h * 128 + 32 * a + 32, a * 128 : a * 128 + 128] = out_w[
                32 * h : 32 * h + 32, :
            ]


NEAR = (0, 1, 3, 2)
FAR = (4, 3, 5, 2, 6, 1, 7, 0)


def scratch1():
    dma = pltpu.SemaphoreType.DMA
    return {
        "nrm": pltpu.VMEM((8, 144, C), BF16),
        "x1f": pltpu.VMEM((2, 2, 8, 144, C), BF16),
        "spread": pltpu.VMEM((64, C), F32),
        "hs": pltpu.VMEM((4, 16, C), BF16),
        "by": pltpu.VMEM((2, 2, 8, 16, C), BF16),
        "bf": pltpu.VMEM((4, 4, 48, 768), BF16),
        "wall": pltpu.VMEM((3, C, 512), BF16),
        "wide": pltpu.VMEM((512, 384), BF16),
        "q": pltpu.VMEM((6, 4, 4, 48, C), BF16),
        "k": pltpu.VMEM((6, 768, C), BF16),
        "v": pltpu.VMEM((6, 768, C), BF16),
        "g": pltpu.VMEM((2, 4, 4, 48, C), BF16),
        "rs": pltpu.VMEM((2, 4, 4, 48, C), BF16),
        "rx": pltpu.VMEM((8, 4, 48, C), BF16),
        "by_s": dma((2, 2, 8)),
        "by_r": dma((2, 2, 8)),
        "xy_s": dma((8,)),
        "xy_r": dma((8,)),
        "xz_s": dma((8,)),
        "xz_r": dma((8,)),
        "xc_s": dma((2,)),
        "xc_r": dma((2,)),
        "bz_s": dma((4,)),
        "bz_r": dma((4,)),
        "bx_s": dma((4, 4)),
        "bx_r": dma((4, 4)),
        "rt_s": dma((2, 4, 4)),
        "rt_r": dma((8, 4)),
    }


def partners(p):
    out = []
    for c in range(2):
        for z in range(2):
            for e in range(8):
                if (c, z, e) != (0, 0, 0):
                    out.append(p.dev(co=(p.co + c) % 2, zl=(p.zl + z) % 2, y=(p.y + e) % 8))
    for a in range(4):
        for b in range(4):
            if (a, b) == (0, 0):
                continue
            zh, x = (p.zh + a) % 4, (p.x + b) % 4
            for co in range(2):
                out.append(p.dev(zh=zh, x=x, co=co))
                out.append(p.dev(zh=zh, x=x, co=co, y=p.y1))
    for a in range(1, 4):
        out.append(p.dev(zh=(p.zh + a) % 4, zl=1 - p.zl))
    return out


def phase1(p, ready, src, mask, proj, bias_w, out_w, dst, nrm, nf, m):
    head = 2 * p.zl + p.co
    copies = []

    def norm_block(b, _):
        at = pl.multiple_of(b * 144, 16)
        m["nrm"][b] = layer_norm(src[pl.ds(at, 144), :]).astype(BF16)
        return 0

    lax.fori_loop(0, 8, norm_block, 0)
    local_bias(m["nrm"][...].reshape(1152, C), bias_w[...], m["spread"], m["hs"])
    ready()
    m["by"][p.co, p.zl, p.y] = m["hs"][head]
    for e in FAR:
        for c in range(2):
            for z in range(2):
                if (c, z, e) != (0, 0, 0):
                    co, zl, y = (p.co + c) % 2, (p.zl + z) % 2, (p.y + e) % 8
                    copies.append(
                        send(
                            m["hs"].at[2 * zl + co],
                            m["by"].at[p.co, p.zl, p.y],
                            m["by_s"].at[c, z, e],
                            m["by_r"].at[p.co, p.zl, p.y],
                            p.dev(co=co, zl=zl, y=y),
                        )
                    )
    for d in FAR[:7]:
        to = (p.y + d) % 8
        copies.append(
            send(
                m["nrm"].at[to],
                m["x1f"].at[p.co, p.zl, p.y],
                m["xy_s"].at[d],
                m["xy_r"].at[p.y],
                p.dev(y=to),
            )
        )
    m["x1f"][p.co, p.zl, p.y] = m["nrm"][p.y]

    for a in range(3):
        first, here = pick(head, 0), pick(head, 32 * a)
        m["wall"][a, :, 0:128] = dot(proj[:, 0:128], first).astype(BF16)
        m["wall"][a, :, 128:256] = dot(proj[:, 128:256], first).astype(BF16)
        m["wall"][a, :, 256:384] = dot(proj[:, 256:384], here).astype(BF16)
        m["wall"][a, :, 384:512] = dot(proj[:, 384:512], here).astype(BF16)
    spread_out(out_w, m["wide"])

    for e in FAR:
        for c in range(2):
            for z in range(2):
                if (c, z, e) != (0, 0, 0):
                    co, zl, y = (p.co + c) % 2, (p.zl + z) % 2, (p.y + e) % 8
                    got(m["by"].at[co, zl, y], m["by_r"].at[co, zl, y], p.dev(co=co, zl=zl, y=y))
    joined = join_columns([m["by"][:, :, y].reshape(64, C).astype(F32) for y in range(8)])
    whole = jnp.concatenate(
        [
            jnp.concatenate([joined[z][j], joined[2 + z][j]], axis=0)
            for z in range(2)
            for j in range(3)
        ],
        axis=1,
    )
    m["bf"][p.x, p.zh] = jnp.where(mask[...].reshape(1, 768) > 0, whole, NEG).astype(BF16)

    def to_columns(zh):
        block = m["bf"].at[p.x, zh]
        for d in NEAR[1:]:
            copies.append(
                send(
                    block,
                    block,
                    m["bx_s"].at[d, zh],
                    m["bx_r"].at[p.x, zh],
                    p.dev(x=(p.x + d) % 4),
                )
            )

    mine = m["bf"].at[p.x, p.zh]
    for d in NEAR[1:]:
        copies.append(
            send(mine, mine, m["bz_s"].at[d], m["bz_r"].at[p.zh], p.dev(zh=(p.zh + d) % 4))
        )
    to_columns(p.zh)
    for d in range(8):
        fr = (p.y + d) % 8
        block = m["x1f"].at[p.co, p.zl, fr]
        if d:
            got(block, m["xy_r"].at[fr], p.dev(y=fr))
        copies.append(
            send(block, block, m["xz_s"].at[d], m["xz_r"].at[fr], p.dev(zl=(p.zl + 1) % 2))
        )
    half = m["x1f"].at[p.co, p.zl]
    copies.append(
        send(half, half, m["xc_s"].at[0], m["xc_r"].at[p.zl], p.dev(co=(p.co + 1) % 2))
    )

    for d in NEAR[1:]:
        zh = (p.zh + d) % 4
        got(m["bf"].at[p.x, zh], m["bz_r"].at[zh], p.dev(zh=zh))
        to_columns(zh)
    other = (p.zl + 1) % 2
    for d in range(8):
        fr = (p.y + d) % 8
        got(m["x1f"].at[p.co, other, fr], m["xz_r"].at[fr], p.dev(zl=other))
    half = m["x1f"].at[p.co, other]
    copies.append(
        send(half, half, m["xc_s"].at[1], m["xc_r"].at[other], p.dev(co=(p.co + 1) % 2))
    )

    lane = iota((768, C), 1)

    def prepare(t, _):
        co = (p.co + t) % 2

        @pl.when(t == 1)
        def _():
            for zl in range(2):
                got(m["x1f"].at[co, zl], m["xc_r"].at[zl], p.dev(co=co))

        gate = jnp.zeros((768, C), F32)
        for a in range(3):
            rows = m["x1f"][co, :, :, a * 48 : a * 48 + 48, :].reshape(768, C)
            mixed = dot(rows, m["wall"][a])
            item = 3 * co + a
            query = (mixed[:, 0:128] * HD ** (-0.5)).astype(BF16)
            m["q"][item] = query.reshape(4, 4, 48, C)
            m["k"][item] = mixed[:, 128:256].astype(BF16)
            value = jnp.where(lane == 96 + a, 1.0, mixed[:, 256:384])
            m["v"][item] = value.astype(BF16)
            gate = gate + mixed[:, 384:512]
        gate = jnp.where(lane < 96, jax.nn.sigmoid(gate), 0.0)
        m["g"][co] = gate.astype(BF16).reshape(4, 4, 48, C)
        return 0

    lax.fori_loop(0, 2, prepare, 0)

    lane = iota((192, C), 1)

    def attend(t, _):
        s, co = t // 2, t % 2
        x = (p.x + s + jnp.where(s == 2, 1, 0) - jnp.where(s == 3, 1, 0)) % 4

        @pl.when((s > 0) & (co == 0))
        def _():
            for zh in range(4):
                got(m["bf"].at[x, zh], m["bx_r"].at[x, zh], p.dev(x=x))

        bias = m["bf"][x].reshape(192, 768)
        out = jnp.zeros((192, C), F32)
        for a in range(3):
            item = 3 * co + a
            query = m["q"][item, :, x].reshape(192, C)
            scores = dot_nt(query, m["k"][item]) + bias.astype(F32)
            top = jnp.max(scores, axis=-1, keepdims=True)
            weights = jnp.exp(scores - top).astype(BF16)
            out = out + dot(weights, m["v"][item])
        inv = [1.0 / out[:, 96 + a : 97 + a] for a in range(3)]
        scale = jnp.where(lane < 32, inv[0], jnp.where(lane < 64, inv[1], inv[2]))
        gated = out * scale * m["g"][co, :, x].reshape(192, C).astype(F32)
        m["rs"][co, :, x] = gated.astype(BF16).reshape(4, 48, C)
        for zh in range(4):
            zl, y = zh // 2, (zh % 2) * 4 + x
            self = (co == p.co) & (zl == p.zl) & (y == p.y)

            @pl.when(self)
            def _():
                m["rx"][p.y, head] = m["rs"][co, zh, x]

            @pl.when(jnp.logical_not(self))
            def _():
                send(
                    m["rs"].at[co, zh, x],
                    m["rx"].at[p.y, head],
                    m["rt_s"].at[co, zh, x],
                    m["rt_r"].at[p.y, head],
                    p.dev(co=co, zl=zl, y=y),
                )

        return 0

    lax.fori_loop(0, 8, attend, 0)

    def finish(y, _):
        for h in range(HEADS):

            @pl.when(jnp.logical_not((y == p.y) & (h == head)))
            def _():
                got(m["rx"].at[y, h], m["rt_r"].at[y, h], p.dev(co=h % 2, zl=h // 2, y=y))

        rows = jnp.concatenate([m["rx"][y, h] for h in range(HEADS)], axis=1)
        update = dot(rows, m["wide"][...])
        for a in range(3):
            at = pl.multiple_of((3 * y + a) * 48, 16)
            mid = src[pl.ds(at, 48), :] + update[:, a * 128 : a * 128 + 128]
            dst[pl.ds(at, 48), :] = mid
            normed = layer_norm(mid).astype(BF16)
            nrm[pl.ds(at, 48), :] = normed
            nf[pl.ds(at, 48), :] = normed.astype(F32)
        return 0

    lax.fori_loop(0, 8, finish, 0)

    def leave(t, _):
        co, zh, x = t // 16, (t // 4) % 4, t % 4
        zl, y = zh // 2, (zh % 2) * 4 + x

        @pl.when(jnp.logical_not((co == p.co) & (zl == p.zl) & (y == p.y)))
        def _():
            sent(m["rs"].at[co, zh, x], m["rt_s"].at[co, zh, x], p.dev(co=co, zl=zl, y=y))

        return 0

    def close():
        for copy in copies:
            copy.wait_send()
        lax.fori_loop(0, 32, leave, 0)

    return close


def scratch2():
    dma = pltpu.SemaphoreType.DMA
    return {
        "nrm": pltpu.VMEM((1152, C), BF16),
        "nf": pltpu.VMEM((1152, C), F32),
        "ns": pltpu.VMEM((4, 4, 80, C), BF16),
        "x2": pltpu.VMEM((2, 2, 4, 4, 80, C), BF16),
        "xx": pltpu.VMEM((6, 16, 48, C), BF16),
        "spread": pltpu.VMEM((64, C), F32),
        "hs": pltpu.VMEM((4, 16, C), BF16),
        "by": pltpu.VMEM((2, 8, 16, C), BF16),
        "b2": pltpu.VMEM((4, 4, 2, 48, 384), BF16),
        "wk": pltpu.VMEM((C, C), BF16),
        "wt": pltpu.VMEM((C, C), BF16),
        "wide": pltpu.VMEM((512, 384), BF16),
        "qt": pltpu.VMEM((6, 2, C, 384), BF16),
        "k": pltpu.VMEM((6, 768, C), BF16),
        "vt": pltpu.VMEM((6, 48, 768), BF16),
        "gt": pltpu.VMEM((6, 2, 32, 384), BF16),
        "ot": pltpu.VMEM((C, 384), BF16),
        "tr": pltpu.VMEM((384, C), F32),
        "rs": pltpu.VMEM((2, 2, 8, 48, C), BF16),
        "rx": pltpu.VMEM((2, 4, 4, 2, 48, C), BF16),
        "by_s": dma((2, 8)),
        "by_r": dma((2, 8)),
        "xa_s": dma((4, 4)),
        "xa_r": dma((4, 4)),
        "xy_s": dma((4, 4)),
        "xy_r": dma((4, 4)),
        "xc_s": dma((2,)),
        "xc_r": dma((2,)),
        "bz_s": dma((4, 2)),
        "bz_r": dma((4, 2)),
        "bx_s": dma((4, 4, 2)),
        "bx_r": dma((4, 4, 2)),
        "rt_s": dma((2, 2, 8)),
        "rt_r": dma((4, 4, 2)),
        "rc_s": dma((4,)),
        "rc_r": dma((4,)),
    }


def pick_rows(head, at):
    row, col = iota((128, 128), 0), iota((128, 128), 1)
    hit = (row - at == col - 32 * head) & (row >= at) & (row < at + 32)
    return jnp.where(hit, 1.0, 0.0).astype(BF16)


def phase2(p, src, mask, proj, bias_w, out_w, dst, m):
    head = 2 * p.yl + p.co
    other = 1 - p.co
    copies = []

    local_bias(m["nrm"][...], bias_w[...], m["spread"], m["hs"])
    m["by"][p.co, p.y] = m["hs"][head]
    for e in FAR:
        for c in range(2):
            if (c, e) != (0, 0):
                co, y = (p.co + c) % 2, (p.y + e) % 8
                copies.append(
                    send(
                        m["hs"].at[2 * (y % 2) + co],
                        m["by"].at[p.co, p.y],
                        m["by_s"].at[c, e],
                        m["by_r"].at[p.co, p.y],
                        p.dev(co=co, y=y),
                    )
                )

    for a in (2, 1, 3, 0):
        for b in (2, 1, 3, 0):
            zh, x = (p.zh + a) % 4, (p.x + b) % 4
            first = 3 * (zh * 4 + x)
            rows = [m["nf"][pl.ds(first + i, 24, stride=48), :] for i in range(3)]
            rows.append(jnp.zeros((8, C), F32))
            m["ns"][zh, x] = jnp.concatenate(rows, axis=0).astype(BF16)
            if (a, b) == (0, 0):
                m["x2"][p.yl, p.co, p.zh, p.x] = m["ns"][zh, x]
            else:
                copies.append(
                    send(
                        m["ns"].at[zh, x],
                        m["x2"].at[p.yl, p.co, p.zh, p.x],
                        m["xa_s"].at[a, b],
                        m["xa_r"].at[p.zh, p.x],
                        p.dev(zh=zh, x=x),
                    )
                )

    m["wk"][...] = dot(proj[:, 128:256], pick(head, 0)).astype(BF16)
    wt = dot_nt(pick_rows(head, 0), proj[:, 0:128])
    wt = wt + dot_nt(pick_rows(head, 32), proj[:, 256:384])
    wt = wt + dot_nt(pick_rows(head, 64), proj[:, 384:512])
    m["wt"][...] = wt.astype(BF16)
    spread_out(out_w, m["wide"])

    row, col = iota((48, 768), 0), iota((48, 768), 1)
    keep = jnp.where(col == row + 48 * (4 * p.zh + p.x), mask[...].reshape(1, 768), 0)
    keep = jnp.sum(keep.astype(F32), axis=1, keepdims=True)
    for e in FAR:
        for c in range(2):
            if (c, e) != (0, 0):
                co, y = (p.co + c) % 2, (p.y + e) % 8
                got(m["by"].at[co, y], m["by_r"].at[co, y], p.dev(co=co, y=y))
    joined = join_columns([m["by"][:, y].reshape(32, C).astype(F32) for y in range(8)])
    whole = jnp.concatenate(
        [jnp.concatenate([joined[0][j], joined[1][j]], axis=0) for j in range(3)], axis=1
    )
    m["b2"][p.zh, p.x, p.zl] = jnp.where(keep > 0.5, whole, NEG).astype(BF16)

    def to_columns(zh, zl):
        block = m["b2"].at[zh, p.x, zl]
        for d in NEAR[1:]:
            copies.append(
                send(
                    block,
                    block,
                    m["bx_s"].at[d, zh, zl],
                    m["bx_r"].at[p.x, zh, zl],
                    p.dev(x=(p.x + d) % 4),
                )
            )

    mine = m["b2"].at[p.zh, p.x, p.zl]
    for z in range(2):
        for a in NEAR:
            if (a, z) != (0, 0):
                zh, zl = (p.zh + a) % 4, (p.zl + z) % 2
                copies.append(
                    send(
                        mine,
                        mine,
                        m["bz_s"].at[a, z],
                        m["bz_r"].at[p.zh, p.zl],
                        p.dev(zh=zh, zl=zl),
                    )
                )
    to_columns(p.zh, p.zl)

    for a in NEAR:
        for b in NEAR:
            zh, x = (p.zh + a) % 4, (p.x + b) % 4
            block = m["x2"].at[p.yl, p.co, zh, x]
            if (a, b) != (0, 0):
                got(block, m["xa_r"].at[zh, x], p.dev(zh=zh, x=x))
            copies.append(
                send(block, block, m["xy_s"].at[a, b], m["xy_r"].at[zh, x], p.dev(y=p.y1))
            )
    part = m["x2"].at[p.yl, p.co]
    copies.append(send(part, part, m["xc_s"].at[0], m["xc_r"].at[p.yl], p.dev(co=other)))

    for z in range(2):
        for a in NEAR:
            if (a, z) != (0, 0):
                zh, zl = (p.zh + a) % 4, (p.zl + z) % 2
                got(m["b2"].at[zh, p.x, zl], m["bz_r"].at[zh, zl], p.dev(zh=zh, zl=zl))
                to_columns(zh, zl)

    for a in NEAR:
        for b in NEAR:
            zh, x = (p.zh + a) % 4, (p.x + b) % 4
            got(m["x2"].at[1 - p.yl, p.co, zh, x], m["xy_r"].at[zh, x], p.dev(y=p.y1))
    part = m["x2"].at[1 - p.yl, p.co]
    copies.append(send(part, part, m["xc_s"].at[1], m["xc_r"].at[1 - p.yl], p.dev(co=other)))

    sub = iota((16, 768), 0)
    ones = jnp.where(sub == 0, 1.0, 0.0)

    def prepare(t, _):
        yl = (p.yl + t) % 2
        got(m["x2"].at[yl, other], m["xc_r"].at[yl], p.dev(co=other))

        def arrange(n, _):
            zh, x = n // 4, n % 4
            cores = [m["x2"][yl, c, zh, x].astype(F32) for c in range(2)]
            for b in range(3):
                rows = [core[24 * b : 24 * b + 24] for core in cores]
                m["xx"][3 * yl + b, n] = jnp.concatenate(rows, axis=0).astype(BF16)
            return 0

        lax.fori_loop(0, 16, arrange, 0)
        for b in range(3):
            item = 3 * yl + b
            rows = m["xx"][item].reshape(768, C)
            m["k"][item] = dot(rows, m["wk"][...]).astype(BF16)
            mixed = dot_nt(m["wt"][...], rows)
            query = (mixed * HD ** (-0.5)).astype(BF16)
            gate = jax.nn.sigmoid(mixed[64:96]).astype(BF16)
            for z in range(2):
                m["qt"][item, z] = query[:, 384 * z : 384 * z + 384]
                m["gt"][item, z] = gate[:, 384 * z : 384 * z + 384]
            m["vt"][item] = jnp.concatenate([mixed[32:64], ones], axis=0).astype(BF16)
        return 0

    lax.fori_loop(0, 2, prepare, 0)

    m["ot"][...] = jnp.zeros_like(m["ot"])
    eye = jnp.where(iota((128, 128), 0) == iota((128, 128), 1), 1.0, 0.0).astype(BF16)

    def attend(t, _):
        z, yl = (p.zl + t // 2) % 2, t % 2

        @pl.when(yl == 0)
        def _():
            for d in range(1, 4):
                x = (p.x + d) % 4
                for zh in range(4):
                    got(m["b2"].at[zh, x, z], m["bx_r"].at[x, zh, z], p.dev(x=x))

        bias = m["b2"][:, :, z].reshape(768, 384)
        for b in range(3):
            item = 3 * yl + b
            scores = dot(m["k"][item], m["qt"][item, z]) + bias.astype(F32)
            top = jnp.max(scores, axis=0, keepdims=True)
            weights = jnp.exp(scores - top).astype(BF16)
            out = dot(m["vt"][item], weights)
            gated = out[0:32] / out[32:33] * m["gt"][item, z].astype(F32)
            m["ot"][32 * b : 32 * b + 32, :] = gated.astype(BF16)
        for j in range(3):
            m["tr"][128 * j : 128 * j + 128, :] = dot_nt(eye, m["ot"][:, 128 * j : 128 * j + 128])
        y = p.y - p.yl + yl
        for n in range(8):
            zh, x = 2 * z + n // 4, n % 4
            m["rs"][z, yl, n] = m["tr"][48 * n : 48 * n + 48, :].astype(BF16)
            self = (zh == p.zh) & (p.x == x) & (yl == p.yl)

            @pl.when(self)
            def _():
                m["rx"][p.co, p.zh, p.x, p.yl] = m["rs"][z, yl, n]

            @pl.when(jnp.logical_not(self))
            def _():
                send(
                    m["rs"].at[z, yl, n],
                    m["rx"].at[p.co, p.zh, p.x, p.yl],
                    m["rt_s"].at[z, yl, n],
                    m["rt_r"].at[p.zh, p.x, p.yl],
                    p.dev(zh=zh, x=x, y=y),
                )

        return 0

    lax.fori_loop(0, 4, attend, 0)

    for d in NEAR:
        zh = (p.zh + d) % 4
        for x in range(4):
            for yl in range(2):

                @pl.when(jnp.logical_not((zh == p.zh) & (x == p.x) & (yl == p.yl)))
                def _():
                    got(
                        m["rx"].at[p.co, zh, x, yl],
                        m["rt_r"].at[zh, x, yl],
                        p.dev(zh=zh, x=x, y=p.y - p.yl + yl),
                    )

        part = m["rx"].at[p.co, zh]
        copies.append(send(part, part, m["rc_s"].at[d], m["rc_r"].at[zh], p.dev(co=other)))

    def finish(t, _):
        zh = (p.zh + t + jnp.where(t == 2, 1, 0) - jnp.where(t == 3, 1, 0)) % 4
        got(m["rx"].at[other, zh], m["rc_r"].at[zh], p.dev(co=other))
        rows = [m["rx"][h % 2, zh, :, h // 2].reshape(192, C) for h in range(HEADS)]
        update = dot(jnp.concatenate(rows, axis=1), m["wide"][...])
        for x in range(4):
            for b in range(3):
                chip = update[48 * x : 48 * x + 48, b * 128 : b * 128 + 128]
                at = pl.ds(3 * (4 * zh + x) + b, 24, stride=48)
                dst[at, :] = src[at, :] + jnp.where(p.co == 0, chip[0:24], chip[24:48])
        return 0

    lax.fori_loop(0, 4, finish, 0)

    def leave(t, _):
        z, yl, n = t // 16, (t // 8) % 2, t % 8
        zh, x = 2 * z + n // 4, n % 4
        y = p.y - p.yl + yl

        @pl.when(jnp.logical_not((zh == p.zh) & (x == p.x) & (yl == p.yl)))
        def _():
            sent(m["rs"].at[z, yl, n], m["rt_s"].at[z, yl, n], p.dev(zh=zh, x=x, y=y))

        return 0

    def close():
        for copy in copies:
            copy.wait_send()
        lax.fori_loop(0, 32, leave, 0)

    return close


def kernel(
    names1, names2, pair, mask, proj1, bias1_w, out1_w, proj2, bias2_w, out2_w, dst, mid, *refs
):
    m1 = dict(zip(names1, refs))
    m2 = dict(zip(names2, refs[len(names1) :]))
    p = Place()
    others = partners(p)
    barrier = pltpu.get_barrier_semaphore()
    for device in others:
        pl.semaphore_signal(barrier, inc=1, device_id=device, device_id_type=MESH)

    def ready():
        pl.semaphore_wait(barrier, len(others))

    nrm, nf = m2["nrm"], m2["nf"]
    close1 = phase1(p, ready, pair, mask, proj1, bias1_w, out1_w, mid, nrm, nf, m1)
    close2 = phase2(p, mid, mask, proj2, bias2_w, out2_w, dst, m2)
    close1()
    close2()


def shards(pair, residue_mask, start_proj, start_bias_w, start_out, end_proj, end_bias_w, end_out):
    rows, cols = pair.shape[:2]
    one, two = scratch1(), scratch2()
    vmem = pl.BlockSpec(memory_space=pltpu.VMEM)
    out = pl.pallas_call(
        functools.partial(kernel, tuple(one), tuple(two)),
        out_shape=jax.ShapeDtypeStruct((rows * cols, C), F32),
        in_specs=[vmem] * 8,
        out_specs=vmem,
        scratch_shapes=[pltpu.VMEM((rows * cols, C), F32)] + list(one.values()) + list(two.values()),
        compiler_params=pltpu.CompilerParams(
            collective_id=0, has_side_effects=True, vmem_limit_bytes=56 << 20
        ),
        name="triangle_attention",
    )(
        pair.reshape(rows * cols, C),
        residue_mask,
        start_proj,
        start_bias_w.T,
        start_out,
        end_proj,
        end_bias_w.T,
        end_out,
    )
    return out.reshape(rows, cols, C)


def solution(mesh):
    placed = (P("row", "col", None), P(), P(), P(), P(), P(), P(), P())
    return jax.shard_map(
        shards, mesh=mesh, in_specs=placed, out_specs=P("row", "col", None), check_vma=False
    )
```

```python
import functools

import jax
import jax.numpy as jnp
from jax import lax
from jax.experimental import pallas as pl
from jax.experimental.pallas import tpu as pltpu
from jax.sharding import PartitionSpec as P

C = 128
HEADS = 4
HD = 32
MESH = pl.DeviceIdType.MESH
F32 = jnp.float32
BF16 = jnp.bfloat16
NT = (((1,), (1,)), ((), ()))
NEG = -1000000000.0


def iota(shape, dim):
    return lax.broadcasted_iota(jnp.int32, shape, dim)


def dot(a, b):
    return jnp.dot(a, b, preferred_element_type=F32)


def dot_nt(a, b):
    return lax.dot_general(a, b, NT, preferred_element_type=F32)


class Place:
    def __init__(self):
        r, c = lax.axis_index("row"), lax.axis_index("col")
        self.zh, self.x, self.co = r // 8, (r // 2) % 4, r % 2
        self.zl, self.y = c // 8, c % 8
        self.yl = self.y % 2
        self.y1 = self.y + 1 - 2 * self.yl

    def dev(self, zh=None, x=None, co=None, zl=None, y=None):
        zh = self.zh if zh is None else zh
        x = self.x if x is None else x
        co = self.co if co is None else co
        zl = self.zl if zl is None else zl
        y = self.y if y is None else y
        return (zh * 8 + x * 2 + co, zl * 8 + y)


def send(src, dst, ssem, rsem, device):
    copy = pltpu.make_async_remote_copy(
        src_ref=src, dst_ref=dst, send_sem=ssem, recv_sem=rsem, device_id=device, device_id_type=MESH
    )
    copy.start()
    return copy


def got(dst, sem, device):
    pltpu.make_async_remote_copy(
        src_ref=dst, dst_ref=dst, send_sem=sem, recv_sem=sem, device_id=device, device_id_type=MESH
    ).wait_recv()


def sent(src, sem, device):
    pltpu.make_async_remote_copy(
        src_ref=src, dst_ref=src, send_sem=sem, recv_sem=sem, device_id=device, device_id_type=MESH
    ).wait_send()


def layer_norm(field):
    mean = jnp.mean(field, axis=-1, keepdims=True)
    centered = field - mean
    var = jnp.mean(centered * centered, axis=-1, keepdims=True)
    return centered * lax.rsqrt(var + 1e-05)


def local_bias(normed, bias_w, spread, heads):
    flat = dot_nt(bias_w, normed)
    spread[...] = jnp.zeros_like(spread)
    for r in range(24):
        row, lane = (r, 0) if r < 8 else (r - 8, 0 if r >= 16 else 64)
        spread[4 * row : 4 * row + 4, lane : lane + 48] = flat[:, 48 * r : 48 * r + 48]
    for h in range(HEADS):
        heads[h] = spread[pl.ds(h, 16, stride=4), :].astype(BF16)


def join_columns(blocks):
    lane = iota(blocks[0].shape, 1)
    parts = []
    for first in (0, 64):
        tiles = [jnp.zeros(blocks[0].shape, F32) for _ in range(3)]
        for b, block in enumerate(blocks):
            tile, at = (48 * b) // 128, (48 * b) % 128
            piece = jnp.where((lane >= first) & (lane < first + 48), block, 0.0)
            if (at - first) % 128:
                piece = pltpu.roll(piece, (at - first) % 128, 1)
            if at + 48 <= 128:
                tiles[tile] = tiles[tile] + piece
            else:
                tiles[tile] = tiles[tile] + jnp.where(lane >= at, piece, 0.0)
                tiles[tile + 1] = tiles[tile + 1] + jnp.where(lane < at, piece, 0.0)
        parts.append(tiles)
    joined = []
    for base in range(0, blocks[0].shape[0], 16):
        near, far = slice(base, base + 8), slice(base + 8, base + 16)
        joined.append(
            [
                jnp.concatenate([a[near], b[near], a[far]], axis=0)
                for a, b in zip(parts[0], parts[1])
            ]
        )
    return joined


def pick(head, at):
    row, col = iota((128, 128), 0), iota((128, 128), 1)
    hit = (row - 32 * head == col - at) & (col >= at) & (col < at + 32)
    return jnp.where(hit, 1.0, 0.0).astype(BF16)


def spread_out(out_w, wide):
    wide[...] = jnp.zeros_like(wide)
    for h in range(HEADS):
        for a in range(3):
            wide[h * 128 + 32 * a : h * 128 + 32 * a + 32, a * 128 : a * 128 + 128] = out_w[
                32 * h : 32 * h + 32, :
            ]


NEAR = (0, 1, 3, 2)
FAR = (4, 3, 5, 2, 6, 1, 7, 0)
CLOSE = FAR[::-1]


def scratch1():
    dma = pltpu.SemaphoreType.DMA
    return {
        "nrm": pltpu.VMEM((8, 144, C), BF16),
        "x1f": pltpu.VMEM((2, 2, 8, 144, C), BF16),
        "spread": pltpu.VMEM((64, C), F32),
        "hs": pltpu.VMEM((4, 16, C), BF16),
        "by": pltpu.VMEM((2, 2, 8, 16, C), BF16),
        "bf": pltpu.VMEM((4, 4, 48, 768), BF16),
        "wall": pltpu.VMEM((3, C, 512), BF16),
        "wide": pltpu.VMEM((512, 384), BF16),
        "q": pltpu.VMEM((6, 4, 4, 48, C), BF16),
        "k": pltpu.VMEM((6, 768, C), BF16),
        "v": pltpu.VMEM((6, 768, C), BF16),
        "g": pltpu.VMEM((2, 4, 4, 48, C), BF16),
        "rs": pltpu.VMEM((2, 4, 4, 48, C), BF16),
        "rx": pltpu.VMEM((8, 4, 48, C), BF16),
        "by_s": dma((2, 2, 8)),
        "by_r": dma((2, 2, 8)),
        "xy_s": dma((8,)),
        "xy_r": dma((8,)),
        "xz_s": dma((8,)),
        "xz_r": dma((8,)),
        "xc_s": dma((2, 8)),
        "xc_r": dma((2, 8)),
        "bz_s": dma((4,)),
        "bz_r": dma((4,)),
        "bx_s": dma((4, 4)),
        "bx_r": dma((4, 4)),
        "rt_s": dma((2, 4, 4)),
        "rt_r": dma((8, 4)),
    }


def partners(p):
    out = []
    for e in FAR:
        for c in range(2):
            for z in range(2):
                if (c, z, e) != (0, 0, 0):
                    out.append(p.dev(co=(p.co + c) % 2, zl=(p.zl + z) % 2, y=(p.y + e) % 8))
    for d in range(1, 4):
        out.append(p.dev(zh=(p.zh + d) % 4))
        out.append(p.dev(x=(p.x + d) % 4))
    return out


def phase1(p, ready, src, mask, proj, bias_w, out_w, dst, nrm, nf, m):
    head = 2 * p.zl + p.co
    copies = []

    def norm_block(b, _):
        at = pl.multiple_of(b * 144, 16)
        m["nrm"][b] = layer_norm(src[pl.ds(at, 144), :]).astype(BF16)
        return 0

    lax.fori_loop(0, 8, norm_block, 0)
    local_bias(m["nrm"][...].reshape(1152, C), bias_w[...], m["spread"], m["hs"])
    ready()
    m["by"][p.co, p.zl, p.y] = m["hs"][head]
    for e in FAR:
        for c in range(2):
            for z in range(2):
                if (c, z, e) != (0, 0, 0):
                    co, zl, y = (p.co + c) % 2, (p.zl + z) % 2, (p.y + e) % 8
                    copies.append(
                        send(
                            m["hs"].at[2 * zl + co],
                            m["by"].at[p.co, p.zl, p.y],
                            m["by_s"].at[c, z, e],
                            m["by_r"].at[p.co, p.zl, p.y],
                            p.dev(co=co, zl=zl, y=y),
                        )
                    )
    for d in FAR[:7]:
        to = (p.y + d) % 8
        copies.append(
            send(
                m["nrm"].at[to],
                m["x1f"].at[p.co, p.zl, p.y],
                m["xy_s"].at[d],
                m["xy_r"].at[p.y],
                p.dev(y=to),
            )
        )
    m["x1f"][p.co, p.zl, p.y] = m["nrm"][p.y]

    for a in range(3):
        first, here = pick(head, 0), pick(head, 32 * a)
        m["wall"][a, :, 0:128] = dot(proj[:, 0:128], first).astype(BF16)
        m["wall"][a, :, 128:256] = dot(proj[:, 128:256], first).astype(BF16)
        m["wall"][a, :, 256:384] = dot(proj[:, 256:384], here).astype(BF16)
        m["wall"][a, :, 384:512] = dot(proj[:, 384:512], here).astype(BF16)
    spread_out(out_w, m["wide"])

    for e in FAR:
        for c in range(2):
            for z in range(2):
                if (c, z, e) != (0, 0, 0):
                    co, zl, y = (p.co + c) % 2, (p.zl + z) % 2, (p.y + e) % 8
                    got(m["by"].at[co, zl, y], m["by_r"].at[co, zl, y], p.dev(co=co, zl=zl, y=y))
    joined = join_columns([m["by"][:, :, y].reshape(64, C).astype(F32) for y in range(8)])
    whole = jnp.concatenate(
        [
            jnp.concatenate([joined[z][j], joined[2 + z][j]], axis=0)
            for z in range(2)
            for j in range(3)
        ],
        axis=1,
    )
    m["bf"][p.x, p.zh] = jnp.where(mask[...].reshape(1, 768) > 0, whole, NEG).astype(BF16)

    def to_columns(zh):
        block = m["bf"].at[p.x, zh]
        for d in NEAR[1:]:
            copies.append(
                send(
                    block,
                    block,
                    m["bx_s"].at[d, zh],
                    m["bx_r"].at[p.x, zh],
                    p.dev(x=(p.x + d) % 4),
                )
            )

    mine = m["bf"].at[p.x, p.zh]
    for d in NEAR[1:]:
        copies.append(
            send(mine, mine, m["bz_s"].at[d], m["bz_r"].at[p.zh], p.dev(zh=(p.zh + d) % 4))
        )
    to_columns(p.zh)
    for d in CLOSE:
        fr = (p.y + d) % 8
        block = m["x1f"].at[p.co, p.zl, fr]
        if d:
            got(block, m["xy_r"].at[fr], p.dev(y=fr))
        copies.append(
            send(block, block, m["xz_s"].at[d], m["xz_r"].at[fr], p.dev(zl=(p.zl + 1) % 2))
        )
        copies.append(
            send(block, block, m["xc_s"].at[0, d], m["xc_r"].at[p.zl, fr], p.dev(co=1 - p.co))
        )

    for d in NEAR[1:]:
        zh = (p.zh + d) % 4
        got(m["bf"].at[p.x, zh], m["bz_r"].at[zh], p.dev(zh=zh))
        to_columns(zh)
    other = (p.zl + 1) % 2
    for d in CLOSE:
        fr = (p.y + d) % 8
        block = m["x1f"].at[p.co, other, fr]
        got(block, m["xz_r"].at[fr], p.dev(zl=other))
        copies.append(
            send(block, block, m["xc_s"].at[1, d], m["xc_r"].at[other, fr], p.dev(co=1 - p.co))
        )

    lane = iota((768, C), 1)

    def prepare(t, _):
        co = (p.co + t) % 2

        @pl.when(t == 1)
        def _():
            for zl in range(2):
                for y in range(8):
                    got(m["x1f"].at[co, zl, y], m["xc_r"].at[zl, y], p.dev(co=co))

        gate = jnp.zeros((768, C), F32)
        for a in range(3):
            rows = m["x1f"][co, :, :, a * 48 : a * 48 + 48, :].reshape(768, C)
            mixed = dot(rows, m["wall"][a])
            item = 3 * co + a
            query = (mixed[:, 0:128] * HD ** (-0.5)).astype(BF16)
            m["q"][item] = query.reshape(4, 4, 48, C)
            m["k"][item] = mixed[:, 128:256].astype(BF16)
            value = jnp.where(lane == 96 + a, 1.0, mixed[:, 256:384])
            m["v"][item] = value.astype(BF16)
            gate = gate + mixed[:, 384:512]
        gate = jnp.where(lane < 96, jax.nn.sigmoid(gate), 0.0)
        m["g"][co] = gate.astype(BF16).reshape(4, 4, 48, C)
        return 0

    lax.fori_loop(0, 2, prepare, 0)

    lane = iota((192, C), 1)

    def attend(t, _):
        s, co = t // 2, t % 2
        x = (p.x + s + jnp.where(s == 2, 1, 0) - jnp.where(s == 3, 1, 0)) % 4

        @pl.when((s > 0) & (co == 0))
        def _():
            for zh in range(4):
                got(m["bf"].at[x, zh], m["bx_r"].at[x, zh], p.dev(x=x))

        bias = m["bf"][x].reshape(192, 768)
        out = jnp.zeros((192, C), F32)
        for a in range(3):
            item = 3 * co + a
            query = m["q"][item, :, x].reshape(192, C)
            scores = dot_nt(query, m["k"][item]) + bias.astype(F32)
            top = jnp.max(scores, axis=-1, keepdims=True)
            weights = jnp.exp(scores - top).astype(BF16)
            out = out + dot(weights, m["v"][item])
        inv = [1.0 / out[:, 96 + a : 97 + a] for a in range(3)]
        scale = jnp.where(lane < 32, inv[0], jnp.where(lane < 64, inv[1], inv[2]))
        gated = out * scale * m["g"][co, :, x].reshape(192, C).astype(F32)
        m["rs"][co, :, x] = gated.astype(BF16).reshape(4, 48, C)
        for zh in range(4):
            zl, y = zh // 2, (zh % 2) * 4 + x
            self = (co == p.co) & (zl == p.zl) & (y == p.y)

            @pl.when(self)
            def _():
                m["rx"][p.y, head] = m["rs"][co, zh, x]

            @pl.when(jnp.logical_not(self))
            def _():
                send(
                    m["rs"].at[co, zh, x],
                    m["rx"].at[p.y, head],
                    m["rt_s"].at[co, zh, x],
                    m["rt_r"].at[p.y, head],
                    p.dev(co=co, zl=zl, y=y),
                )

        return 0

    lax.fori_loop(0, 8, attend, 0)

    def finish(t, _):
        y = (p.y + (1 - 2 * (t % 2)) * (t // 2) - t % 2 + 8) % 8
        for h in range(HEADS):

            @pl.when(jnp.logical_not((y == p.y) & (h == head)))
            def _():
                got(m["rx"].at[y, h], m["rt_r"].at[y, h], p.dev(co=h % 2, zl=h // 2, y=y))

        rows = jnp.concatenate([m["rx"][y, h] for h in range(HEADS)], axis=1)
        update = dot(rows, m["wide"][...])
        for a in range(3):
            at = pl.multiple_of((3 * y + a) * 48, 16)
            mid = src[pl.ds(at, 48), :] + update[:, a * 128 : a * 128 + 128]
            dst[pl.ds(at, 48), :] = mid
            normed = layer_norm(mid).astype(BF16)
            nrm[pl.ds(at, 48), :] = normed
            nf[pl.ds(at, 48), :] = normed.astype(F32)
        return 0

    lax.fori_loop(0, 8, finish, 0)

    def leave(t, _):
        co, zh, x = t // 16, (t // 4) % 4, t % 4
        zl, y = zh // 2, (zh % 2) * 4 + x

        @pl.when(jnp.logical_not((co == p.co) & (zl == p.zl) & (y == p.y)))
        def _():
            sent(m["rs"].at[co, zh, x], m["rt_s"].at[co, zh, x], p.dev(co=co, zl=zl, y=y))

        return 0

    def close():
        for copy in copies:
            copy.wait_send()
        lax.fori_loop(0, 32, leave, 0)

    return close


def scratch2():
    dma = pltpu.SemaphoreType.DMA
    return {
        "nrm": pltpu.VMEM((1152, C), BF16),
        "nf": pltpu.VMEM((1152, C), F32),
        "ns": pltpu.VMEM((4, 4, 80, C), BF16),
        "x2": pltpu.VMEM((2, 2, 4, 4, 80, C), BF16),
        "xx": pltpu.VMEM((6, 16, 48, C), BF16),
        "spread": pltpu.VMEM((64, C), F32),
        "hs": pltpu.VMEM((4, 16, C), BF16),
        "by": pltpu.VMEM((2, 8, 16, C), BF16),
        "b2": pltpu.VMEM((4, 4, 2, 48, 384), BF16),
        "wk": pltpu.VMEM((C, C), BF16),
        "wt": pltpu.VMEM((C, C), BF16),
        "wide": pltpu.VMEM((512, 384), BF16),
        "qt": pltpu.VMEM((6, 2, C, 384), BF16),
        "k": pltpu.VMEM((6, 768, C), BF16),
        "vt": pltpu.VMEM((6, 48, 768), BF16),
        "gt": pltpu.VMEM((6, 2, 32, 384), BF16),
        "ot": pltpu.VMEM((C, 384), BF16),
        "tr": pltpu.VMEM((384, C), F32),
        "rs": pltpu.VMEM((2, 2, 8, 48, C), BF16),
        "rx": pltpu.VMEM((2, 4, 4, 2, 48, C), BF16),
        "by_s": dma((2, 8)),
        "by_r": dma((2, 8)),
        "xa_s": dma((4, 4)),
        "xa_r": dma((4, 4)),
        "xy_s": dma((4, 4)),
        "xy_r": dma((4, 4)),
        "xc_s": dma((2, 4)),
        "xc_r": dma((2, 4)),
        "bz_s": dma((4, 2)),
        "bz_r": dma((4, 2)),
        "bx_s": dma((4, 4, 2)),
        "bx_r": dma((4, 4, 2)),
        "rt_s": dma((2, 2, 8)),
        "rt_r": dma((4, 4, 2)),
        "rc_s": dma((4,)),
        "rc_r": dma((4,)),
    }


def pick_rows(head, at):
    row, col = iota((128, 128), 0), iota((128, 128), 1)
    hit = (row - at == col - 32 * head) & (row >= at) & (row < at + 32)
    return jnp.where(hit, 1.0, 0.0).astype(BF16)


def phase2(p, mask, proj, bias_w, out_w, dst, m):
    head = 2 * p.yl + p.co
    other = 1 - p.co
    copies = []

    local_bias(m["nrm"][...], bias_w[...], m["spread"], m["hs"])
    m["by"][p.co, p.y] = m["hs"][head]
    for e in FAR:
        for c in range(2):
            if (c, e) != (0, 0):
                co, y = (p.co + c) % 2, (p.y + e) % 8
                copies.append(
                    send(
                        m["hs"].at[2 * (y % 2) + co],
                        m["by"].at[p.co, p.y],
                        m["by_s"].at[c, e],
                        m["by_r"].at[p.co, p.y],
                        p.dev(co=co, y=y),
                    )
                )

    for a in (2, 1, 3, 0):
        for b in (2, 1, 3, 0):
            zh, x = (p.zh + a) % 4, (p.x + b) % 4
            first = 3 * (zh * 4 + x)
            rows = [m["nf"][pl.ds(first + i, 24, stride=48), :] for i in range(3)]
            rows.append(jnp.zeros((8, C), F32))
            m["ns"][zh, x] = jnp.concatenate(rows, axis=0).astype(BF16)
            if (a, b) == (0, 0):
                m["x2"][p.yl, p.co, p.zh, p.x] = m["ns"][zh, x]
            else:
                copies.append(
                    send(
                        m["ns"].at[zh, x],
                        m["x2"].at[p.yl, p.co, p.zh, p.x],
                        m["xa_s"].at[a, b],
                        m["xa_r"].at[p.zh, p.x],
                        p.dev(zh=zh, x=x),
                    )
                )

    m["wk"][...] = dot(proj[:, 128:256], pick(head, 0)).astype(BF16)
    wt = dot_nt(pick_rows(head, 0), proj[:, 0:128])
    wt = wt + dot_nt(pick_rows(head, 32), proj[:, 256:384])
    wt = wt + dot_nt(pick_rows(head, 64), proj[:, 384:512])
    m["wt"][...] = wt.astype(BF16)
    spread_out(out_w, m["wide"])

    row, col = iota((48, 768), 0), iota((48, 768), 1)
    keep = jnp.where(col == row + 48 * (4 * p.zh + p.x), mask[...].reshape(1, 768), 0)
    keep = jnp.sum(keep.astype(F32), axis=1, keepdims=True)
    for e in FAR:
        for c in range(2):
            if (c, e) != (0, 0):
                co, y = (p.co + c) % 2, (p.y + e) % 8
                got(m["by"].at[co, y], m["by_r"].at[co, y], p.dev(co=co, y=y))
    joined = join_columns([m["by"][:, y].reshape(32, C).astype(F32) for y in range(8)])
    whole = jnp.concatenate(
        [jnp.concatenate([joined[0][j], joined[1][j]], axis=0) for j in range(3)], axis=1
    )
    m["b2"][p.zh, p.x, p.zl] = jnp.where(keep > 0.5, whole, NEG).astype(BF16)

    def to_columns(zh, zl):
        block = m["b2"].at[zh, p.x, zl]
        for d in NEAR[1:]:
            copies.append(
                send(
                    block,
                    block,
                    m["bx_s"].at[d, zh, zl],
                    m["bx_r"].at[p.x, zh, zl],
                    p.dev(x=(p.x + d) % 4),
                )
            )

    mine = m["b2"].at[p.zh, p.x, p.zl]
    for z in range(2):
        for a in NEAR:
            if (a, z) != (0, 0):
                zh, zl = (p.zh + a) % 4, (p.zl + z) % 2
                copies.append(
                    send(
                        mine,
                        mine,
                        m["bz_s"].at[a, z],
                        m["bz_r"].at[p.zh, p.zl],
                        p.dev(zh=zh, zl=zl),
                    )
                )
    to_columns(p.zh, p.zl)

    for a in NEAR:
        for b in NEAR:
            zh, x = (p.zh + a) % 4, (p.x + b) % 4
            block = m["x2"].at[p.yl, p.co, zh, x]
            if (a, b) != (0, 0):
                got(block, m["xa_r"].at[zh, x], p.dev(zh=zh, x=x))
            copies.append(
                send(block, block, m["xy_s"].at[a, b], m["xy_r"].at[zh, x], p.dev(y=p.y1))
            )
        part = m["x2"].at[p.yl, p.co, zh]
        copies.append(
            send(part, part, m["xc_s"].at[0, a], m["xc_r"].at[p.yl, zh], p.dev(co=other))
        )

    for z in range(2):
        for a in NEAR:
            if (a, z) != (0, 0):
                zh, zl = (p.zh + a) % 4, (p.zl + z) % 2
                got(m["b2"].at[zh, p.x, zl], m["bz_r"].at[zh, zl], p.dev(zh=zh, zl=zl))
                to_columns(zh, zl)

    for a in NEAR:
        for b in NEAR:
            zh, x = (p.zh + a) % 4, (p.x + b) % 4
            got(m["x2"].at[1 - p.yl, p.co, zh, x], m["xy_r"].at[zh, x], p.dev(y=p.y1))
        part = m["x2"].at[1 - p.yl, p.co, zh]
        copies.append(
            send(part, part, m["xc_s"].at[1, a], m["xc_r"].at[1 - p.yl, zh], p.dev(co=other))
        )

    sub = iota((16, 768), 0)
    ones = jnp.where(sub == 0, 1.0, 0.0)

    def prepare(t, _):
        yl = (p.yl + t) % 2
        for zh in range(4):
            got(m["x2"].at[yl, other, zh], m["xc_r"].at[yl, zh], p.dev(co=other))

        def arrange(n, _):
            zh, x = n // 4, n % 4
            cores = [m["x2"][yl, c, zh, x].astype(F32) for c in range(2)]
            for b in range(3):
                rows = [core[24 * b : 24 * b + 24] for core in cores]
                m["xx"][3 * yl + b, n] = jnp.concatenate(rows, axis=0).astype(BF16)
            return 0

        lax.fori_loop(0, 16, arrange, 0)
        for b in range(3):
            item = 3 * yl + b
            rows = m["xx"][item].reshape(768, C)
            m["k"][item] = dot(rows, m["wk"][...]).astype(BF16)
            mixed = dot_nt(m["wt"][...], rows)
            query = (mixed * HD ** (-0.5)).astype(BF16)
            gate = jax.nn.sigmoid(mixed[64:96]).astype(BF16)
            for z in range(2):
                m["qt"][item, z] = query[:, 384 * z : 384 * z + 384]
                m["gt"][item, z] = gate[:, 384 * z : 384 * z + 384]
            m["vt"][item] = jnp.concatenate([mixed[32:64], ones], axis=0).astype(BF16)
        return 0

    lax.fori_loop(0, 2, prepare, 0)

    m["ot"][...] = jnp.zeros_like(m["ot"])
    eye = jnp.where(iota((128, 128), 0) == iota((128, 128), 1), 1.0, 0.0).astype(BF16)

    def attend(t, _):
        z, yl = (p.zl + t // 2) % 2, t % 2

        @pl.when(yl == 0)
        def _():
            for d in range(1, 4):
                x = (p.x + d) % 4
                for zh in range(4):
                    got(m["b2"].at[zh, x, z], m["bx_r"].at[x, zh, z], p.dev(x=x))

        bias = m["b2"][:, :, z].reshape(768, 384)
        for b in range(3):
            item = 3 * yl + b
            scores = dot(m["k"][item], m["qt"][item, z]) + bias.astype(F32)
            top = jnp.max(scores, axis=0, keepdims=True)
            weights = jnp.exp(scores - top).astype(BF16)
            out = dot(m["vt"][item], weights)
            gated = out[0:32] / out[32:33] * m["gt"][item, z].astype(F32)
            m["ot"][32 * b : 32 * b + 32, :] = gated.astype(BF16)
        for j in range(3):
            m["tr"][128 * j : 128 * j + 128, :] = dot_nt(eye, m["ot"][:, 128 * j : 128 * j + 128])
        y = p.y - p.yl + yl
        for n in range(8):
            zh, x = 2 * z + n // 4, n % 4
            m["rs"][z, yl, n] = m["tr"][48 * n : 48 * n + 48, :].astype(BF16)
            self = (zh == p.zh) & (p.x == x) & (yl == p.yl)

            @pl.when(self)
            def _():
                m["rx"][p.co, p.zh, p.x, p.yl] = m["rs"][z, yl, n]

            @pl.when(jnp.logical_not(self))
            def _():
                send(
                    m["rs"].at[z, yl, n],
                    m["rx"].at[p.co, p.zh, p.x, p.yl],
                    m["rt_s"].at[z, yl, n],
                    m["rt_r"].at[p.zh, p.x, p.yl],
                    p.dev(zh=zh, x=x, y=y),
                )

        return 0

    lax.fori_loop(0, 4, attend, 0)

    for d in NEAR:
        zh = (p.zh + d) % 4
        for x in range(4):
            for yl in range(2):

                @pl.when(jnp.logical_not((zh == p.zh) & (x == p.x) & (yl == p.yl)))
                def _():
                    got(
                        m["rx"].at[p.co, zh, x, yl],
                        m["rt_r"].at[zh, x, yl],
                        p.dev(zh=zh, x=x, y=p.y - p.yl + yl),
                    )

        part = m["rx"].at[p.co, zh]
        copies.append(send(part, part, m["rc_s"].at[d], m["rc_r"].at[zh], p.dev(co=other)))

    def finish(t, _):
        zh = (p.zh + t + jnp.where(t == 2, 1, 0) - jnp.where(t == 3, 1, 0)) % 4
        got(m["rx"].at[other, zh], m["rc_r"].at[zh], p.dev(co=other))
        rows = [m["rx"][h % 2, zh, :, h // 2].reshape(192, C) for h in range(HEADS)]
        update = dot(jnp.concatenate(rows, axis=1), m["wide"][...])
        for x in range(4):
            for b in range(3):
                chip = update[48 * x : 48 * x + 48, b * 128 : b * 128 + 128]
                at = pl.ds(3 * (4 * zh + x) + b, 24, stride=48)
                dst[at, :] = jnp.where(p.co == 0, chip[0:24], chip[24:48])
        return 0

    lax.fori_loop(0, 4, finish, 0)

    def leave(t, _):
        z, yl, n = t // 16, (t // 8) % 2, t % 8
        zh, x = 2 * z + n // 4, n % 4
        y = p.y - p.yl + yl

        @pl.when(jnp.logical_not((zh == p.zh) & (x == p.x) & (yl == p.yl)))
        def _():
            sent(m["rs"].at[z, yl, n], m["rt_s"].at[z, yl, n], p.dev(zh=zh, x=x, y=y))

        return 0

    def close():
        for copy in copies:
            copy.wait_send()
        lax.fori_loop(0, 32, leave, 0)

    return close


def kernel(
    names1, names2, pair, mask, proj1, bias1_w, out1_w, proj2, bias2_w, out2_w, dst, mid_out, mid, mid_sem, *refs
):
    m1 = dict(zip(names1, refs))
    m2 = dict(zip(names2, refs[len(names1) :]))
    p = Place()
    others = partners(p)
    barrier = pltpu.get_barrier_semaphore()
    for device in others:
        pl.semaphore_signal(barrier, inc=1, device_id=device, device_id_type=MESH)

    def ready():
        pl.semaphore_wait(barrier, len(others))

    nrm, nf = m2["nrm"], m2["nf"]
    close1 = phase1(p, ready, pair, mask, proj1, bias1_w, out1_w, mid, nrm, nf, m1)
    keep = pltpu.make_async_copy(mid, mid_out, mid_sem)
    keep.start()
    close2 = phase2(p, mask, proj2, bias2_w, out2_w, dst, m2)
    close1()
    close2()
    keep.wait()


def shards(pair, residue_mask, start_proj, start_bias_w, start_out, end_proj, end_bias_w, end_out):
    rows, cols = pair.shape[:2]
    one, two = scratch1(), scratch2()
    vmem = pl.BlockSpec(memory_space=pltpu.VMEM)
    update, mid = pl.pallas_call(
        functools.partial(kernel, tuple(one), tuple(two)),
        out_shape=[jax.ShapeDtypeStruct((rows * cols, C), F32)] * 2,
        in_specs=[vmem] * 8,
        out_specs=[vmem, pl.BlockSpec(memory_space=pl.ANY)],
        scratch_shapes=[pltpu.VMEM((rows * cols, C), F32), pltpu.SemaphoreType.DMA] + list(one.values()) + list(two.values()),
        compiler_params=pltpu.CompilerParams(
            collective_id=0, has_side_effects=True, vmem_limit_bytes=56 << 20
        ),
        name="triangle_attention",
    )(
        pair.reshape(rows * cols, C),
        residue_mask,
        start_proj,
        start_bias_w.T,
        start_out,
        end_proj,
        end_bias_w.T,
        end_out,
    )
    return (mid + update).reshape(rows, cols, C)


def solution(mesh):
    placed = (P("row", "col", None), P(), P(), P(), P(), P(), P(), P())
    return jax.shard_map(
        shards, mesh=mesh, in_specs=placed, out_specs=P("row", "col", None), check_vma=False
    )
```

```python
import functools

import jax
import jax.numpy as jnp
from jax import lax
from jax.experimental import pallas as pl
from jax.experimental.pallas import tpu as pltpu
from jax.sharding import PartitionSpec as P

C = 128
HEADS = 4
HD = 32
MESH = pl.DeviceIdType.MESH
F32 = jnp.float32
BF16 = jnp.bfloat16
NT = (((1,), (1,)), ((), ()))
NEG = -1000000000.0


def iota(shape, dim):
    return lax.broadcasted_iota(jnp.int32, shape, dim)


def dot(a, b):
    return jnp.dot(a, b, preferred_element_type=F32)


def dot_nt(a, b):
    return lax.dot_general(a, b, NT, preferred_element_type=F32)


class Place:
    def __init__(self):
        r, c = lax.axis_index("row"), lax.axis_index("col")
        self.zh, self.x, self.co = r // 8, (r // 2) % 4, r % 2
        self.zl, self.y = c // 8, c % 8
        self.yl = self.y % 2
        self.y1 = self.y + 1 - 2 * self.yl

    def dev(self, zh=None, x=None, co=None, zl=None, y=None):
        zh = self.zh if zh is None else zh
        x = self.x if x is None else x
        co = self.co if co is None else co
        zl = self.zl if zl is None else zl
        y = self.y if y is None else y
        return (zh * 8 + x * 2 + co, zl * 8 + y)


def send(src, dst, ssem, rsem, device):
    copy = pltpu.make_async_remote_copy(
        src_ref=src, dst_ref=dst, send_sem=ssem, recv_sem=rsem, device_id=device, device_id_type=MESH
    )
    copy.start()
    return copy


def got(dst, sem, device):
    pltpu.make_async_remote_copy(
        src_ref=dst, dst_ref=dst, send_sem=sem, recv_sem=sem, device_id=device, device_id_type=MESH
    ).wait_recv()


def sent(src, sem, device):
    pltpu.make_async_remote_copy(
        src_ref=src, dst_ref=src, send_sem=sem, recv_sem=sem, device_id=device, device_id_type=MESH
    ).wait_send()


def layer_norm(field):
    mean = jnp.mean(field, axis=-1, keepdims=True)
    centered = field - mean
    var = jnp.mean(centered * centered, axis=-1, keepdims=True)
    return centered * lax.rsqrt(var + 1e-05)


def local_bias(normed, bias_w, spread, heads):
    flat = dot_nt(bias_w, normed)
    spread[...] = jnp.zeros_like(spread)
    for r in range(24):
        row, lane = (r, 0) if r < 8 else (r - 8, 0 if r >= 16 else 64)
        spread[4 * row : 4 * row + 4, lane : lane + 48] = flat[:, 48 * r : 48 * r + 48]
    for h in range(HEADS):
        heads[h] = spread[pl.ds(h, 16, stride=4), :].astype(BF16)


def join_columns(blocks):
    lane = iota(blocks[0].shape, 1)
    parts = []
    for first in (0, 64):
        tiles = [jnp.zeros(blocks[0].shape, F32) for _ in range(3)]
        for b, block in enumerate(blocks):
            tile, at = (48 * b) // 128, (48 * b) % 128
            piece = jnp.where((lane >= first) & (lane < first + 48), block, 0.0)
            if (at - first) % 128:
                piece = pltpu.roll(piece, (at - first) % 128, 1)
            if at + 48 <= 128:
                tiles[tile] = tiles[tile] + piece
            else:
                tiles[tile] = tiles[tile] + jnp.where(lane >= at, piece, 0.0)
                tiles[tile + 1] = tiles[tile + 1] + jnp.where(lane < at, piece, 0.0)
        parts.append(tiles)
    joined = []
    for base in range(0, blocks[0].shape[0], 16):
        near, far = slice(base, base + 8), slice(base + 8, base + 16)
        joined.append(
            [
                jnp.concatenate([a[near], b[near], a[far]], axis=0)
                for a, b in zip(parts[0], parts[1])
            ]
        )
    return joined


def pick(head, at):
    row, col = iota((128, 128), 0), iota((128, 128), 1)
    hit = (row - 32 * head == col - at) & (col >= at) & (col < at + 32)
    return jnp.where(hit, 1.0, 0.0).astype(BF16)


def spread_out(out_w, wide):
    wide[...] = jnp.zeros_like(wide)
    for h in range(HEADS):
        for a in range(3):
            wide[h * 128 + 32 * a : h * 128 + 32 * a + 32, a * 128 : a * 128 + 128] = out_w[
                32 * h : 32 * h + 32, :
            ]


NEAR = (0, 1, 3, 2)
FAR = (4, 3, 5, 2, 6, 1, 7, 0)
CLOSE = FAR[::-1]


def scratch1():
    dma = pltpu.SemaphoreType.DMA
    return {
        "nrm": pltpu.VMEM((8, 144, C), BF16),
        "x1f": pltpu.VMEM((2, 2, 8, 144, C), BF16),
        "spread": pltpu.VMEM((64, C), F32),
        "hs": pltpu.VMEM((4, 16, C), BF16),
        "by": pltpu.VMEM((2, 2, 8, 16, C), BF16),
        "bf": pltpu.VMEM((4, 4, 48, 768), BF16),
        "wall": pltpu.VMEM((3, C, 512), BF16),
        "wide": pltpu.VMEM((512, 384), BF16),
        "q": pltpu.VMEM((6, 4, 4, 48, C), BF16),
        "k": pltpu.VMEM((6, 768, C), BF16),
        "v": pltpu.VMEM((6, 768, C), BF16),
        "g": pltpu.VMEM((2, 4, 4, 48, C), BF16),
        "rs": pltpu.VMEM((2, 4, 4, 48, C), BF16),
        "rx": pltpu.VMEM((8, 4, 48, C), BF16),
        "by_s": dma((2, 2, 8)),
        "by_r": dma((2, 2, 8)),
        "xy_s": dma((8,)),
        "xy_r": dma((8,)),
        "xz_s": dma((8,)),
        "xz_r": dma((8,)),
        "xc_s": dma((2, 8)),
        "xc_r": dma((2, 8)),
        "bz_s": dma((4,)),
        "bz_r": dma((4,)),
        "bx_s": dma((4, 4)),
        "bx_r": dma((4, 4)),
        "rt_s": dma((2, 4, 4)),
        "rt_r": dma((8, 4)),
    }


def partners(p):
    out = []
    for e in FAR:
        for c in range(2):
            for z in range(2):
                if (c, z, e) != (0, 0, 0):
                    out.append(p.dev(co=(p.co + c) % 2, zl=(p.zl + z) % 2, y=(p.y + e) % 8))
    for d in range(1, 4):
        out.append(p.dev(zh=(p.zh + d) % 4))
        out.append(p.dev(x=(p.x + d) % 4))
    return out


def phase1(p, fetches, ready, src, mask, proj, bias_w, out_w, dst, nrm, nf, m):
    head = 2 * p.zl + p.co
    copies = []

    for b, fetch in enumerate(fetches):
        fetch.wait()
        normed = layer_norm(src[288 * b : 288 * b + 288, :]).astype(BF16)
        m["nrm"][2 * b : 2 * b + 2] = normed.reshape(2, 144, C)
    local_bias(m["nrm"][...].reshape(1152, C), bias_w[...], m["spread"], m["hs"])
    ready()
    m["by"][p.co, p.zl, p.y] = m["hs"][head]
    for e in FAR:
        for c in range(2):
            for z in range(2):
                if (c, z, e) != (0, 0, 0):
                    co, zl, y = (p.co + c) % 2, (p.zl + z) % 2, (p.y + e) % 8
                    copies.append(
                        send(
                            m["hs"].at[2 * zl + co],
                            m["by"].at[p.co, p.zl, p.y],
                            m["by_s"].at[c, z, e],
                            m["by_r"].at[p.co, p.zl, p.y],
                            p.dev(co=co, zl=zl, y=y),
                        )
                    )
    for d in FAR[:7]:
        to = (p.y + d) % 8
        copies.append(
            send(
                m["nrm"].at[to],
                m["x1f"].at[p.co, p.zl, p.y],
                m["xy_s"].at[d],
                m["xy_r"].at[p.y],
                p.dev(y=to),
            )
        )
    m["x1f"][p.co, p.zl, p.y] = m["nrm"][p.y]

    for a in range(3):
        first, here = pick(head, 0), pick(head, 32 * a)
        m["wall"][a, :, 0:128] = dot(proj[:, 0:128], first).astype(BF16)
        m["wall"][a, :, 128:256] = dot(proj[:, 128:256], first).astype(BF16)
        m["wall"][a, :, 256:384] = dot(proj[:, 256:384], here).astype(BF16)
        m["wall"][a, :, 384:512] = dot(proj[:, 384:512], here).astype(BF16)
    spread_out(out_w, m["wide"])

    for e in FAR:
        for c in range(2):
            for z in range(2):
                if (c, z, e) != (0, 0, 0):
                    co, zl, y = (p.co + c) % 2, (p.zl + z) % 2, (p.y + e) % 8
                    got(m["by"].at[co, zl, y], m["by_r"].at[co, zl, y], p.dev(co=co, zl=zl, y=y))
    joined = join_columns([m["by"][:, :, y].reshape(64, C).astype(F32) for y in range(8)])
    whole = jnp.concatenate(
        [
            jnp.concatenate([joined[z][j], joined[2 + z][j]], axis=0)
            for z in range(2)
            for j in range(3)
        ],
        axis=1,
    )
    m["bf"][p.x, p.zh] = jnp.where(mask[...].reshape(1, 768) > 0, whole, NEG).astype(BF16)

    def to_columns(zh):
        block = m["bf"].at[p.x, zh]
        for d in NEAR[1:]:
            copies.append(
                send(
                    block,
                    block,
                    m["bx_s"].at[d, zh],
                    m["bx_r"].at[p.x, zh],
                    p.dev(x=(p.x + d) % 4),
                )
            )

    mine = m["bf"].at[p.x, p.zh]
    for d in NEAR[1:]:
        copies.append(
            send(mine, mine, m["bz_s"].at[d], m["bz_r"].at[p.zh], p.dev(zh=(p.zh + d) % 4))
        )
    to_columns(p.zh)
    for d in CLOSE:
        fr = (p.y + d) % 8
        block = m["x1f"].at[p.co, p.zl, fr]
        if d:
            got(block, m["xy_r"].at[fr], p.dev(y=fr))
        copies.append(
            send(block, block, m["xz_s"].at[d], m["xz_r"].at[fr], p.dev(zl=(p.zl + 1) % 2))
        )
        copies.append(
            send(block, block, m["xc_s"].at[0, d], m["xc_r"].at[p.zl, fr], p.dev(co=1 - p.co))
        )

    for d in NEAR[1:]:
        zh = (p.zh + d) % 4
        got(m["bf"].at[p.x, zh], m["bz_r"].at[zh], p.dev(zh=zh))
        to_columns(zh)
    other = (p.zl + 1) % 2
    for d in CLOSE:
        fr = (p.y + d) % 8
        block = m["x1f"].at[p.co, other, fr]
        got(block, m["xz_r"].at[fr], p.dev(zl=other))
        copies.append(
            send(block, block, m["xc_s"].at[1, d], m["xc_r"].at[other, fr], p.dev(co=1 - p.co))
        )

    lane = iota((768, C), 1)

    def prepare(t, _):
        co = (p.co + t) % 2

        @pl.when(t == 1)
        def _():
            for zl in range(2):
                for y in range(8):
                    got(m["x1f"].at[co, zl, y], m["xc_r"].at[zl, y], p.dev(co=co))

        gate = jnp.zeros((768, C), F32)
        for a in range(3):
            rows = m["x1f"][co, :, :, a * 48 : a * 48 + 48, :].reshape(768, C)
            mixed = dot(rows, m["wall"][a])
            item = 3 * co + a
            query = (mixed[:, 0:128] * HD ** (-0.5)).astype(BF16)
            m["q"][item] = query.reshape(4, 4, 48, C)
            m["k"][item] = mixed[:, 128:256].astype(BF16)
            value = jnp.where(lane == 96 + a, 1.0, mixed[:, 256:384])
            m["v"][item] = value.astype(BF16)
            gate = gate + mixed[:, 384:512]
        gate = jnp.where(lane < 96, jax.nn.sigmoid(gate), 0.0)
        m["g"][co] = gate.astype(BF16).reshape(4, 4, 48, C)
        return 0

    lax.fori_loop(0, 2, prepare, 0)

    lane = iota((192, C), 1)

    def attend(t, _):
        s, co = t // 2, t % 2
        x = (p.x + s + jnp.where(s == 2, 1, 0) - jnp.where(s == 3, 1, 0)) % 4

        @pl.when((s > 0) & (co == 0))
        def _():
            for zh in range(4):
                got(m["bf"].at[x, zh], m["bx_r"].at[x, zh], p.dev(x=x))

        bias = m["bf"][x].reshape(192, 768)
        out = jnp.zeros((192, C), F32)
        for a in range(3):
            item = 3 * co + a
            query = m["q"][item, :, x].reshape(192, C)
            scores = dot_nt(query, m["k"][item]) + bias.astype(F32)
            top = jnp.max(scores, axis=-1, keepdims=True)
            weights = jnp.exp(scores - top).astype(BF16)
            out = out + dot(weights, m["v"][item])
        inv = [1.0 / out[:, 96 + a : 97 + a] for a in range(3)]
        scale = jnp.where(lane < 32, inv[0], jnp.where(lane < 64, inv[1], inv[2]))
        gated = out * scale * m["g"][co, :, x].reshape(192, C).astype(F32)
        m["rs"][co, :, x] = gated.astype(BF16).reshape(4, 48, C)
        for zh in range(4):
            zl, y = zh // 2, (zh % 2) * 4 + x
            self = (co == p.co) & (zl == p.zl) & (y == p.y)

            @pl.when(self)
            def _():
                m["rx"][p.y, head] = m["rs"][co, zh, x]

            @pl.when(jnp.logical_not(self))
            def _():
                send(
                    m["rs"].at[co, zh, x],
                    m["rx"].at[p.y, head],
                    m["rt_s"].at[co, zh, x],
                    m["rt_r"].at[p.y, head],
                    p.dev(co=co, zl=zl, y=y),
                )

        return 0

    lax.fori_loop(0, 8, attend, 0)

    def finish(t, _):
        places = [(p.y + 8 - t) % 8, (p.y + t + 1) % 8]
        for y in places:
            for h in range(HEADS):

                @pl.when(jnp.logical_not((y == p.y) & (h == head)))
                def _():
                    got(m["rx"].at[y, h], m["rt_r"].at[y, h], p.dev(co=h % 2, zl=h // 2, y=y))

        for y in places:
            rows = jnp.concatenate([m["rx"][y, h] for h in range(HEADS)], axis=1)
            update = dot(rows, m["wide"][...])
            for a in range(3):
                at = pl.multiple_of((3 * y + a) * 48, 16)
                mid = src[pl.ds(at, 48), :] + update[:, a * 128 : a * 128 + 128]
                dst[pl.ds(at, 48), :] = mid
                normed = layer_norm(mid).astype(BF16)
                nrm[pl.ds(at, 48), :] = normed
                nf[pl.ds(at, 48), :] = normed.astype(F32)
        return 0

    lax.fori_loop(0, 4, finish, 0)

    def leave(t, _):
        co, zh, x = t // 16, (t // 4) % 4, t % 4
        zl, y = zh // 2, (zh % 2) * 4 + x

        @pl.when(jnp.logical_not((co == p.co) & (zl == p.zl) & (y == p.y)))
        def _():
            sent(m["rs"].at[co, zh, x], m["rt_s"].at[co, zh, x], p.dev(co=co, zl=zl, y=y))

        return 0

    def close():
        for copy in copies:
            copy.wait_send()
        lax.fori_loop(0, 32, leave, 0)

    return close


def scratch2():
    dma = pltpu.SemaphoreType.DMA
    return {
        "nrm": pltpu.VMEM((1152, C), BF16),
        "nf": pltpu.VMEM((1152, C), F32),
        "ns": pltpu.VMEM((4, 4, 80, C), BF16),
        "x2": pltpu.VMEM((2, 2, 4, 4, 80, C), BF16),
        "xx": pltpu.VMEM((6, 16, 48, C), BF16),
        "spread": pltpu.VMEM((64, C), F32),
        "hs": pltpu.VMEM((4, 16, C), BF16),
        "by": pltpu.VMEM((2, 8, 16, C), BF16),
        "b2": pltpu.VMEM((4, 4, 2, 48, 384), BF16),
        "wk": pltpu.VMEM((C, C), BF16),
        "wt": pltpu.VMEM((C, C), BF16),
        "wide": pltpu.VMEM((512, 384), BF16),
        "qt": pltpu.VMEM((6, 2, C, 384), BF16),
        "k": pltpu.VMEM((6, 768, C), BF16),
        "vt": pltpu.VMEM((6, 48, 768), BF16),
        "gt": pltpu.VMEM((6, 2, 32, 384), BF16),
        "ot": pltpu.VMEM((C, 384), BF16),
        "tr": pltpu.VMEM((384, C), F32),
        "rs": pltpu.VMEM((2, 2, 8, 48, C), BF16),
        "rx": pltpu.VMEM((2, 4, 4, 2, 48, C), BF16),
        "by_s": dma((2, 8)),
        "by_r": dma((2, 8)),
        "xa_s": dma((4, 4)),
        "xa_r": dma((4, 4)),
        "xy_s": dma((4, 4)),
        "xy_r": dma((4, 4)),
        "xc_s": dma((2, 4)),
        "xc_r": dma((2, 4)),
        "bz_s": dma((4, 2)),
        "bz_r": dma((4, 2)),
        "bx_s": dma((4, 4, 2)),
        "bx_r": dma((4, 4, 2)),
        "rt_s": dma((2, 2, 8)),
        "rt_r": dma((4, 4, 2)),
        "rc_s": dma((4, 4)),
        "rc_r": dma((4, 4)),
    }


def pick_rows(head, at):
    row, col = iota((128, 128), 0), iota((128, 128), 1)
    hit = (row - at == col - 32 * head) & (row >= at) & (row < at + 32)
    return jnp.where(hit, 1.0, 0.0).astype(BF16)


def phase2(p, mid, mask, proj, bias_w, out_w, dst, m):
    head = 2 * p.yl + p.co
    other = 1 - p.co
    copies = []

    local_bias(m["nrm"][...], bias_w[...], m["spread"], m["hs"])
    m["by"][p.co, p.y] = m["hs"][head]
    for e in FAR:
        for c in range(2):
            if (c, e) != (0, 0):
                co, y = (p.co + c) % 2, (p.y + e) % 8
                copies.append(
                    send(
                        m["hs"].at[2 * (y % 2) + co],
                        m["by"].at[p.co, p.y],
                        m["by_s"].at[c, e],
                        m["by_r"].at[p.co, p.y],
                        p.dev(co=co, y=y),
                    )
                )

    for a in (2, 1, 3, 0):
        for b in (2, 1, 3, 0):
            zh, x = (p.zh + a) % 4, (p.x + b) % 4
            first = 3 * (zh * 4 + x)
            rows = [m["nf"][pl.ds(first + i, 24, stride=48), :] for i in range(3)]
            rows.append(jnp.zeros((8, C), F32))
            m["ns"][zh, x] = jnp.concatenate(rows, axis=0).astype(BF16)
            if (a, b) == (0, 0):
                m["x2"][p.yl, p.co, p.zh, p.x] = m["ns"][zh, x]
            else:
                copies.append(
                    send(
                        m["ns"].at[zh, x],
                        m["x2"].at[p.yl, p.co, p.zh, p.x],
                        m["xa_s"].at[a, b],
                        m["xa_r"].at[p.zh, p.x],
                        p.dev(zh=zh, x=x),
                    )
                )

    m["wk"][...] = dot(proj[:, 128:256], pick(head, 0)).astype(BF16)
    wt = dot_nt(pick_rows(head, 0), proj[:, 0:128])
    wt = wt + dot_nt(pick_rows(head, 32), proj[:, 256:384])
    wt = wt + dot_nt(pick_rows(head, 64), proj[:, 384:512])
    m["wt"][...] = wt.astype(BF16)
    spread_out(out_w, m["wide"])

    row, col = iota((48, 768), 0), iota((48, 768), 1)
    keep = jnp.where(col == row + 48 * (4 * p.zh + p.x), mask[...].reshape(1, 768), 0)
    keep = jnp.sum(keep.astype(F32), axis=1, keepdims=True)
    for e in FAR:
        for c in range(2):
            if (c, e) != (0, 0):
                co, y = (p.co + c) % 2, (p.y + e) % 8
                got(m["by"].at[co, y], m["by_r"].at[co, y], p.dev(co=co, y=y))
    joined = join_columns([m["by"][:, y].reshape(32, C).astype(F32) for y in range(8)])
    whole = jnp.concatenate(
        [jnp.concatenate([joined[0][j], joined[1][j]], axis=0) for j in range(3)], axis=1
    )
    m["b2"][p.zh, p.x, p.zl] = jnp.where(keep > 0.5, whole, NEG).astype(BF16)

    def to_columns(zh, zl):
        block = m["b2"].at[zh, p.x, zl]
        for d in NEAR[1:]:
            copies.append(
                send(
                    block,
                    block,
                    m["bx_s"].at[d, zh, zl],
                    m["bx_r"].at[p.x, zh, zl],
                    p.dev(x=(p.x + d) % 4),
                )
            )

    mine = m["b2"].at[p.zh, p.x, p.zl]
    for z in range(2):
        for a in NEAR:
            if (a, z) != (0, 0):
                zh, zl = (p.zh + a) % 4, (p.zl + z) % 2
                copies.append(
                    send(
                        mine,
                        mine,
                        m["bz_s"].at[a, z],
                        m["bz_r"].at[p.zh, p.zl],
                        p.dev(zh=zh, zl=zl),
                    )
                )
    to_columns(p.zh, p.zl)

    for a in NEAR:
        for b in NEAR:
            zh, x = (p.zh + a) % 4, (p.x + b) % 4
            block = m["x2"].at[p.yl, p.co, zh, x]
            if (a, b) != (0, 0):
                got(block, m["xa_r"].at[zh, x], p.dev(zh=zh, x=x))
            copies.append(
                send(block, block, m["xy_s"].at[a, b], m["xy_r"].at[zh, x], p.dev(y=p.y1))
            )
        part = m["x2"].at[p.yl, p.co, zh]
        copies.append(
            send(part, part, m["xc_s"].at[0, a], m["xc_r"].at[p.yl, zh], p.dev(co=other))
        )

    for z in range(2):
        for a in NEAR:
            if (a, z) != (0, 0):
                zh, zl = (p.zh + a) % 4, (p.zl + z) % 2
                got(m["b2"].at[zh, p.x, zl], m["bz_r"].at[zh, zl], p.dev(zh=zh, zl=zl))
                to_columns(zh, zl)

    for a in NEAR:
        for b in NEAR:
            zh, x = (p.zh + a) % 4, (p.x + b) % 4
            got(m["x2"].at[1 - p.yl, p.co, zh, x], m["xy_r"].at[zh, x], p.dev(y=p.y1))
        part = m["x2"].at[1 - p.yl, p.co, zh]
        copies.append(
            send(part, part, m["xc_s"].at[1, a], m["xc_r"].at[1 - p.yl, zh], p.dev(co=other))
        )

    sub = iota((16, 768), 0)
    ones = jnp.where(sub == 0, 1.0, 0.0)

    def prepare(t, _):
        yl = (p.yl + t) % 2
        for zh in range(4):
            got(m["x2"].at[yl, other, zh], m["xc_r"].at[yl, zh], p.dev(co=other))

        def arrange(n, _):
            zh, x = n // 4, n % 4
            cores = [m["x2"][yl, c, zh, x].astype(F32) for c in range(2)]
            for b in range(3):
                rows = [core[24 * b : 24 * b + 24] for core in cores]
                m["xx"][3 * yl + b, n] = jnp.concatenate(rows, axis=0).astype(BF16)
            return 0

        lax.fori_loop(0, 16, arrange, 0)
        for b in range(3):
            item = 3 * yl + b
            rows = m["xx"][item].reshape(768, C)
            m["k"][item] = dot(rows, m["wk"][...]).astype(BF16)
            mixed = dot_nt(m["wt"][...], rows)
            query = (mixed * HD ** (-0.5)).astype(BF16)
            gate = jax.nn.sigmoid(mixed[64:96]).astype(BF16)
            for z in range(2):
                m["qt"][item, z] = query[:, 384 * z : 384 * z + 384]
                m["gt"][item, z] = gate[:, 384 * z : 384 * z + 384]
            m["vt"][item] = jnp.concatenate([mixed[32:64], ones], axis=0).astype(BF16)
        return 0

    lax.fori_loop(0, 2, prepare, 0)

    m["ot"][...] = jnp.zeros_like(m["ot"])
    eye = jnp.where(iota((128, 128), 0) == iota((128, 128), 1), 1.0, 0.0).astype(BF16)

    def attend(t, _):
        z, yl = (p.zl + t // 2) % 2, t % 2

        @pl.when(yl == 0)
        def _():
            for d in range(1, 4):
                x = (p.x + d) % 4
                for zh in range(4):
                    got(m["b2"].at[zh, x, z], m["bx_r"].at[x, zh, z], p.dev(x=x))

        bias = m["b2"][:, :, z].reshape(768, 384)
        for b in range(3):
            item = 3 * yl + b
            scores = dot(m["k"][item], m["qt"][item, z]) + bias.astype(F32)
            top = jnp.max(scores, axis=0, keepdims=True)
            weights = jnp.exp(scores - top).astype(BF16)
            out = dot(m["vt"][item], weights)
            gated = out[0:32] / out[32:33] * m["gt"][item, z].astype(F32)
            m["ot"][32 * b : 32 * b + 32, :] = gated.astype(BF16)
        for j in range(3):
            m["tr"][128 * j : 128 * j + 128, :] = dot_nt(eye, m["ot"][:, 128 * j : 128 * j + 128])
        y = p.y - p.yl + yl
        for n in range(8):
            zh, x = 2 * z + n // 4, n % 4
            m["rs"][z, yl, n] = m["tr"][48 * n : 48 * n + 48, :].astype(BF16)
            self = (zh == p.zh) & (p.x == x) & (yl == p.yl)

            @pl.when(self)
            def _():
                m["rx"][p.co, p.zh, p.x, p.yl] = m["rs"][z, yl, n]

            @pl.when(jnp.logical_not(self))
            def _():
                send(
                    m["rs"].at[z, yl, n],
                    m["rx"].at[p.co, p.zh, p.x, p.yl],
                    m["rt_s"].at[z, yl, n],
                    m["rt_r"].at[p.zh, p.x, p.yl],
                    p.dev(zh=zh, x=x, y=y),
                )

        return 0

    lax.fori_loop(0, 4, attend, 0)

    for d in NEAR:
        zh = (p.zh + d) % 4
        for x in range(4):
            for yl in range(2):

                @pl.when(jnp.logical_not((zh == p.zh) & (x == p.x) & (yl == p.yl)))
                def _():
                    got(
                        m["rx"].at[p.co, zh, x, yl],
                        m["rt_r"].at[zh, x, yl],
                        p.dev(zh=zh, x=x, y=p.y - p.yl + yl),
                    )

            part = m["rx"].at[p.co, zh, x]
            copies.append(
                send(part, part, m["rc_s"].at[d, x], m["rc_r"].at[zh, x], p.dev(co=other))
            )

    def finish(t, _):
        zh = (p.zh + t + jnp.where(t == 2, 1, 0) - jnp.where(t == 3, 1, 0)) % 4
        for x in range(4):
            got(m["rx"].at[other, zh, x], m["rc_r"].at[zh, x], p.dev(co=other))
        rows = [m["rx"][h % 2, zh, :, h // 2].reshape(192, C) for h in range(HEADS)]
        update = dot(jnp.concatenate(rows, axis=1), m["wide"][...])
        for x in range(4):
            for b in range(3):
                chip = update[48 * x : 48 * x + 48, b * 128 : b * 128 + 128]
                at = pl.ds(3 * (4 * zh + x) + b, 24, stride=48)
                dst[at, :] = mid[at, :] + jnp.where(p.co == 0, chip[0:24], chip[24:48])
        return 0

    lax.fori_loop(0, 4, finish, 0)

    def leave(t, _):
        z, yl, n = t // 16, (t // 8) % 2, t % 8
        zh, x = 2 * z + n // 4, n % 4
        y = p.y - p.yl + yl

        @pl.when(jnp.logical_not((zh == p.zh) & (x == p.x) & (yl == p.yl)))
        def _():
            sent(m["rs"].at[z, yl, n], m["rt_s"].at[z, yl, n], p.dev(zh=zh, x=x, y=y))

        return 0

    def close():
        for copy in copies:
            copy.wait_send()
        lax.fori_loop(0, 32, leave, 0)

    return close


def kernel(
    names1, names2, pair, mask, proj1, bias1_w, out1_w, proj2, bias2_w, out2_w, dst, mid, src, sems, *refs
):
    m1 = dict(zip(names1, refs))
    m2 = dict(zip(names2, refs[len(names1) :]))
    p = Place()
    fetches = []
    for b in range(4):
        piece = pl.ds(288 * b, 288)
        fetches.append(pltpu.make_async_copy(pair.at[piece], src.at[piece], sems.at[b]))
        fetches[-1].start()
    others = partners(p)
    barrier = pltpu.get_barrier_semaphore()
    for device in others:
        pl.semaphore_signal(barrier, inc=1, device_id=device, device_id_type=MESH)

    def ready():
        pl.semaphore_wait(barrier, len(others))

    nrm, nf = m2["nrm"], m2["nf"]
    close1 = phase1(p, fetches, ready, src, mask, proj1, bias1_w, out1_w, mid, nrm, nf, m1)
    close2 = phase2(p, mid, mask, proj2, bias2_w, out2_w, dst, m2)
    close1()
    close2()


def shards(pair, residue_mask, start_proj, start_bias_w, start_out, end_proj, end_bias_w, end_out):
    rows, cols = pair.shape[:2]
    one, two = scratch1(), scratch2()
    vmem = pl.BlockSpec(memory_space=pltpu.VMEM)
    out = pl.pallas_call(
        functools.partial(kernel, tuple(one), tuple(two)),
        out_shape=jax.ShapeDtypeStruct((rows * cols, C), F32),
        in_specs=[pl.BlockSpec(memory_space=pl.ANY)] + [vmem] * 7,
        out_specs=vmem,
        scratch_shapes=[
            pltpu.VMEM((rows * cols, C), F32),
            pltpu.VMEM((rows * cols, C), F32),
            pltpu.SemaphoreType.DMA((4,)),
        ]
        + list(one.values()) + list(two.values()),
        compiler_params=pltpu.CompilerParams(
            collective_id=0, has_side_effects=True, vmem_limit_bytes=56 << 20
        ),
        name="triangle_attention",
    )(
        pair.reshape(rows * cols, C),
        residue_mask,
        start_proj,
        start_bias_w.T,
        start_out,
        end_proj,
        end_bias_w.T,
        end_out,
    )
    return out.reshape(rows, cols, C)


def solution(mesh):
    placed = (P("row", "col", None), P(), P(), P(), P(), P(), P(), P())
    return jax.shard_map(
        shards, mesh=mesh, in_specs=placed, out_specs=P("row", "col", None), check_vma=False
    )
```

```python
import functools

import jax
import jax.numpy as jnp
from jax import lax
from jax.experimental import pallas as pl
from jax.experimental.pallas import tpu as pltpu
from jax.sharding import PartitionSpec as P

C = 128
HEADS = 4
HD = 32
MESH = pl.DeviceIdType.MESH
F32 = jnp.float32
BF16 = jnp.bfloat16
NT = (((1,), (1,)), ((), ()))
NEG = -1000000000.0


def iota(shape, dim):
    return lax.broadcasted_iota(jnp.int32, shape, dim)


def dot(a, b):
    return jnp.dot(a, b, preferred_element_type=F32)


def dot_nt(a, b):
    return lax.dot_general(a, b, NT, preferred_element_type=F32)


class Place:
    def __init__(self):
        r, c = lax.axis_index("row"), lax.axis_index("col")
        self.zh, self.x, self.co = r // 8, (r // 2) % 4, r % 2
        self.zl, self.y = c // 8, c % 8
        self.yl = self.y % 2
        self.y1 = self.y + 1 - 2 * self.yl

    def dev(self, zh=None, x=None, co=None, zl=None, y=None):
        zh = self.zh if zh is None else zh
        x = self.x if x is None else x
        co = self.co if co is None else co
        zl = self.zl if zl is None else zl
        y = self.y if y is None else y
        return (zh * 8 + x * 2 + co, zl * 8 + y)


def send(src, dst, ssem, rsem, device):
    copy = pltpu.make_async_remote_copy(
        src_ref=src, dst_ref=dst, send_sem=ssem, recv_sem=rsem, device_id=device, device_id_type=MESH
    )
    copy.start()
    return copy


def got(dst, sem, device):
    pltpu.make_async_remote_copy(
        src_ref=dst, dst_ref=dst, send_sem=sem, recv_sem=sem, device_id=device, device_id_type=MESH
    ).wait_recv()


def sent(src, sem, device):
    pltpu.make_async_remote_copy(
        src_ref=src, dst_ref=src, send_sem=sem, recv_sem=sem, device_id=device, device_id_type=MESH
    ).wait_send()


def wait_all(copies):
    for copy in copies:
        copy.wait()


def layer_norm(field):
    mean = jnp.mean(field, axis=-1, keepdims=True)
    centered = field - mean
    var = jnp.mean(centered * centered, axis=-1, keepdims=True)
    return centered * lax.rsqrt(var + 1e-05)


def local_bias(normed, bias_w, spread, heads):
    flat = dot_nt(bias_w, normed)
    spread[...] = jnp.zeros_like(spread)
    for r in range(24):
        row, lane = (r, 0) if r < 8 else (r - 8, 0 if r >= 16 else 64)
        spread[4 * row : 4 * row + 4, lane : lane + 48] = flat[:, 48 * r : 48 * r + 48]
    for h in range(HEADS):
        heads[h] = spread[pl.ds(h, 16, stride=4), :].astype(BF16)


def join_columns(blocks):
    lane = iota(blocks[0].shape, 1)
    parts = []
    for first in (0, 64):
        tiles = [jnp.zeros(blocks[0].shape, F32) for _ in range(3)]
        for b, block in enumerate(blocks):
            tile, at = (48 * b) // 128, (48 * b) % 128
            piece = jnp.where((lane >= first) & (lane < first + 48), block, 0.0)
            if (at - first) % 128:
                piece = pltpu.roll(piece, (at - first) % 128, 1)
            if at + 48 <= 128:
                tiles[tile] = tiles[tile] + piece
            else:
                tiles[tile] = tiles[tile] + jnp.where(lane >= at, piece, 0.0)
                tiles[tile + 1] = tiles[tile + 1] + jnp.where(lane < at, piece, 0.0)
        parts.append(tiles)
    joined = []
    for base in range(0, blocks[0].shape[0], 16):
        near, far = slice(base, base + 8), slice(base + 8, base + 16)
        joined.append(
            [
                jnp.concatenate([a[near], b[near], a[far]], axis=0)
                for a, b in zip(parts[0], parts[1])
            ]
        )
    return joined


def pick(head, at):
    row, col = iota((128, 128), 0), iota((128, 128), 1)
    hit = (row - 32 * head == col - at) & (col >= at) & (col < at + 32)
    return jnp.where(hit, 1.0, 0.0).astype(BF16)


def spread_out(out_w, wide):
    wide[...] = jnp.zeros_like(wide)
    for h in range(HEADS):
        for a in range(3):
            wide[h * 128 + 32 * a : h * 128 + 32 * a + 32, a * 128 : a * 128 + 128] = out_w[
                32 * h : 32 * h + 32, :
            ]


NEAR = (0, 1, 3, 2)
FAR = (4, 3, 5, 2, 6, 1, 7, 0)
CLOSE = FAR[::-1]


def scratch1():
    dma = pltpu.SemaphoreType.DMA
    return {
        "nrm": pltpu.VMEM((8, 144, C), BF16),
        "x1f": pltpu.VMEM((2, 2, 8, 144, C), BF16),
        "spread": pltpu.VMEM((64, C), F32),
        "hs": pltpu.VMEM((4, 16, C), BF16),
        "by": pltpu.VMEM((2, 2, 8, 16, C), BF16),
        "bf": pltpu.VMEM((4, 4, 48, 768), BF16),
        "wall": pltpu.VMEM((3, C, 512), BF16),
        "wide": pltpu.VMEM((512, 384), BF16),
        "q": pltpu.VMEM((6, 4, 4, 48, C), BF16),
        "k": pltpu.VMEM((6, 768, C), BF16),
        "v": pltpu.VMEM((6, 768, C), BF16),
        "g": pltpu.VMEM((2, 4, 4, 48, C), BF16),
        "rs": pltpu.VMEM((2, 4, 4, 48, C), BF16),
        "rx": pltpu.VMEM((8, 4, 48, C), BF16),
        "by_s": dma((2, 2, 8)),
        "by_r": dma((2, 2, 8)),
        "xy_s": dma((8,)),
        "xy_r": dma((8,)),
        "xz_s": dma((8,)),
        "xz_r": dma((8,)),
        "xc_s": dma((2, 8)),
        "xc_r": dma((2, 8)),
        "bz_s": dma((4,)),
        "bz_r": dma((4,)),
        "bx_s": dma((4, 4)),
        "bx_r": dma((4, 4)),
        "rt_s": dma((2, 4, 4)),
        "rt_r": dma((8, 4)),
    }


def partners(p):
    out = []
    for e in FAR:
        for c in range(2):
            for z in range(2):
                if (c, z, e) != (0, 0, 0):
                    out.append(p.dev(co=(p.co + c) % 2, zl=(p.zl + z) % 2, y=(p.y + e) % 8))
    for d in range(1, 4):
        out.append(p.dev(zh=(p.zh + d) % 4))
        out.append(p.dev(x=(p.x + d) % 4))
    return out


def phase1(p, fetches, fetched, ready, src, mask, proj, bias_w, out_w, dst, nrm, nf, m):
    head = 2 * p.zl + p.co
    copies = []

    for b, fetch in enumerate(fetches):
        fetch.wait()
        normed = layer_norm(src[288 * b : 288 * b + 288, :]).astype(BF16)
        m["nrm"][2 * b : 2 * b + 2] = normed.reshape(2, 144, C)
    local_bias(m["nrm"][...].reshape(1152, C), bias_w[...], m["spread"], m["hs"])
    ready()
    m["by"][p.co, p.zl, p.y] = m["hs"][head]
    for e in FAR:
        for c in range(2):
            for z in range(2):
                if (c, z, e) != (0, 0, 0):
                    co, zl, y = (p.co + c) % 2, (p.zl + z) % 2, (p.y + e) % 8
                    copies.append(
                        send(
                            m["hs"].at[2 * zl + co],
                            m["by"].at[p.co, p.zl, p.y],
                            m["by_s"].at[c, z, e],
                            m["by_r"].at[p.co, p.zl, p.y],
                            p.dev(co=co, zl=zl, y=y),
                        )
                    )
    for d in FAR[:7]:
        to = (p.y + d) % 8
        copies.append(
            send(
                m["nrm"].at[to],
                m["x1f"].at[p.co, p.zl, p.y],
                m["xy_s"].at[d],
                m["xy_r"].at[p.y],
                p.dev(y=to),
            )
        )
    m["x1f"][p.co, p.zl, p.y] = m["nrm"][p.y]

    fetched()
    for a in range(3):
        first, here = pick(head, 0), pick(head, 32 * a)
        m["wall"][a, :, 0:128] = dot(proj[:, 0:128], first).astype(BF16)
        m["wall"][a, :, 128:256] = dot(proj[:, 128:256], first).astype(BF16)
        m["wall"][a, :, 256:384] = dot(proj[:, 256:384], here).astype(BF16)
        m["wall"][a, :, 384:512] = dot(proj[:, 384:512], here).astype(BF16)
    spread_out(out_w, m["wide"])

    for e in FAR:
        for c in range(2):
            for z in range(2):
                if (c, z, e) != (0, 0, 0):
                    co, zl, y = (p.co + c) % 2, (p.zl + z) % 2, (p.y + e) % 8
                    got(m["by"].at[co, zl, y], m["by_r"].at[co, zl, y], p.dev(co=co, zl=zl, y=y))
    joined = join_columns([m["by"][:, :, y].reshape(64, C).astype(F32) for y in range(8)])
    whole = jnp.concatenate(
        [
            jnp.concatenate([joined[z][j], joined[2 + z][j]], axis=0)
            for z in range(2)
            for j in range(3)
        ],
        axis=1,
    )
    m["bf"][p.x, p.zh] = jnp.where(mask[...].reshape(1, 768) > 0, whole, NEG).astype(BF16)

    def to_columns(zh):
        block = m["bf"].at[p.x, zh]
        for d in NEAR[1:]:
            copies.append(
                send(
                    block,
                    block,
                    m["bx_s"].at[d, zh],
                    m["bx_r"].at[p.x, zh],
                    p.dev(x=(p.x + d) % 4),
                )
            )

    mine = m["bf"].at[p.x, p.zh]
    for d in NEAR[1:]:
        copies.append(
            send(mine, mine, m["bz_s"].at[d], m["bz_r"].at[p.zh], p.dev(zh=(p.zh + d) % 4))
        )
    to_columns(p.zh)
    for d in CLOSE:
        fr = (p.y + d) % 8
        block = m["x1f"].at[p.co, p.zl, fr]
        if d:
            got(block, m["xy_r"].at[fr], p.dev(y=fr))
        copies.append(
            send(block, block, m["xz_s"].at[d], m["xz_r"].at[fr], p.dev(zl=(p.zl + 1) % 2))
        )
        copies.append(
            send(block, block, m["xc_s"].at[0, d], m["xc_r"].at[p.zl, fr], p.dev(co=1 - p.co))
        )

    for d in NEAR[1:]:
        zh = (p.zh + d) % 4
        got(m["bf"].at[p.x, zh], m["bz_r"].at[zh], p.dev(zh=zh))
        to_columns(zh)
    other = (p.zl + 1) % 2
    for d in CLOSE:
        fr = (p.y + d) % 8
        block = m["x1f"].at[p.co, other, fr]
        got(block, m["xz_r"].at[fr], p.dev(zl=other))
        copies.append(
            send(block, block, m["xc_s"].at[1, d], m["xc_r"].at[other, fr], p.dev(co=1 - p.co))
        )

    lane = iota((768, C), 1)

    def prepare(t, _):
        co = (p.co + t) % 2

        @pl.when(t == 1)
        def _():
            for zl in range(2):
                for y in range(8):
                    got(m["x1f"].at[co, zl, y], m["xc_r"].at[zl, y], p.dev(co=co))

        gate = jnp.zeros((768, C), F32)
        for a in range(3):
            rows = m["x1f"][co, :, :, a * 48 : a * 48 + 48, :].reshape(768, C)
            mixed = dot(rows, m["wall"][a])
            item = 3 * co + a
            query = (mixed[:, 0:128] * HD ** (-0.5)).astype(BF16)
            m["q"][item] = query.reshape(4, 4, 48, C)
            m["k"][item] = mixed[:, 128:256].astype(BF16)
            value = jnp.where(lane == 96 + a, 1.0, mixed[:, 256:384])
            m["v"][item] = value.astype(BF16)
            gate = gate + mixed[:, 384:512]
        gate = jnp.where(lane < 96, jax.nn.sigmoid(gate), 0.0)
        m["g"][co] = gate.astype(BF16).reshape(4, 4, 48, C)
        return 0

    lax.fori_loop(0, 2, prepare, 0)

    lane = iota((192, C), 1)

    def attend(t, _):
        s, co = t // 2, t % 2
        x = (p.x + s + jnp.where(s == 2, 1, 0) - jnp.where(s == 3, 1, 0)) % 4

        @pl.when((s > 0) & (co == 0))
        def _():
            for zh in range(4):
                got(m["bf"].at[x, zh], m["bx_r"].at[x, zh], p.dev(x=x))

        bias = m["bf"][x].reshape(192, 768)
        out = jnp.zeros((192, C), F32)
        for a in range(3):
            item = 3 * co + a
            query = m["q"][item, :, x].reshape(192, C)
            scores = dot_nt(query, m["k"][item]) + bias.astype(F32)
            top = jnp.max(scores, axis=-1, keepdims=True)
            weights = jnp.exp(scores - top).astype(BF16)
            out = out + dot(weights, m["v"][item])
        inv = [1.0 / out[:, 96 + a : 97 + a] for a in range(3)]
        scale = jnp.where(lane < 32, inv[0], jnp.where(lane < 64, inv[1], inv[2]))
        gated = out * scale * m["g"][co, :, x].reshape(192, C).astype(F32)
        m["rs"][co, :, x] = gated.astype(BF16).reshape(4, 48, C)
        for zh in range(4):
            zl, y = zh // 2, (zh % 2) * 4 + x
            self = (co == p.co) & (zl == p.zl) & (y == p.y)

            @pl.when(self)
            def _():
                m["rx"][p.y, head] = m["rs"][co, zh, x]

            @pl.when(jnp.logical_not(self))
            def _():
                send(
                    m["rs"].at[co, zh, x],
                    m["rx"].at[p.y, head],
                    m["rt_s"].at[co, zh, x],
                    m["rt_r"].at[p.y, head],
                    p.dev(co=co, zl=zl, y=y),
                )

        return 0

    lax.fori_loop(0, 8, attend, 0)

    def finish(t, _):
        places = [(p.y + 8 - t) % 8, (p.y + t + 1) % 8]
        for y in places:
            for h in range(HEADS):

                @pl.when(jnp.logical_not((y == p.y) & (h == head)))
                def _():
                    got(m["rx"].at[y, h], m["rt_r"].at[y, h], p.dev(co=h % 2, zl=h // 2, y=y))

        for y in places:
            rows = jnp.concatenate([m["rx"][y, h] for h in range(HEADS)], axis=1)
            update = dot(rows, m["wide"][...])
            for a in range(3):
                at = pl.multiple_of((3 * y + a) * 48, 16)
                mid = src[pl.ds(at, 48), :] + update[:, a * 128 : a * 128 + 128]
                dst[pl.ds(at, 48), :] = mid
                normed = layer_norm(mid).astype(BF16)
                nrm[pl.ds(at, 48), :] = normed
                nf[pl.ds(at, 48), :] = normed.astype(F32)
        return 0

    lax.fori_loop(0, 4, finish, 0)

    def leave(t, _):
        co, zh, x = t // 16, (t // 4) % 4, t % 4
        zl, y = zh // 2, (zh % 2) * 4 + x

        @pl.when(jnp.logical_not((co == p.co) & (zl == p.zl) & (y == p.y)))
        def _():
            sent(m["rs"].at[co, zh, x], m["rt_s"].at[co, zh, x], p.dev(co=co, zl=zl, y=y))

        return 0

    def close():
        for copy in copies:
            copy.wait_send()
        lax.fori_loop(0, 32, leave, 0)

    return close


def scratch2():
    dma = pltpu.SemaphoreType.DMA
    return {
        "nrm": pltpu.VMEM((1152, C), BF16),
        "nf": pltpu.VMEM((1152, C), F32),
        "ns": pltpu.VMEM((4, 4, 80, C), BF16),
        "x2": pltpu.VMEM((2, 2, 4, 4, 80, C), BF16),
        "xx": pltpu.VMEM((6, 16, 48, C), BF16),
        "spread": pltpu.VMEM((64, C), F32),
        "hs": pltpu.VMEM((4, 16, C), BF16),
        "by": pltpu.VMEM((2, 8, 16, C), BF16),
        "b2": pltpu.VMEM((4, 4, 2, 48, 384), BF16),
        "wk": pltpu.VMEM((C, C), BF16),
        "wt": pltpu.VMEM((C, C), BF16),
        "wide": pltpu.VMEM((512, 384), BF16),
        "qt": pltpu.VMEM((6, 2, C, 384), BF16),
        "k": pltpu.VMEM((6, 768, C), BF16),
        "vt": pltpu.VMEM((6, 48, 768), BF16),
        "gt": pltpu.VMEM((6, 2, 32, 384), BF16),
        "ot": pltpu.VMEM((C, 384), BF16),
        "tr": pltpu.VMEM((384, C), F32),
        "rs": pltpu.VMEM((2, 2, 8, 48, C), BF16),
        "rx": pltpu.VMEM((2, 4, 4, 2, 48, C), BF16),
        "by_s": dma((2, 8)),
        "by_r": dma((2, 8)),
        "xa_s": dma((4, 4)),
        "xa_r": dma((4, 4)),
        "xy_s": dma((4, 4)),
        "xy_r": dma((4, 4)),
        "xc_s": dma((2, 4)),
        "xc_r": dma((2, 4)),
        "bz_s": dma((4, 2)),
        "bz_r": dma((4, 2)),
        "bx_s": dma((4, 4, 2)),
        "bx_r": dma((4, 4, 2)),
        "rt_s": dma((2, 2, 8)),
        "rt_r": dma((4, 4, 2)),
        "rc_s": dma((4, 4)),
        "rc_r": dma((4, 4)),
    }


def pick_rows(head, at):
    row, col = iota((128, 128), 0), iota((128, 128), 1)
    hit = (row - at == col - 32 * head) & (row >= at) & (row < at + 32)
    return jnp.where(hit, 1.0, 0.0).astype(BF16)


def phase2(p, close1, fetched, mid, mask, proj, bias_w, out_w, dst, m):
    head = 2 * p.yl + p.co
    other = 1 - p.co
    copies = []

    local_bias(m["nrm"][...], bias_w[...], m["spread"], m["hs"])
    m["by"][p.co, p.y] = m["hs"][head]
    for e in FAR:
        for c in range(2):
            if (c, e) != (0, 0):
                co, y = (p.co + c) % 2, (p.y + e) % 8
                copies.append(
                    send(
                        m["hs"].at[2 * (y % 2) + co],
                        m["by"].at[p.co, p.y],
                        m["by_s"].at[c, e],
                        m["by_r"].at[p.co, p.y],
                        p.dev(co=co, y=y),
                    )
                )

    for a in (2, 1, 3, 0):
        for b in (2, 1, 3, 0):
            zh, x = (p.zh + a) % 4, (p.x + b) % 4
            first = 3 * (zh * 4 + x)
            rows = [m["nf"][pl.ds(first + i, 24, stride=48), :] for i in range(3)]
            rows.append(jnp.zeros((8, C), F32))
            m["ns"][zh, x] = jnp.concatenate(rows, axis=0).astype(BF16)
            if (a, b) == (0, 0):
                m["x2"][p.yl, p.co, p.zh, p.x] = m["ns"][zh, x]
            else:
                copies.append(
                    send(
                        m["ns"].at[zh, x],
                        m["x2"].at[p.yl, p.co, p.zh, p.x],
                        m["xa_s"].at[a, b],
                        m["xa_r"].at[p.zh, p.x],
                        p.dev(zh=zh, x=x),
                    )
                )

    fetched()
    m["wk"][...] = dot(proj[:, 128:256], pick(head, 0)).astype(BF16)
    wt = dot_nt(pick_rows(head, 0), proj[:, 0:128])
    wt = wt + dot_nt(pick_rows(head, 32), proj[:, 256:384])
    wt = wt + dot_nt(pick_rows(head, 64), proj[:, 384:512])
    m["wt"][...] = wt.astype(BF16)
    spread_out(out_w, m["wide"])
    close1()

    row, col = iota((48, 768), 0), iota((48, 768), 1)
    keep = jnp.where(col == row + 48 * (4 * p.zh + p.x), mask[...].reshape(1, 768), 0)
    keep = jnp.sum(keep.astype(F32), axis=1, keepdims=True)
    for e in FAR:
        for c in range(2):
            if (c, e) != (0, 0):
                co, y = (p.co + c) % 2, (p.y + e) % 8
                got(m["by"].at[co, y], m["by_r"].at[co, y], p.dev(co=co, y=y))
    joined = join_columns([m["by"][:, y].reshape(32, C).astype(F32) for y in range(8)])
    whole = jnp.concatenate(
        [jnp.concatenate([joined[0][j], joined[1][j]], axis=0) for j in range(3)], axis=1
    )
    m["b2"][p.zh, p.x, p.zl] = jnp.where(keep > 0.5, whole, NEG).astype(BF16)

    def to_columns(zh, zl):
        block = m["b2"].at[zh, p.x, zl]
        for d in NEAR[1:]:
            copies.append(
                send(
                    block,
                    block,
                    m["bx_s"].at[d, zh, zl],
                    m["bx_r"].at[p.x, zh, zl],
                    p.dev(x=(p.x + d) % 4),
                )
            )

    mine = m["b2"].at[p.zh, p.x, p.zl]
    for z in range(2):
        for a in NEAR:
            if (a, z) != (0, 0):
                zh, zl = (p.zh + a) % 4, (p.zl + z) % 2
                copies.append(
                    send(
                        mine,
                        mine,
                        m["bz_s"].at[a, z],
                        m["bz_r"].at[p.zh, p.zl],
                        p.dev(zh=zh, zl=zl),
                    )
                )
    to_columns(p.zh, p.zl)

    for a in NEAR:
        for b in NEAR:
            zh, x = (p.zh + a) % 4, (p.x + b) % 4
            block = m["x2"].at[p.yl, p.co, zh, x]
            if (a, b) != (0, 0):
                got(block, m["xa_r"].at[zh, x], p.dev(zh=zh, x=x))
            copies.append(
                send(block, block, m["xy_s"].at[a, b], m["xy_r"].at[zh, x], p.dev(y=p.y1))
            )
        part = m["x2"].at[p.yl, p.co, zh]
        copies.append(
            send(part, part, m["xc_s"].at[0, a], m["xc_r"].at[p.yl, zh], p.dev(co=other))
        )

    for z in range(2):
        for a in NEAR:
            if (a, z) != (0, 0):
                zh, zl = (p.zh + a) % 4, (p.zl + z) % 2
                got(m["b2"].at[zh, p.x, zl], m["bz_r"].at[zh, zl], p.dev(zh=zh, zl=zl))
                to_columns(zh, zl)

    for a in NEAR:
        for b in NEAR:
            zh, x = (p.zh + a) % 4, (p.x + b) % 4
            got(m["x2"].at[1 - p.yl, p.co, zh, x], m["xy_r"].at[zh, x], p.dev(y=p.y1))
        part = m["x2"].at[1 - p.yl, p.co, zh]
        copies.append(
            send(part, part, m["xc_s"].at[1, a], m["xc_r"].at[1 - p.yl, zh], p.dev(co=other))
        )

    sub = iota((16, 768), 0)
    ones = jnp.where(sub == 0, 1.0, 0.0)

    def prepare(t, _):
        yl = (p.yl + t) % 2
        for zh in range(4):
            got(m["x2"].at[yl, other, zh], m["xc_r"].at[yl, zh], p.dev(co=other))

        def arrange(n, _):
            zh, x = n // 4, n % 4
            cores = [m["x2"][yl, c, zh, x].astype(F32) for c in range(2)]
            for b in range(3):
                rows = [core[24 * b : 24 * b + 24] for core in cores]
                m["xx"][3 * yl + b, n] = jnp.concatenate(rows, axis=0).astype(BF16)
            return 0

        lax.fori_loop(0, 16, arrange, 0)
        for b in range(3):
            item = 3 * yl + b
            rows = m["xx"][item].reshape(768, C)
            m["k"][item] = dot(rows, m["wk"][...]).astype(BF16)
            mixed = dot_nt(m["wt"][...], rows)
            query = (mixed * HD ** (-0.5)).astype(BF16)
            gate = jax.nn.sigmoid(mixed[64:96]).astype(BF16)
            for z in range(2):
                m["qt"][item, z] = query[:, 384 * z : 384 * z + 384]
                m["gt"][item, z] = gate[:, 384 * z : 384 * z + 384]
            m["vt"][item] = jnp.concatenate([mixed[32:64], ones], axis=0).astype(BF16)
        return 0

    lax.fori_loop(0, 2, prepare, 0)

    m["ot"][...] = jnp.zeros_like(m["ot"])
    eye = jnp.where(iota((128, 128), 0) == iota((128, 128), 1), 1.0, 0.0).astype(BF16)

    def attend(t, _):
        z, yl = (p.zl + t // 2) % 2, t % 2

        @pl.when(yl == 0)
        def _():
            for d in range(1, 4):
                x = (p.x + d) % 4
                for zh in range(4):
                    got(m["b2"].at[zh, x, z], m["bx_r"].at[x, zh, z], p.dev(x=x))

        bias = m["b2"][:, :, z].reshape(768, 384)
        for b in range(3):
            item = 3 * yl + b
            scores = dot(m["k"][item], m["qt"][item, z]) + bias.astype(F32)
            top = jnp.max(scores, axis=0, keepdims=True)
            weights = jnp.exp(scores - top).astype(BF16)
            out = dot(m["vt"][item], weights)
            gated = out[0:32] / out[32:33] * m["gt"][item, z].astype(F32)
            m["ot"][32 * b : 32 * b + 32, :] = gated.astype(BF16)
        for j in range(3):
            m["tr"][128 * j : 128 * j + 128, :] = dot_nt(eye, m["ot"][:, 128 * j : 128 * j + 128])
        y = p.y - p.yl + yl
        for n in range(8):
            zh, x = 2 * z + n // 4, n % 4
            m["rs"][z, yl, n] = m["tr"][48 * n : 48 * n + 48, :].astype(BF16)
            self = (zh == p.zh) & (p.x == x) & (yl == p.yl)

            @pl.when(self)
            def _():
                m["rx"][p.co, p.zh, p.x, p.yl] = m["rs"][z, yl, n]

            @pl.when(jnp.logical_not(self))
            def _():
                send(
                    m["rs"].at[z, yl, n],
                    m["rx"].at[p.co, p.zh, p.x, p.yl],
                    m["rt_s"].at[z, yl, n],
                    m["rt_r"].at[p.zh, p.x, p.yl],
                    p.dev(zh=zh, x=x, y=y),
                )

        return 0

    lax.fori_loop(0, 4, attend, 0)

    for copy in copies:
        copy.wait_send()
    copies.clear()

    for d in NEAR:
        zh = (p.zh + d) % 4
        for x in range(4):
            for yl in range(2):

                @pl.when(jnp.logical_not((zh == p.zh) & (x == p.x) & (yl == p.yl)))
                def _():
                    got(
                        m["rx"].at[p.co, zh, x, yl],
                        m["rt_r"].at[zh, x, yl],
                        p.dev(zh=zh, x=x, y=p.y - p.yl + yl),
                    )

            part = m["rx"].at[p.co, zh, x]
            copies.append(
                send(part, part, m["rc_s"].at[d, x], m["rc_r"].at[zh, x], p.dev(co=other))
            )

    def finish(t, _):
        zh = (p.zh + t + jnp.where(t == 2, 1, 0) - jnp.where(t == 3, 1, 0)) % 4
        for x in range(4):
            got(m["rx"].at[other, zh, x], m["rc_r"].at[zh, x], p.dev(co=other))
        rows = [m["rx"][h % 2, zh, :, h // 2].reshape(192, C) for h in range(HEADS)]
        update = dot(jnp.concatenate(rows, axis=1), m["wide"][...])
        for x in range(4):
            for b in range(3):
                chip = update[48 * x : 48 * x + 48, b * 128 : b * 128 + 128]
                at = pl.ds(3 * (4 * zh + x) + b, 24, stride=48)
                dst[at, :] = mid[at, :] + jnp.where(p.co == 0, chip[0:24], chip[24:48])
        return 0

    lax.fori_loop(0, 4, finish, 0)

    def leave(t, _):
        z, yl, n = t // 16, (t // 8) % 2, t % 8
        zh, x = 2 * z + n // 4, n % 4
        y = p.y - p.yl + yl

        @pl.when(jnp.logical_not((zh == p.zh) & (x == p.x) & (yl == p.yl)))
        def _():
            sent(m["rs"].at[z, yl, n], m["rt_s"].at[z, yl, n], p.dev(zh=zh, x=x, y=y))

        return 0

    def close():
        for copy in copies:
            copy.wait_send()
        lax.fori_loop(0, 32, leave, 0)

    return close


def kernel(
    names1, names2, pair, mask, proj1, bias1_w, out1_w, proj2, bias2_w, out2_w, dst, mid, src, proj1_v, out1_v, proj2_v, out2_v, sems, *refs
):
    m1 = dict(zip(names1, refs))
    m2 = dict(zip(names2, refs[len(names1) :]))
    p = Place()
    fetches = []
    for b in range(4):
        piece = pl.ds(288 * b, 288)
        fetches.append(pltpu.make_async_copy(pair.at[piece], src.at[piece], sems.at[b]))
        fetches[-1].start()
    weights = []
    for n, (given, held) in enumerate(
        zip((proj1, out1_w, proj2, out2_w), (proj1_v, out1_v, proj2_v, out2_v))
    ):
        weights.append(pltpu.make_async_copy(given, held, sems.at[4 + n]))
        weights[-1].start()
    others = partners(p)
    barrier = pltpu.get_barrier_semaphore()
    for device in others:
        pl.semaphore_signal(barrier, inc=1, device_id=device, device_id_type=MESH)

    def ready():
        pl.semaphore_wait(barrier, len(others))

    nrm, nf = m2["nrm"], m2["nf"]
    fetched1 = functools.partial(wait_all, weights[:2])
    fetched2 = functools.partial(wait_all, weights[2:])
    close1 = phase1(p, fetches, fetched1, ready, src, mask, proj1_v, bias1_w, out1_v, mid, nrm, nf, m1)
    close2 = phase2(p, close1, fetched2, mid, mask, proj2_v, bias2_w, out2_v, dst, m2)
    close2()


def shards(pair, residue_mask, start_proj, start_bias_w, start_out, end_proj, end_bias_w, end_out):
    rows, cols = pair.shape[:2]
    one, two = scratch1(), scratch2()
    vmem, hbm = pl.BlockSpec(memory_space=pltpu.VMEM), pl.BlockSpec(memory_space=pl.ANY)
    out = pl.pallas_call(
        functools.partial(kernel, tuple(one), tuple(two)),
        out_shape=jax.ShapeDtypeStruct((rows * cols, C), F32),
        in_specs=[hbm, vmem, hbm, vmem, hbm, hbm, vmem, hbm],
        out_specs=vmem,
        scratch_shapes=[
            pltpu.VMEM((rows * cols, C), F32),
            pltpu.VMEM((rows * cols, C), F32),
            pltpu.VMEM(start_proj.shape, BF16),
            pltpu.VMEM(start_out.shape, BF16),
            pltpu.VMEM(end_proj.shape, BF16),
            pltpu.VMEM(end_out.shape, BF16),
            pltpu.SemaphoreType.DMA((8,)),
        ]
        + list(one.values()) + list(two.values()),
        compiler_params=pltpu.CompilerParams(
            collective_id=0, has_side_effects=True, vmem_limit_bytes=56 << 20
        ),
        name="triangle_attention",
    )(
        pair.reshape(rows * cols, C),
        residue_mask,
        start_proj,
        start_bias_w.T,
        start_out,
        end_proj,
        end_bias_w.T,
        end_out,
    )
    return out.reshape(rows, cols, C)


def solution(mesh):
    placed = (P("row", "col", None), P(), P(), P(), P(), P(), P(), P())
    return jax.shard_map(
        shards, mesh=mesh, in_specs=placed, out_specs=P("row", "col", None), check_vma=False
    )
```

```python
import functools

import jax
import jax.numpy as jnp
from jax import lax
from jax.experimental import pallas as pl
from jax.experimental.pallas import tpu as pltpu
from jax.sharding import PartitionSpec as P

C = 128
HEADS = 4
HD = 32
MESH = pl.DeviceIdType.MESH
F32 = jnp.float32
BF16 = jnp.bfloat16
NT = (((1,), (1,)), ((), ()))
NEG = -1000000000.0


def iota(shape, dim):
    return lax.broadcasted_iota(jnp.int32, shape, dim)


def dot(a, b):
    return jnp.dot(a, b, preferred_element_type=F32)


def dot_nt(a, b):
    return lax.dot_general(a, b, NT, preferred_element_type=F32)


class Place:
    def __init__(self):
        r, c = lax.axis_index("row"), lax.axis_index("col")
        self.zh, self.x, self.co = r // 8, (r // 2) % 4, r % 2
        self.zl, self.y = c // 8, c % 8
        self.yl = self.y % 2
        self.y1 = self.y + 1 - 2 * self.yl

    def dev(self, zh=None, x=None, co=None, zl=None, y=None):
        zh = self.zh if zh is None else zh
        x = self.x if x is None else x
        co = self.co if co is None else co
        zl = self.zl if zl is None else zl
        y = self.y if y is None else y
        return (zh * 8 + x * 2 + co, zl * 8 + y)


def send(src, dst, ssem, rsem, device):
    copy = pltpu.make_async_remote_copy(
        src_ref=src, dst_ref=dst, send_sem=ssem, recv_sem=rsem, device_id=device, device_id_type=MESH
    )
    copy.start()
    return copy


def got(dst, sem, device):
    pltpu.make_async_remote_copy(
        src_ref=dst, dst_ref=dst, send_sem=sem, recv_sem=sem, device_id=device, device_id_type=MESH
    ).wait_recv()


def sent(src, sem, device):
    pltpu.make_async_remote_copy(
        src_ref=src, dst_ref=src, send_sem=sem, recv_sem=sem, device_id=device, device_id_type=MESH
    ).wait_send()


def wait_all(copies):
    for copy in copies:
        copy.wait()


def layer_norm(field):
    mean = jnp.mean(field, axis=-1, keepdims=True)
    centered = field - mean
    var = jnp.mean(centered * centered, axis=-1, keepdims=True)
    return centered * lax.rsqrt(var + 1e-05)


def local_bias(normed, bias_w, spread, heads):
    flat = dot_nt(bias_w, normed)
    spread[...] = jnp.zeros_like(spread)
    for r in range(24):
        row, lane = (r, 0) if r < 8 else (r - 8, 0 if r >= 16 else 64)
        spread[4 * row : 4 * row + 4, lane : lane + 48] = flat[:, 48 * r : 48 * r + 48]
    for h in range(HEADS):
        heads[h] = spread[pl.ds(h, 16, stride=4), :].astype(BF16)


def join_columns(blocks):
    lane = iota(blocks[0].shape, 1)
    parts = []
    for first in (0, 64):
        tiles = [jnp.zeros(blocks[0].shape, F32) for _ in range(3)]
        for b, block in enumerate(blocks):
            tile, at = (48 * b) // 128, (48 * b) % 128
            piece = jnp.where((lane >= first) & (lane < first + 48), block, 0.0)
            if (at - first) % 128:
                piece = pltpu.roll(piece, (at - first) % 128, 1)
            if at + 48 <= 128:
                tiles[tile] = tiles[tile] + piece
            else:
                tiles[tile] = tiles[tile] + jnp.where(lane >= at, piece, 0.0)
                tiles[tile + 1] = tiles[tile + 1] + jnp.where(lane < at, piece, 0.0)
        parts.append(tiles)
    joined = []
    for base in range(0, blocks[0].shape[0], 16):
        near, far = slice(base, base + 8), slice(base + 8, base + 16)
        joined.append(
            [
                jnp.concatenate([a[near], b[near], a[far]], axis=0)
                for a, b in zip(parts[0], parts[1])
            ]
        )
    return joined


def pick(head, at):
    row, col = iota((128, 128), 0), iota((128, 128), 1)
    hit = (row - 32 * head == col - at) & (col >= at) & (col < at + 32)
    return jnp.where(hit, 1.0, 0.0).astype(BF16)


def spread_out(out_w, wide):
    wide[...] = jnp.zeros_like(wide)
    for h in range(HEADS):
        for a in range(3):
            wide[h * 128 + 32 * a : h * 128 + 32 * a + 32, a * 128 : a * 128 + 128] = out_w[
                32 * h : 32 * h + 32, :
            ]


NEAR = (0, 1, 3, 2)
FAR = (4, 3, 5, 2, 6, 1, 7, 0)
CLOSE = FAR[::-1]


def scratch1():
    dma = pltpu.SemaphoreType.DMA
    return {
        "nrm": pltpu.VMEM((8, 144, C), BF16),
        "x1f": pltpu.VMEM((2, 2, 8, 144, C), BF16),
        "spread": pltpu.VMEM((64, C), F32),
        "hs": pltpu.VMEM((4, 16, C), BF16),
        "by": pltpu.VMEM((2, 2, 8, 16, C), BF16),
        "bf": pltpu.VMEM((4, 4, 48, 768), BF16),
        "wall": pltpu.VMEM((3, C, 512), BF16),
        "wide": pltpu.VMEM((512, 384), BF16),
        "q": pltpu.VMEM((6, 4, 4, 48, C), BF16),
        "k": pltpu.VMEM((6, 768, C), BF16),
        "v": pltpu.VMEM((6, 768, C), BF16),
        "g": pltpu.VMEM((2, 4, 4, 48, C), BF16),
        "rs": pltpu.VMEM((2, 4, 4, 48, C), BF16),
        "rx": pltpu.VMEM((8, 4, 48, C), BF16),
        "by_s": dma((2, 2, 8)),
        "by_r": dma((2, 2, 8)),
        "xy_s": dma((8,)),
        "xy_r": dma((8,)),
        "xz_s": dma((8,)),
        "xz_r": dma((8,)),
        "xc_s": dma((2, 8)),
        "xc_r": dma((2, 8)),
        "bz_s": dma((4,)),
        "bz_r": dma((4,)),
        "bx_s": dma((4, 4)),
        "bx_r": dma((4, 4)),
        "rt_s": dma((2, 4, 4)),
        "rt_r": dma((8, 4)),
    }


def partners(p):
    out = []
    for e in FAR:
        for c in range(2):
            for z in range(2):
                if (c, z, e) != (0, 0, 0):
                    out.append(p.dev(co=(p.co + c) % 2, zl=(p.zl + z) % 2, y=(p.y + e) % 8))
    for d in range(1, 4):
        out.append(p.dev(zh=(p.zh + d) % 4))
        out.append(p.dev(x=(p.x + d) % 4))
    return out


def phase1(p, fetches, fetched, ready, src, mask, proj, bias_w, out_w, dst, nrm, nf, m):
    head = 2 * p.zl + p.co
    copies = []

    for b, fetch in enumerate(fetches):
        fetch.wait()
        normed = layer_norm(src[288 * b : 288 * b + 288, :]).astype(BF16)
        m["nrm"][2 * b : 2 * b + 2] = normed.reshape(2, 144, C)
    local_bias(m["nrm"][...].reshape(1152, C), bias_w[...], m["spread"], m["hs"])
    ready()
    m["by"][p.co, p.zl, p.y] = m["hs"][head]
    for e in FAR:
        for c in range(2):
            for z in range(2):
                if (c, z, e) != (0, 0, 0):
                    co, zl, y = (p.co + c) % 2, (p.zl + z) % 2, (p.y + e) % 8
                    copies.append(
                        send(
                            m["hs"].at[2 * zl + co],
                            m["by"].at[p.co, p.zl, p.y],
                            m["by_s"].at[c, z, e],
                            m["by_r"].at[p.co, p.zl, p.y],
                            p.dev(co=co, zl=zl, y=y),
                        )
                    )
    for d in FAR[:7]:
        to = (p.y + d) % 8
        copies.append(
            send(
                m["nrm"].at[to],
                m["x1f"].at[p.co, p.zl, p.y],
                m["xy_s"].at[d],
                m["xy_r"].at[p.y],
                p.dev(y=to),
            )
        )
    m["x1f"][p.co, p.zl, p.y] = m["nrm"][p.y]

    def hand_on(d):
        fr = (p.y + d) % 8
        block = m["x1f"].at[p.co, p.zl, fr]
        copies.append(send(block, block, m["xz_s"].at[d], m["xz_r"].at[fr], p.dev(zl=1 - p.zl)))
        copies.append(
            send(block, block, m["xc_s"].at[0, d], m["xc_r"].at[p.zl, fr], p.dev(co=1 - p.co))
        )

    hand_on(0)

    fetched()
    for a in range(3):
        first, here = pick(head, 0), pick(head, 32 * a)
        m["wall"][a, :, 0:128] = dot(proj[:, 0:128], first).astype(BF16)
        m["wall"][a, :, 128:256] = dot(proj[:, 128:256], first).astype(BF16)
        m["wall"][a, :, 256:384] = dot(proj[:, 256:384], here).astype(BF16)
        m["wall"][a, :, 384:512] = dot(proj[:, 384:512], here).astype(BF16)
    spread_out(out_w, m["wide"])

    for e in FAR:
        for c in range(2):
            for z in range(2):
                if (c, z, e) != (0, 0, 0):
                    co, zl, y = (p.co + c) % 2, (p.zl + z) % 2, (p.y + e) % 8
                    got(m["by"].at[co, zl, y], m["by_r"].at[co, zl, y], p.dev(co=co, zl=zl, y=y))
    joined = join_columns([m["by"][:, :, y].reshape(64, C).astype(F32) for y in range(8)])
    whole = jnp.concatenate(
        [
            jnp.concatenate([joined[z][j], joined[2 + z][j]], axis=0)
            for z in range(2)
            for j in range(3)
        ],
        axis=1,
    )
    m["bf"][p.x, p.zh] = jnp.where(mask[...].reshape(1, 768) > 0, whole, NEG).astype(BF16)

    def to_columns(zh):
        block = m["bf"].at[p.x, zh]
        for d in NEAR[1:]:
            copies.append(
                send(
                    block,
                    block,
                    m["bx_s"].at[d, zh],
                    m["bx_r"].at[p.x, zh],
                    p.dev(x=(p.x + d) % 4),
                )
            )

    mine = m["bf"].at[p.x, p.zh]
    for d in NEAR[1:]:
        copies.append(
            send(mine, mine, m["bz_s"].at[d], m["bz_r"].at[p.zh], p.dev(zh=(p.zh + d) % 4))
        )
    to_columns(p.zh)
    for d in CLOSE[1:]:
        fr = (p.y + d) % 8
        got(m["x1f"].at[p.co, p.zl, fr], m["xy_r"].at[fr], p.dev(y=fr))
        hand_on(d)

    for d in NEAR[1:]:
        zh = (p.zh + d) % 4
        got(m["bf"].at[p.x, zh], m["bz_r"].at[zh], p.dev(zh=zh))
        to_columns(zh)
    other = (p.zl + 1) % 2
    for d in CLOSE:
        fr = (p.y + d) % 8
        block = m["x1f"].at[p.co, other, fr]
        got(block, m["xz_r"].at[fr], p.dev(zl=other))
        copies.append(
            send(block, block, m["xc_s"].at[1, d], m["xc_r"].at[other, fr], p.dev(co=1 - p.co))
        )

    lane = iota((768, C), 1)

    def prepare(t, _):
        co = (p.co + t) % 2

        @pl.when(t == 1)
        def _():
            for zl in range(2):
                for y in range(8):
                    got(m["x1f"].at[co, zl, y], m["xc_r"].at[zl, y], p.dev(co=co))

        gate = jnp.zeros((768, C), F32)
        for a in range(3):
            rows = m["x1f"][co, :, :, a * 48 : a * 48 + 48, :].reshape(768, C)
            mixed = dot(rows, m["wall"][a])
            item = 3 * co + a
            query = (mixed[:, 0:128] * HD ** (-0.5)).astype(BF16)
            m["q"][item] = query.reshape(4, 4, 48, C)
            m["k"][item] = mixed[:, 128:256].astype(BF16)
            value = jnp.where(lane == 96 + a, 1.0, mixed[:, 256:384])
            m["v"][item] = value.astype(BF16)
            gate = gate + mixed[:, 384:512]
        gate = jnp.where(lane < 96, jax.nn.sigmoid(gate), 0.0)
        m["g"][co] = gate.astype(BF16).reshape(4, 4, 48, C)
        return 0

    lax.fori_loop(0, 2, prepare, 0)

    lane = iota((192, C), 1)

    def attend(t, _):
        s, co = t // 2, t % 2
        x = (p.x + s + jnp.where(s == 2, 1, 0) - jnp.where(s == 3, 1, 0)) % 4

        @pl.when((s > 0) & (co == 0))
        def _():
            for zh in range(4):
                got(m["bf"].at[x, zh], m["bx_r"].at[x, zh], p.dev(x=x))

        bias = m["bf"][x].reshape(192, 768)
        out = jnp.zeros((192, C), F32)
        for a in range(3):
            item = 3 * co + a
            query = m["q"][item, :, x].reshape(192, C)
            scores = dot_nt(query, m["k"][item]) + bias.astype(F32)
            top = jnp.max(scores, axis=-1, keepdims=True)
            weights = jnp.exp(scores - top).astype(BF16)
            out = out + dot(weights, m["v"][item])
        inv = [1.0 / out[:, 96 + a : 97 + a] for a in range(3)]
        scale = jnp.where(lane < 32, inv[0], jnp.where(lane < 64, inv[1], inv[2]))
        gated = out * scale * m["g"][co, :, x].reshape(192, C).astype(F32)
        m["rs"][co, :, x] = gated.astype(BF16).reshape(4, 48, C)
        for zh in range(4):
            zl, y = zh // 2, (zh % 2) * 4 + x
            self = (co == p.co) & (zl == p.zl) & (y == p.y)

            @pl.when(self)
            def _():
                m["rx"][p.y, head] = m["rs"][co, zh, x]

            @pl.when(jnp.logical_not(self))
            def _():
                send(
                    m["rs"].at[co, zh, x],
                    m["rx"].at[p.y, head],
                    m["rt_s"].at[co, zh, x],
                    m["rt_r"].at[p.y, head],
                    p.dev(co=co, zl=zl, y=y),
                )

        return 0

    lax.fori_loop(0, 8, attend, 0)

    def finish(t, _):
        places = [(p.y + 8 - t) % 8, (p.y + t + 1) % 8]
        for y in places:
            for h in range(HEADS):

                @pl.when(jnp.logical_not((y == p.y) & (h == head)))
                def _():
                    got(m["rx"].at[y, h], m["rt_r"].at[y, h], p.dev(co=h % 2, zl=h // 2, y=y))

        for y in places:
            rows = jnp.concatenate([m["rx"][y, h] for h in range(HEADS)], axis=1)
            update = dot(rows, m["wide"][...])
            for a in range(3):
                at = pl.multiple_of((3 * y + a) * 48, 16)
                mid = src[pl.ds(at, 48), :] + update[:, a * 128 : a * 128 + 128]
                dst[pl.ds(at, 48), :] = mid
                normed = layer_norm(mid).astype(BF16)
                nrm[pl.ds(at, 48), :] = normed
                nf[pl.ds(at, 48), :] = normed.astype(F32)
        return 0

    lax.fori_loop(0, 4, finish, 0)

    def leave(t, _):
        co, zh, x = t // 16, (t // 4) % 4, t % 4
        zl, y = zh // 2, (zh % 2) * 4 + x

        @pl.when(jnp.logical_not((co == p.co) & (zl == p.zl) & (y == p.y)))
        def _():
            sent(m["rs"].at[co, zh, x], m["rt_s"].at[co, zh, x], p.dev(co=co, zl=zl, y=y))

        return 0

    def close():
        for copy in copies:
            copy.wait_send()
        lax.fori_loop(0, 32, leave, 0)

    return close


def scratch2():
    dma = pltpu.SemaphoreType.DMA
    return {
        "nrm": pltpu.VMEM((1152, C), BF16),
        "nf": pltpu.VMEM((1152, C), F32),
        "ns": pltpu.VMEM((4, 4, 80, C), BF16),
        "x2": pltpu.VMEM((2, 2, 4, 4, 80, C), BF16),
        "xx": pltpu.VMEM((6, 16, 48, C), BF16),
        "spread": pltpu.VMEM((64, C), F32),
        "hs": pltpu.VMEM((4, 16, C), BF16),
        "by": pltpu.VMEM((2, 8, 16, C), BF16),
        "b2": pltpu.VMEM((4, 4, 2, 48, 384), BF16),
        "wk": pltpu.VMEM((C, C), BF16),
        "wt": pltpu.VMEM((C, C), BF16),
        "wide": pltpu.VMEM((512, 384), BF16),
        "qt": pltpu.VMEM((6, 2, C, 384), BF16),
        "k": pltpu.VMEM((6, 768, C), BF16),
        "vt": pltpu.VMEM((6, 48, 768), BF16),
        "gt": pltpu.VMEM((6, 2, 32, 384), BF16),
        "ot": pltpu.VMEM((C, 384), BF16),
        "tr": pltpu.VMEM((384, C), F32),
        "rs": pltpu.VMEM((2, 2, 8, 48, C), BF16),
        "rx": pltpu.VMEM((2, 4, 4, 2, 48, C), BF16),
        "by_s": dma((2, 8)),
        "by_r": dma((2, 8)),
        "xa_s": dma((4, 4)),
        "xa_r": dma((4, 4)),
        "xy_s": dma((4, 4)),
        "xy_r": dma((4, 4)),
        "xc_s": dma((2, 4)),
        "xc_r": dma((2, 4)),
        "bz_s": dma((4, 2)),
        "bz_r": dma((4, 2)),
        "bx_s": dma((4, 4, 2)),
        "bx_r": dma((4, 4, 2)),
        "rt_s": dma((2, 2, 8)),
        "rt_r": dma((4, 4, 2)),
        "rc_s": dma((4, 4)),
        "rc_r": dma((4, 4)),
    }


def pick_rows(head, at):
    row, col = iota((128, 128), 0), iota((128, 128), 1)
    hit = (row - at == col - 32 * head) & (row >= at) & (row < at + 32)
    return jnp.where(hit, 1.0, 0.0).astype(BF16)


def phase2(p, close1, fetched, mid, mask, proj, bias_w, out_w, dst, m):
    head = 2 * p.yl + p.co
    other = 1 - p.co
    copies = []

    local_bias(m["nrm"][...], bias_w[...], m["spread"], m["hs"])
    m["by"][p.co, p.y] = m["hs"][head]
    for e in FAR:
        for c in range(2):
            if (c, e) != (0, 0):
                co, y = (p.co + c) % 2, (p.y + e) % 8
                copies.append(
                    send(
                        m["hs"].at[2 * (y % 2) + co],
                        m["by"].at[p.co, p.y],
                        m["by_s"].at[c, e],
                        m["by_r"].at[p.co, p.y],
                        p.dev(co=co, y=y),
                    )
                )

    for a in (2, 1, 3, 0):
        for b in (2, 1, 3, 0):
            zh, x = (p.zh + a) % 4, (p.x + b) % 4
            first = 3 * (zh * 4 + x)
            rows = [m["nf"][pl.ds(first + i, 24, stride=48), :] for i in range(3)]
            rows.append(jnp.zeros((8, C), F32))
            m["ns"][zh, x] = jnp.concatenate(rows, axis=0).astype(BF16)
            if (a, b) == (0, 0):
                m["x2"][p.yl, p.co, p.zh, p.x] = m["ns"][zh, x]
                block = m["x2"].at[p.yl, p.co, p.zh, p.x]
                copies.append(
                    send(block, block, m["xy_s"].at[0, 0], m["xy_r"].at[zh, x], p.dev(y=p.y1))
                )
            else:
                copies.append(
                    send(
                        m["ns"].at[zh, x],
                        m["x2"].at[p.yl, p.co, p.zh, p.x],
                        m["xa_s"].at[a, b],
                        m["xa_r"].at[p.zh, p.x],
                        p.dev(zh=zh, x=x),
                    )
                )

    fetched()
    m["wk"][...] = dot(proj[:, 128:256], pick(head, 0)).astype(BF16)
    wt = dot_nt(pick_rows(head, 0), proj[:, 0:128])
    wt = wt + dot_nt(pick_rows(head, 32), proj[:, 256:384])
    wt = wt + dot_nt(pick_rows(head, 64), proj[:, 384:512])
    m["wt"][...] = wt.astype(BF16)
    spread_out(out_w, m["wide"])
    close1()

    row, col = iota((48, 768), 0), iota((48, 768), 1)
    keep = jnp.where(col == row + 48 * (4 * p.zh + p.x), mask[...].reshape(1, 768), 0)
    keep = jnp.sum(keep.astype(F32), axis=1, keepdims=True)
    for e in FAR:
        for c in range(2):
            if (c, e) != (0, 0):
                co, y = (p.co + c) % 2, (p.y + e) % 8
                got(m["by"].at[co, y], m["by_r"].at[co, y], p.dev(co=co, y=y))
    joined = join_columns([m["by"][:, y].reshape(32, C).astype(F32) for y in range(8)])
    whole = jnp.concatenate(
        [jnp.concatenate([joined[0][j], joined[1][j]], axis=0) for j in range(3)], axis=1
    )
    m["b2"][p.zh, p.x, p.zl] = jnp.where(keep > 0.5, whole, NEG).astype(BF16)

    def to_columns(zh, zl):
        block = m["b2"].at[zh, p.x, zl]
        for d in NEAR[1:]:
            copies.append(
                send(
                    block,
                    block,
                    m["bx_s"].at[d, zh, zl],
                    m["bx_r"].at[p.x, zh, zl],
                    p.dev(x=(p.x + d) % 4),
                )
            )

    mine = m["b2"].at[p.zh, p.x, p.zl]
    for z in range(2):
        for a in NEAR:
            if (a, z) != (0, 0):
                zh, zl = (p.zh + a) % 4, (p.zl + z) % 2
                copies.append(
                    send(
                        mine,
                        mine,
                        m["bz_s"].at[a, z],
                        m["bz_r"].at[p.zh, p.zl],
                        p.dev(zh=zh, zl=zl),
                    )
                )
    to_columns(p.zh, p.zl)

    for a in NEAR:
        for b in NEAR:
            zh, x = (p.zh + a) % 4, (p.x + b) % 4
            block = m["x2"].at[p.yl, p.co, zh, x]
            if (a, b) != (0, 0):
                got(block, m["xa_r"].at[zh, x], p.dev(zh=zh, x=x))
                copies.append(
                    send(block, block, m["xy_s"].at[a, b], m["xy_r"].at[zh, x], p.dev(y=p.y1))
                )
        part = m["x2"].at[p.yl, p.co, zh]
        copies.append(
            send(part, part, m["xc_s"].at[0, a], m["xc_r"].at[p.yl, zh], p.dev(co=other))
        )

    for z in range(2):
        for a in NEAR:
            if (a, z) != (0, 0):
                zh, zl = (p.zh + a) % 4, (p.zl + z) % 2
                got(m["b2"].at[zh, p.x, zl], m["bz_r"].at[zh, zl], p.dev(zh=zh, zl=zl))
                to_columns(zh, zl)

    for a in NEAR:
        for b in NEAR:
            zh, x = (p.zh + a) % 4, (p.x + b) % 4
            got(m["x2"].at[1 - p.yl, p.co, zh, x], m["xy_r"].at[zh, x], p.dev(y=p.y1))
        part = m["x2"].at[1 - p.yl, p.co, zh]
        copies.append(
            send(part, part, m["xc_s"].at[1, a], m["xc_r"].at[1 - p.yl, zh], p.dev(co=other))
        )

    sub = iota((16, 768), 0)
    ones = jnp.where(sub == 0, 1.0, 0.0)

    def prepare(t, _):
        yl = (p.yl + t) % 2
        for zh in range(4):
            got(m["x2"].at[yl, other, zh], m["xc_r"].at[yl, zh], p.dev(co=other))

        def arrange(n, _):
            zh, x = n // 4, n % 4
            cores = [m["x2"][yl, c, zh, x].astype(F32) for c in range(2)]
            for b in range(3):
                rows = [core[24 * b : 24 * b + 24] for core in cores]
                m["xx"][3 * yl + b, n] = jnp.concatenate(rows, axis=0).astype(BF16)
            return 0

        lax.fori_loop(0, 16, arrange, 0)
        for b in range(3):
            item = 3 * yl + b
            rows = m["xx"][item].reshape(768, C)
            m["k"][item] = dot(rows, m["wk"][...]).astype(BF16)
            mixed = dot_nt(m["wt"][...], rows)
            query = (mixed * HD ** (-0.5)).astype(BF16)
            gate = jax.nn.sigmoid(mixed[64:96]).astype(BF16)
            for z in range(2):
                m["qt"][item, z] = query[:, 384 * z : 384 * z + 384]
                m["gt"][item, z] = gate[:, 384 * z : 384 * z + 384]
            m["vt"][item] = jnp.concatenate([mixed[32:64], ones], axis=0).astype(BF16)
        return 0

    lax.fori_loop(0, 2, prepare, 0)

    m["ot"][...] = jnp.zeros_like(m["ot"])
    eye = jnp.where(iota((128, 128), 0) == iota((128, 128), 1), 1.0, 0.0).astype(BF16)

    def attend(t, _):
        z, yl = (p.zl + t // 2) % 2, t % 2

        @pl.when(yl == 0)
        def _():
            for d in range(1, 4):
                x = (p.x + d) % 4
                for zh in range(4):
                    got(m["b2"].at[zh, x, z], m["bx_r"].at[x, zh, z], p.dev(x=x))

        bias = m["b2"][:, :, z].reshape(768, 384)
        for b in range(3):
            item = 3 * yl + b
            scores = dot(m["k"][item], m["qt"][item, z]) + bias.astype(F32)
            top = jnp.max(scores, axis=0, keepdims=True)
            weights = jnp.exp(scores - top).astype(BF16)
            out = dot(m["vt"][item], weights)
            gated = out[0:32] / out[32:33] * m["gt"][item, z].astype(F32)
            m["ot"][32 * b : 32 * b + 32, :] = gated.astype(BF16)
        for j in range(3):
            m["tr"][128 * j : 128 * j + 128, :] = dot_nt(eye, m["ot"][:, 128 * j : 128 * j + 128])
        y = p.y - p.yl + yl
        for n in range(8):
            zh, x = 2 * z + n // 4, n % 4
            m["rs"][z, yl, n] = m["tr"][48 * n : 48 * n + 48, :].astype(BF16)
            self = (zh == p.zh) & (p.x == x) & (yl == p.yl)

            @pl.when(self)
            def _():
                m["rx"][p.co, p.zh, p.x, p.yl] = m["rs"][z, yl, n]

            @pl.when(jnp.logical_not(self))
            def _():
                send(
                    m["rs"].at[z, yl, n],
                    m["rx"].at[p.co, p.zh, p.x, p.yl],
                    m["rt_s"].at[z, yl, n],
                    m["rt_r"].at[p.zh, p.x, p.yl],
                    p.dev(zh=zh, x=x, y=y),
                )

        return 0

    lax.fori_loop(0, 4, attend, 0)

    for copy in copies:
        copy.wait_send()
    copies.clear()

    for d in NEAR:
        zh = (p.zh + d) % 4
        for x in range(4):
            for yl in range(2):

                @pl.when(jnp.logical_not((zh == p.zh) & (x == p.x) & (yl == p.yl)))
                def _():
                    got(
                        m["rx"].at[p.co, zh, x, yl],
                        m["rt_r"].at[zh, x, yl],
                        p.dev(zh=zh, x=x, y=p.y - p.yl + yl),
                    )

            part = m["rx"].at[p.co, zh, x]
            copies.append(
                send(part, part, m["rc_s"].at[d, x], m["rc_r"].at[zh, x], p.dev(co=other))
            )

    def finish(t, _):
        zh = (p.zh + t + jnp.where(t == 2, 1, 0) - jnp.where(t == 3, 1, 0)) % 4
        for x in range(4):
            got(m["rx"].at[other, zh, x], m["rc_r"].at[zh, x], p.dev(co=other))
        rows = [m["rx"][h % 2, zh, :, h // 2].reshape(192, C) for h in range(HEADS)]
        update = dot(jnp.concatenate(rows, axis=1), m["wide"][...])
        for x in range(4):
            for b in range(3):
                chip = update[48 * x : 48 * x + 48, b * 128 : b * 128 + 128]
                at = pl.ds(3 * (4 * zh + x) + b, 24, stride=48)
                dst[at, :] = mid[at, :] + jnp.where(p.co == 0, chip[0:24], chip[24:48])
        return 0

    lax.fori_loop(0, 4, finish, 0)

    def leave(t, _):
        z, yl, n = t // 16, (t // 8) % 2, t % 8
        zh, x = 2 * z + n // 4, n % 4
        y = p.y - p.yl + yl

        @pl.when(jnp.logical_not((zh == p.zh) & (x == p.x) & (yl == p.yl)))
        def _():
            sent(m["rs"].at[z, yl, n], m["rt_s"].at[z, yl, n], p.dev(zh=zh, x=x, y=y))

        return 0

    def close():
        for copy in copies:
            copy.wait_send()
        lax.fori_loop(0, 32, leave, 0)

    return close


def kernel(
    names1, names2, pair, mask, proj1, bias1_w, out1_w, proj2, bias2_w, out2_w, dst, mid, src, proj1_v, out1_v, proj2_v, out2_v, sems, *refs
):
    m1 = dict(zip(names1, refs))
    m2 = dict(zip(names2, refs[len(names1) :]))
    p = Place()
    fetches = []
    for b in range(4):
        piece = pl.ds(288 * b, 288)
        fetches.append(pltpu.make_async_copy(pair.at[piece], src.at[piece], sems.at[b]))
        fetches[-1].start()
    weights = []
    for n, (given, held) in enumerate(
        zip((proj1, out1_w, proj2, out2_w), (proj1_v, out1_v, proj2_v, out2_v))
    ):
        weights.append(pltpu.make_async_copy(given, held, sems.at[4 + n]))
        weights[-1].start()
    others = partners(p)
    barrier = pltpu.get_barrier_semaphore()
    for device in others:
        pl.semaphore_signal(barrier, inc=1, device_id=device, device_id_type=MESH)

    def ready():
        pl.semaphore_wait(barrier, len(others))

    nrm, nf = m2["nrm"], m2["nf"]
    fetched1 = functools.partial(wait_all, weights[:2])
    fetched2 = functools.partial(wait_all, weights[2:])
    close1 = phase1(p, fetches, fetched1, ready, src, mask, proj1_v, bias1_w, out1_v, mid, nrm, nf, m1)
    close2 = phase2(p, close1, fetched2, mid, mask, proj2_v, bias2_w, out2_v, dst, m2)
    close2()


def shards(pair, residue_mask, start_proj, start_bias_w, start_out, end_proj, end_bias_w, end_out):
    rows, cols = pair.shape[:2]
    one, two = scratch1(), scratch2()
    vmem, hbm = pl.BlockSpec(memory_space=pltpu.VMEM), pl.BlockSpec(memory_space=pl.ANY)
    out = pl.pallas_call(
        functools.partial(kernel, tuple(one), tuple(two)),
        out_shape=jax.ShapeDtypeStruct((rows * cols, C), F32),
        in_specs=[hbm, vmem, hbm, vmem, hbm, hbm, vmem, hbm],
        out_specs=vmem,
        scratch_shapes=[
            pltpu.VMEM((rows * cols, C), F32),
            pltpu.VMEM((rows * cols, C), F32),
            pltpu.VMEM(start_proj.shape, BF16),
            pltpu.VMEM(start_out.shape, BF16),
            pltpu.VMEM(end_proj.shape, BF16),
            pltpu.VMEM(end_out.shape, BF16),
            pltpu.SemaphoreType.DMA((8,)),
        ]
        + list(one.values()) + list(two.values()),
        compiler_params=pltpu.CompilerParams(
            collective_id=0, has_side_effects=True, vmem_limit_bytes=56 << 20
        ),
        name="triangle_attention",
    )(
        pair.reshape(rows * cols, C),
        residue_mask,
        start_proj,
        start_bias_w.T,
        start_out,
        end_proj,
        end_bias_w.T,
        end_out,
    )
    return out.reshape(rows, cols, C)


def solution(mesh):
    placed = (P("row", "col", None), P(), P(), P(), P(), P(), P(), P())
    return jax.shard_map(
        shards, mesh=mesh, in_specs=placed, out_specs=P("row", "col", None), check_vma=False
    )
```
